32 devices in a mesh: src: 4 (over x, core), dst: 8 (over z, y).
Axes of the slice: x: 2, y: 2, z: 4, core: 2. Of those that a mesh axis runs over, the one named last changes fastest.
Arguments:
- edge_state: bfloat16 [65536, 512], P(('src', 'dst')), may hold values from -6 to 6
- directions: float32 [3, 65536], P(None, ('src', 'dst')), as said below
- src_atom: int32 [65536], P(('src', 'dst')), may hold values from 0 to 255
- dst_atom: int32 [65536], P(('src', 'dst')), may hold values from 0 to 127
- rev_pos: int32 [65536], P(('src', 'dst')), may hold values from 0 to 63, as said below
- counts: int32 [32, 32], P(('src', 'dst')), may hold values from 0 to 64, as said below
- triplets: int32 [512, 4], P(('src', 'dst')), may hold values from 0 to 63
- down_w: bfloat16 [2, 512, 64], replicated, may hold values from -0.25 to 0.25
- trip_w: bfloat16 [2, 256, 512], replicated, may hold values from -0.75 to 0.75
- edge_w: bfloat16 [2, 6, 512, 512], replicated, may hold values from -0.25 to 0.25
Outputs:
- new_state: bfloat16 [65536, 512], P(('src', 'dst'))
The draws below stay inside these ranges and needn't reach their ends.
Inputs may be any that keep to these rules, and one draw needn't show every extreme that they name: `counts`: Symmetric, zero on the diagonal, and equal to 64 for some pair in every draw. Within each bucket b of device f, rev_pos maps the live positions one to one onto live positions of bucket f of device b, and the map for (b, f) is the inverse of that for (f, b); dead positions map to themselves. `directions`: unit vectors.
All inputs are finite; a program needn't handle non-finite values.
Results may differ from the reference program's by a relative error of at most 0.017.
Values may be sent and summed in bfloat16 or wider, within the bound.
No kernel may reach another device: no remote copies, remote signals or barrier semaphores. Data moves between devices by JAX's collectives and lax.ppermute only.
A program may use at most 128 MiB of HBM per device.

```python
import math
import jax
import jax.numpy as jnp
from jax import lax

D = 512
TRIP = 64
NSPH = 4
BLK = 128
PAIRS = 4
NBLK = 2
EDGE_DEV = 2048
BUCKETS = 32
CAP = 64
EDGES = 65536
BLOCKS = 512
ATOMS = 1024
DST_ATOMS = 128
SRC_ATOMS = 256
DEGREE = 64
N_SRC = 4
N_DST = 8


def pair_tables(key):
    key = jax.random.fold_in(key, 7)
    key_w, key_a, key_b, key_r = jax.random.split(key, 4)
    weights = jax.random.randint(key_w, (BUCKETS,), 1, 5)
    first = jax.random.randint(key_a, (), 0, BUCKETS)
    second = (first + 1 + jax.random.randint(key_b, (), 0, max(BUCKETS - 1, 1))) % BUCKETS
    weights = weights.at[first].set(4).at[second].set(4)
    rowid = jnp.arange(BUCKETS, dtype=jnp.int32)[:, None]
    colid = jnp.arange(BUCKETS, dtype=jnp.int32)[None, :]
    table = CAP * weights[:, None] * weights[None, :] // 16
    table = jnp.where(rowid == colid, 0, table).astype(jnp.int32)
    raw = jax.random.randint(key_r, (BUCKETS, BUCKETS, CAP), 0, 2 ** 20)
    lower = jnp.minimum(rowid, colid)
    upper = jnp.maximum(rowid, colid)
    shared = raw[lower, upper]
    slot = jnp.arange(CAP, dtype=jnp.int32)[None, None, :]
    keys = jnp.where(slot < table[:, :, None], shared * CAP + slot, 2 ** 20 * CAP + slot)
    order = jnp.argsort(keys, axis=-1, stable=True).astype(jnp.int32)
    inverse = jnp.argsort(order, axis=-1, stable=True).astype(jnp.int32)
    reverse = jnp.where((rowid < colid)[:, :, None], order, inverse).astype(jnp.int32)
    return (table, reverse.reshape(-1))


def draw_counts(key, part):
    return pair_tables(key)[0]


def draw_rev_pos(key, part):
    return pair_tables(key)[1]


def draw_directions(key, part):
    key = jax.random.fold_in(key, 11)
    key_z, key_p = jax.random.split(key)
    total = BUCKETS * EDGE_DEV
    height = jax.random.uniform(key_z, (total,), jnp.float32, -1.0, 1.0)
    angle = jax.random.uniform(key_p, (total,), jnp.float32, -math.pi, math.pi)
    radius = jnp.sqrt(jnp.maximum(1.0 - height * height, 0.0))
    return jnp.stack([radius * jnp.cos(angle), radius * jnp.sin(angle), height]).astype(jnp.float32)


def set_ends(result, key, smallest, largest):
    place = [jax.random.randint(jax.random.fold_in(key, axis), (), 0, length) for axis, length in enumerate(result.shape)]
    longest = result.shape.index(max(result.shape))
    neighbour = place[:longest] + [(place[longest] + 1) % result.shape[longest]] + place[longest + 1:]
    return result.at[tuple(place)].set(smallest).at[tuple(neighbour)].set(largest)


def levels(own_key, extent, cuts, low, high):
    gain, own = 1.0, jax.random.fold_in(own_key, 6)
    for dim, parts in cuts:
        draws = jnp.exp(jax.random.uniform(jax.random.fold_in(own, dim), (parts,), jnp.float32, low / len(cuts), high / len(cuts)))
        gain = gain * jnp.repeat(draws, extent[dim] // parts).reshape([-1 if axis == dim else 1 for axis in range(len(extent))])
    return gain


def noise(own_key, shape, width, limit, shards=(), kind=jnp.bfloat16):
    entries = jax.random.normal(own_key, shape, jnp.float32) * width
    if len(shards) > 0:
        entries = levels(own_key, shape, shards, -0.22, 0.18) * entries
    return jnp.clip(entries, min=-limit, max=limit).astype(kind)


def setup_inputs(seed: int = 0) -> dict:
    key_of = jax.random.split(jax.random.key(seed), 11)
    return {
        "edge_state": noise(key_of[0], (EDGES, D), 1.0, 6.0, ((0, 32),)),
        "directions": draw_directions(jax.random.fold_in(key_of[10], 71), 0),
        "src_atom": set_ends(jax.random.randint(key_of[2], (EDGES,), 0, SRC_ATOMS), jax.random.fold_in(key_of[2], 1), 0, SRC_ATOMS - 1).astype(jnp.int32),
        "dst_atom": set_ends(jax.random.randint(key_of[3], (EDGES,), 0, DST_ATOMS), jax.random.fold_in(key_of[3], 1), 0, DST_ATOMS - 1).astype(jnp.int32),
        "rev_pos": draw_rev_pos(jax.random.fold_in(key_of[10], 71), 0),
        "counts": draw_counts(jax.random.fold_in(key_of[10], 71), 0),
        "triplets": set_ends(jax.random.randint(key_of[6], (BLOCKS, PAIRS), 0, N_SRC * EDGE_DEV // BLK), jax.random.fold_in(key_of[6], 1), 0, (N_SRC * EDGE_DEV // BLK) - 1).astype(jnp.int32),
        "down_w": noise(key_of[7], (NBLK, D, TRIP), D ** -0.5, 0.25),
        "trip_w": noise(key_of[8], (NBLK, NSPH * TRIP, D), TRIP ** -0.5, 0.75),
        "edge_w": noise(key_of[9], (NBLK, 6, D, D), D ** -0.5, 0.25),
    }


def legendre(cosine):
    square = cosine * cosine
    return [cosine, 1.5 * square - 0.5, 2.5 * square * cosine - 1.5 * cosine, (35.0 * square * square - 30.0 * square + 3.0) / 8.0]


def silu(value):
    return value / (1.0 + jnp.exp(-value))


def reference(edge_state, directions, src_atom, dst_atom, rev_pos, counts, triplets, down_w, trip_w, edge_w):
    nblock = EDGE_DEV // BLK
    live = (jnp.arange(CAP)[None, None, :] < counts[:, :, None]).reshape(EDGES)
    live_f = live.astype(jnp.float32)[:, None]
    dirs_dev = directions.reshape(3, BUCKETS, nblock, BLK)
    dirs_grid = directions.reshape(3, N_SRC, N_DST, nblock, BLK)
    trip_dev = triplets.reshape(BUCKETS, nblock, PAIRS)
    tri_scale = (BLK * PAIRS) ** -0.5
    slot_dev = jnp.arange(EDGES, dtype=jnp.int32) // EDGE_DEV
    dst_id = (slot_dev % N_DST) * DST_ATOMS + dst_atom
    src_id = (slot_dev // N_DST) * SRC_ATOMS + src_atom
    state = edge_state
    for level in range(NBLK):
        lowered = (silu(jnp.dot(state, down_w[level], preferred_element_type=jnp.float32)) * live_f).astype(jnp.bfloat16)
        low_grid = lowered.reshape(N_SRC, N_DST, nblock, BLK, TRIP)

        def triple_for(flat):
            column = flat % N_DST
            local = dirs_dev[:, flat]
            pool_dirs = dirs_grid[:, :, column].reshape(3, N_SRC * nblock, BLK)
            chosen_dirs = pool_dirs[:, trip_dev[flat]]
            cosine = jnp.einsum("cbk,cbqm->bqkm", local, chosen_dirs, precision=lax.Precision.HIGHEST)
            tiles = jnp.stack(legendre(cosine)).astype(jnp.bfloat16)
            pool = low_grid[:, column].reshape(N_SRC * nblock, BLK, TRIP)
            chosen = pool[trip_dev[flat]]
            summed = jnp.einsum("lbqkm,bqmt->bklt", tiles.astype(jnp.float32), chosen.astype(jnp.float32))
            return (summed * tri_scale).reshape(EDGE_DEV, NSPH * TRIP).astype(jnp.bfloat16)

        triple = lax.map(triple_for, jnp.arange(BUCKETS, dtype=jnp.int32)).reshape(EDGES, NSPH * TRIP)
        layer_w = edge_w[level]
        pre = jnp.dot(state, layer_w[0], preferred_element_type=jnp.float32) + jnp.dot(triple, trip_w[level], preferred_element_type=jnp.float32)
        message = (silu(pre) * live_f).astype(jnp.bfloat16)
        swapped = message.reshape(BUCKETS, BUCKETS, CAP, D).transpose(1, 0, 2, 3)
        mirrored = jnp.take_along_axis(swapped, rev_pos.reshape(BUCKETS, BUCKETS, CAP, 1), axis=2).reshape(EDGES, D)
        symmetric = (message.astype(jnp.float32) + mirrored.astype(jnp.float32) * live_f).astype(jnp.bfloat16)
        inner = silu(jnp.dot(symmetric, layer_w[1], preferred_element_type=jnp.float32)).astype(jnp.bfloat16)
        refined = (symmetric.astype(jnp.float32) + jnp.dot(inner, layer_w[2], preferred_element_type=jnp.float32)).astype(jnp.bfloat16)
        totals = jax.ops.segment_sum(refined.astype(jnp.float32), dst_id, num_segments=ATOMS)
        atoms = (totals * (DEGREE ** -0.5)).astype(jnp.bfloat16)
        feed = atoms[src_id]
        joined = (refined.astype(jnp.float32) + feed.astype(jnp.float32)).astype(jnp.bfloat16)
        first = silu(jnp.dot(joined, layer_w[3], preferred_element_type=jnp.float32)).astype(jnp.bfloat16)
        second = silu(jnp.dot(first, layer_w[4], preferred_element_type=jnp.float32)).astype(jnp.bfloat16)
        update = state.astype(jnp.float32) + refined.astype(jnp.float32) + jnp.dot(second, layer_w[5], preferred_element_type=jnp.float32)
        state = (update * live_f * (0.5 ** 0.5)).astype(jnp.bfloat16)
    return state
```

```python
import functools

import jax
import jax.numpy as jnp
from jax import lax
from jax.experimental import pallas as pl
from jax.experimental.pallas import tpu as pltpu
from jax.sharding import PartitionSpec as P

BLK = 128
PAIRS = 4
NBLK = 2
NSPH = 4
ATOM_DEV = 32
DEGREE = 64
SB = 512
HALF = SB // 2
SPB = SB // BLK
VMEM_LIMIT = 48 * 1024 * 1024

F32 = jnp.float32
BF16 = jnp.bfloat16


def silu(value):
    half = 0.5 * value
    return half + half * jnp.tanh(half)


def dot(a, b):
    return jnp.dot(a, b, preferred_element_type=F32)


def legendre(cosine):
    square = cosine * cosine
    return [
        cosine,
        1.5 * square - 0.5,
        (2.5 * square - 1.5) * cosine,
        (35.0 * square * square - 30.0 * square + 3.0) * 0.125,
    ]


def masked(value, cap, counts):
    position = lax.broadcasted_iota(jnp.int32, (cap, value.shape[1]), 0)
    return [
        jnp.where(position < count, value[i * cap : (i + 1) * cap], 0.0)
        for i, count in enumerate(counts)
    ]


def pack(low):
    return jnp.concatenate([low[:HALF], low[HALF:]], axis=1)


def call(kernel, meta, args, in_specs, out_shape, out_specs, grid, scratch, flops, nbytes, aliases=None):
    return pl.pallas_call(
        kernel,
        grid_spec=pltpu.PrefetchScalarGridSpec(
            num_scalar_prefetch=1,
            grid=grid,
            in_specs=in_specs,
            out_specs=out_specs,
            scratch_shapes=scratch,
        ),
        out_shape=out_shape,
        input_output_aliases=aliases or {},
        compiler_params=pltpu.CompilerParams(vmem_limit_bytes=VMEM_LIMIT),
        cost_estimate=pl.CostEstimate(flops=flops, bytes_accessed=nbytes, transcendentals=0),
    )(meta, *args)


def whole(shape):
    return pl.BlockSpec(shape, lambda i, m: (0,) * len(shape))


def layer(level, index, width):
    return pl.BlockSpec((None, None, width, width), lambda i, m: (level, index, 0, 0))


def body(
    edge_state, directions, src_atom, dst_atom, rev_pos, counts, triplets, down_w, trip_w, edge_w
):
    n_src = lax.axis_size("src")
    n_dst = lax.axis_size("dst")
    n = n_src * n_dst
    rows, width = edge_state.shape
    trip = down_w.shape[2]
    cap = rows // n
    bps = SB // cap
    shift = bps.bit_length() - 1
    nsb = rows // SB
    nblock = rows // BLK
    group = n_dst // n_src
    dst_rows = ATOM_DEV * n_src
    region_rows = group * dst_rows
    prows = rows // 2
    both = ("src", "dst")

    s = lax.axis_index("src")
    d = lax.axis_index("dst")
    f = s * n_dst + d

    flat = triplets.reshape(-1)
    rel = (flat // nblock) ^ s
    block = flat % nblock
    pool_row = rel * prows + (block // SPB) * HALF + (block % (SPB // 2)) * BLK
    pool_half = (block % SPB) // (SPB // 2)
    pool_lane = block * BLK
    meta = jnp.concatenate(
        [jnp.stack([f, s]), counts.reshape(-1), pool_row, pool_half, rel, pool_lane]
    ).astype(jnp.int32)
    at_counts = 2
    at_row = at_counts + n
    at_half = at_row + nblock * PAIRS
    at_rel = at_half + nblock * PAIRS
    at_lane = at_rel + nblock * PAIRS

    def sb_of(m, g):
        return (m[0] >> shift) ^ g

    def low_bits(m):
        return m[0] & (bps - 1)

    def counts_abs(m, sb):
        return [m[at_counts + sb * bps + i] for i in range(bps)]

    def counts_rel(m, g):
        return [m[at_counts + (m[0] ^ (g * bps + i))] for i in range(bps)]

    def lower_kernel(m, state_ref, down_ref, out_ref):
        low = silu(dot(state_ref[...], down_ref[...]))
        low = masked(low, cap, counts_abs(m, pl.program_id(0)))
        out_ref[...] = pack(jnp.concatenate(low, axis=0).astype(BF16))

    lowered = call(
        lower_kernel,
        meta,
        (edge_state, down_w),
        [
            pl.BlockSpec((SB, width), lambda i, m: (i, 0)),
            pl.BlockSpec((None, width, trip), lambda i, m: (0, 0, 0)),
        ],
        jax.ShapeDtypeStruct((prows, 2 * trip), BF16),
        pl.BlockSpec((HALF, 2 * trip), lambda i, m: (i, 0)),
        (nsb,),
        [],
        2 * rows * width * trip,
        rows * width * 2,
    )

    def src_perm(i):
        return [(a, a ^ i) for a in range(n_src)]

    def gather_src(x):
        slots = [None] * n_src
        slots[0] = x
        for i in range(2, n_src, 2):
            slots[i] = lax.ppermute(x, "src", src_perm(i))
        for i in range(0, n_src, 2):
            slots[i + 1] = lax.ppermute(slots[i], "src", src_perm(1))
        return slots

    dirs_pool = [directions] + [
        lax.ppermute(directions, "src", src_perm(i)) for i in range(1, n_src)
    ]
    dirs_col = directions.T

    def tiles_kernel(m, col_ref, *refs):
        pool_refs, out_ref, pool = refs[:n_src], refs[n_src], refs[n_src + 1]
        c = pl.program_id(0)

        @pl.when(c == 0)
        def _():
            for i in range(n_src):
                pool[i] = pool_refs[i][...]

        col = col_ref[...]
        for q in range(PAIRS):
            which = c * PAIRS + q
            lane = pl.multiple_of(m[at_lane + which], BLK)
            chosen = pool[m[at_rel + which], :, pl.ds(lane, BLK)]
            cosine = (
                col[:, 0:1] * chosen[0:1] + col[:, 1:2] * chosen[1:2] + col[:, 2:3] * chosen[2:3]
            )
            for degree, tile in enumerate(legendre(cosine)):
                out_ref[degree, :, q * BLK : (q + 1) * BLK] = tile.astype(BF16)

    tiles = call(
        tiles_kernel,
        meta,
        (dirs_col, *dirs_pool),
        [pl.BlockSpec((BLK, 3), lambda i, m: (i, 0))] + [whole((3, rows))] * n_src,
        jax.ShapeDtypeStruct((nblock, NSPH, BLK, PAIRS * BLK), BF16),
        pl.BlockSpec((None, NSPH, BLK, PAIRS * BLK), lambda i, m: (i, 0, 0, 0)),
        (nblock,),
        [pltpu.VMEM((n_src, 3, rows), F32)],
        nblock * BLK * PAIRS * BLK * 2000,
        nblock * NSPH * BLK * PAIRS * BLK * 2,
    )

    order = f ^ jnp.arange(n, dtype=jnp.int32)
    ints = jnp.stack([rev_pos, src_atom, dst_atom]).reshape(3, n, cap)
    ints = jnp.take(ints, order, axis=1)
    live = jnp.arange(cap, dtype=jnp.int32)[None, :] < jnp.take(counts[0], order)[:, None]
    first_of = (jnp.arange(n, dtype=jnp.int32) * cap % HALF)[:, None]
    mirror = jnp.where(live, ints[0] + first_of, -1).reshape(rows)
    atom = ints[1].reshape(rows)
    which = (atom % dst_rows) // ATOM_DEV * group + atom // dst_rows
    atom_row = (which ^ d) * ATOM_DEV + atom % ATOM_DEV
    cols = jnp.stack([mirror, atom_row], axis=1)
    dst_rows_of = ints[2].reshape(nsb, 1, SB)

    tri_scale = (BLK * PAIRS) ** (-0.5)

    def message_call(level, g, state, pool):
        def kernel(m, tiles_ref, state_ref, w_ref, up_ref, *refs):
            pool_refs, out_refs = refs[:n_src], refs[n_src : n_src + bps]
            pool_all, hold = refs[n_src + bps :]
            sb = sb_of(m, g)
            for i in range(n_src):
                pool_all[i * prows : (i + 1) * prows, :] = pool_refs[i][...]
            blocks = []
            for c in range(SPB):
                chosen = []
                for q in range(PAIRS):
                    which = (sb * SPB + c) * PAIRS + q
                    x = pool_all[pl.ds(pl.multiple_of(m[at_row + which], BLK), BLK), :]
                    chosen.append(jnp.where(m[at_half + which] == 1, x[:, trip:], x[:, :trip]))
                summed = dot(
                    tiles_ref[c].reshape(NSPH * BLK, PAIRS * BLK), jnp.concatenate(chosen, axis=0)
                )
                summed = (summed * tri_scale).astype(BF16)
                blocks.append(
                    jnp.concatenate(
                        [summed[l * BLK : (l + 1) * BLK] for l in range(NSPH)], axis=1
                    )
                )
            triple = jnp.concatenate(blocks, axis=0)
            pre = dot(state_ref[...], w_ref[...]) + dot(triple, up_ref[...])
            for i, part in enumerate(masked(silu(pre), cap, counts_abs(m, sb))):
                hold[i * cap : (i + 1) * cap, :] = part.astype(BF16)
            for j in range(bps):
                start = pl.multiple_of((j ^ low_bits(m)) * cap, cap)
                out_refs[j][...] = hold[pl.ds(start, cap), :]

        return call(
            kernel,
            meta,
            (tiles, state, edge_w, trip_w, *pool),
            [
                pl.BlockSpec(
                    (SPB, NSPH, BLK, PAIRS * BLK), lambda i, m: (sb_of(m, g), 0, 0, 0)
                ),
                pl.BlockSpec((SB, width), lambda i, m: (sb_of(m, g), 0)),
                layer(level, 0, width),
                pl.BlockSpec((None, NSPH * trip, width), lambda i, m: (level, 0, 0)),
            ]
            + [whole((prows, 2 * trip))] * n_src,
            [jax.ShapeDtypeStruct((cap, width), BF16)] * bps,
            [whole((cap, width))] * bps,
            (1,),
            [pltpu.VMEM((n_src * prows, 2 * trip), BF16), pltpu.VMEM((SB, width), BF16)],
            2 * SB * width * (width + 2 * NSPH * trip) + 2 * SB * NSPH * 512 * 256,
            5 * 2**20,
        )

    def refine_call(level, g, mine, theirs, refined, sums):
        last = g == nsb - 1
        first = g == 0

        def kernel(m, col_ref, dst_ref, w1_ref, w2_ref, *refs):
            mine_refs, their_refs, refs = refs[:bps], refs[bps : 2 * bps], refs[2 * bps :]
            if not first:
                sums_ref, refs = refs[1], refs[2:]
            out_ref, sum_refs = refs[0], refs[1:]
            per = HALF // cap
            halves = []
            for h in range(SB // HALF):
                theirs_h = jnp.concatenate(
                    [r[...] for r in their_refs[h * per : (h + 1) * per]], axis=0
                )
                mine_h = jnp.concatenate(
                    [r[...] for r in mine_refs[h * per : (h + 1) * per]], axis=0
                )
                target = col_ref[h * HALF : (h + 1) * HALF, 0:1]
                lanes = lax.broadcasted_iota(jnp.int32, (HALF, HALF), 1)
                pick = jnp.where(lanes == target, 1.0, 0.0).astype(BF16)
                halves.append(mine_h.astype(F32) + dot(pick, theirs_h))
            symmetric = jnp.concatenate(halves, axis=0).astype(BF16)
            inner = silu(dot(symmetric, w1_ref[...])).astype(BF16)
            out = (symmetric.astype(F32) + dot(inner, w2_ref[...])).astype(BF16)
            out_ref[...] = out
            atoms = lax.broadcasted_iota(jnp.int32, (dst_rows, SB), 0)
            onehot = jnp.where(atoms == dst_ref[...], 1.0, 0.0).astype(BF16)
            total = dot(onehot, out)
            if not first:
                total = total + sums_ref[...]
            if last:
                hold = sum_refs[n_src]
                hold[...] = total
                for i in range(n_src):
                    start = pl.multiple_of((m[1] ^ i) * ATOM_DEV, ATOM_DEV)
                    sum_refs[i][...] = hold[pl.ds(start, ATOM_DEV), :].astype(BF16)
            else:
                sum_refs[0][...] = total

        args = (cols, dst_rows_of, edge_w, edge_w, *mine, *theirs)
        in_specs = (
            [
                pl.BlockSpec((SB, 2), lambda i, m: (g, 0)),
                pl.BlockSpec((None, 1, SB), lambda i, m: (g, 0, 0)),
                layer(level, 1, width),
                layer(level, 2, width),
            ]
            + [whole((cap, width))] * (2 * bps)
        )
        aliases = {}
        if not first:
            aliases = {1 + len(args): 0}
            args = (*args, refined, sums)
            in_specs = in_specs + [pl.BlockSpec(memory_space=pl.ANY), whole((dst_rows, width))]
        if last:
            sum_shape = [jax.ShapeDtypeStruct((ATOM_DEV, width), BF16)] * n_src
            sum_specs = [whole((ATOM_DEV, width))] * n_src
            scratch = [pltpu.VMEM((dst_rows, width), F32)]
        else:
            sum_shape = [jax.ShapeDtypeStruct((dst_rows, width), F32)]
            sum_specs = [whole((dst_rows, width))]
            scratch = []
        out = call(
            kernel,
            meta,
            args,
            in_specs,
            [jax.ShapeDtypeStruct((rows, width), BF16)] + sum_shape,
            [pl.BlockSpec((SB, width), lambda i, m: (g, 0))] + sum_specs,
            (1,),
            scratch,
            2 * SB * width * (2 * width + HALF + dst_rows),
            4 * 2**20,
            aliases,
        )
        return out[0], (out[1:] if last else out[1])

    def update_call(level, state, refined, pieces):
        last = level == NBLK - 1

        def kernel(m, col_ref, state_ref, refined_ref, w3_ref, w4_ref, w5_ref, down_ref, *refs):
            piece_refs, refs = refs[:n_dst], refs[n_dst:]
            out_ref, refs = refs[0], refs[1:]
            region = refs[-1]
            g = pl.program_id(0)
            sb = sb_of(m, g)

            @pl.when(g == 0)
            def _():
                for i in range(n_dst):
                    region[i * ATOM_DEV : (i + 1) * ATOM_DEV, :] = piece_refs[i][...]

            refined_v = refined_ref[...].astype(F32)
            lanes = lax.broadcasted_iota(jnp.int32, (SB, region_rows), 1)
            pick = jnp.where(lanes == col_ref[:, 1:2], 1.0, 0.0).astype(BF16)
            joined = (refined_v + dot(pick, region[...])).astype(BF16)
            one = silu(dot(joined, w3_ref[...])).astype(BF16)
            two = silu(dot(one, w4_ref[...])).astype(BF16)
            delta = refined_v + dot(two, w5_ref[...])
            parts = masked(delta, cap, counts_rel(m, g))
            position = lax.broadcasted_iota(jnp.int32, (cap, width), 0)
            for j, count in enumerate(counts_rel(m, g)):
                start = pl.multiple_of((j ^ low_bits(m)) * cap, cap)
                old = state_ref[pl.ds(start, cap), :].astype(F32)
                new = jnp.where(position < count, (old + parts[j]) * (0.5**0.5), 0.0)
                out_ref[pl.ds(start, cap), :] = new.astype(BF16)
            if not last:
                low = silu(dot(out_ref[...], down_ref[...]))
                low = masked(low, cap, counts_abs(m, sb))
                refs[0][...] = pack(jnp.concatenate(low, axis=0).astype(BF16))

        out_shape = [jax.ShapeDtypeStruct((rows, width), BF16)]
        out_specs = [pl.BlockSpec((SB, width), lambda i, m: (sb_of(m, i), 0))]
        if not last:
            out_shape.append(jax.ShapeDtypeStruct((prows, 2 * trip), BF16))
            out_specs.append(pl.BlockSpec((HALF, 2 * trip), lambda i, m: (sb_of(m, i), 0)))
        return call(
            kernel,
            meta,
            (cols, state, refined, edge_w, edge_w, edge_w, down_w, *pieces),
            [
                pl.BlockSpec((SB, 2), lambda i, m: (i, 0)),
                pl.BlockSpec((SB, width), lambda i, m: (sb_of(m, i), 0)),
                pl.BlockSpec((SB, width), lambda i, m: (i, 0)),
                layer(level, 3, width),
                layer(level, 4, width),
                layer(level, 5, width),
                pl.BlockSpec(
                    (None, width, trip), lambda i, m: (min(level + 1, NBLK - 1), 0, 0)
                ),
            ]
            + [whole((ATOM_DEV, width))] * n_dst,
            out_shape,
            out_specs,
            (nsb,),
            [pltpu.VMEM((region_rows, width), BF16)],
            2 * rows * width * (3 * width + region_rows + trip),
            8 * 2**20,
        )

    state = edge_state
    for level in range(NBLK):
        pool = gather_src(lowered)
        mine, theirs = [], []
        for g in range(nsb):
            out = message_call(level, g, state, pool)
            mine.append(out)
            theirs.append(
                [
                    lax.ppermute(out[j], both, [(a, a ^ (g * bps + j)) for a in range(n)])
                    if g * bps + j
                    else out[j]
                    for j in range(bps)
                ]
            )
        refined, sums = None, None
        for g in range(nsb):
            refined, sums = refine_call(level, g, mine[g], theirs[g], refined, sums)
        parts = []
        for i in range(n_src):
            perm = []
            for a in range(n):
                sa, ua, ja = a // n_dst, (a % n_dst) // group, a % group
                perm.append((a, ua * n_dst + (sa ^ i) * group + ja))
            parts.append(lax.ppermute(sums[i], both, perm))
        total = functools.reduce(lambda a, b: a + b, [p.astype(F32) for p in parts])
        piece = (total * DEGREE ** (-0.5)).astype(BF16)
        pieces = [piece] + [
            lax.ppermute(piece, "dst", [(a, a ^ i) for a in range(n_dst)])
            for i in range(1, n_dst)
        ]
        out = update_call(level, state, refined, pieces)
        state = out[0]
        if level < NBLK - 1:
            lowered = out[1]
    return state


def solution(mesh):
    placed = (
        P(("src", "dst"), None),
        P(None, ("src", "dst")),
        P(("src", "dst")),
        P(("src", "dst")),
        P(("src", "dst")),
        P(("src", "dst"), None),
        P(("src", "dst"), None),
        P(),
        P(),
        P(),
    )
    return jax.shard_map(
        body, mesh=mesh, in_specs=placed, out_specs=P(("src", "dst"), None), check_vma=False
    )
```

```python
import functools

import jax
import jax.numpy as jnp
from jax import lax
from jax.experimental import pallas as pl
from jax.experimental.pallas import tpu as pltpu
from jax.sharding import PartitionSpec as P

BLK = 128
PAIRS = 4
NBLK = 2
NSPH = 4
ATOM_DEV = 32
DEGREE = 64
SB = 512
HALF = SB // 2
SPB = SB // BLK
VMEM_LIMIT = 40 * 1024 * 1024

F32 = jnp.float32
BF16 = jnp.bfloat16


def silu(value):
    half = 0.5 * value
    return half + half * jnp.tanh(half)


def dot(a, b):
    return jnp.dot(a, b, preferred_element_type=F32)


def dot_first(a, b):
    return lax.dot_general(a, b, (((0,), (0,)), ((), ())), preferred_element_type=F32)


def legendre(cosine):
    square = cosine * cosine
    return [
        cosine,
        1.5 * square - 0.5,
        (2.5 * square - 1.5) * cosine,
        (35.0 * square * square - 30.0 * square + 3.0) * 0.125,
    ]


def masked(value, cap, counts):
    position = lax.broadcasted_iota(jnp.int32, (cap, value.shape[1]), 0)
    parts = [
        jnp.where(position < count, value[i * cap : (i + 1) * cap], 0.0)
        for i, count in enumerate(counts)
    ]
    return jnp.concatenate(parts, axis=0)


def pack(low):
    return jnp.concatenate([low[:HALF], low[HALF:]], axis=1)


def call(kernel, meta, args, in_specs, out_shape, out_specs, grid, scratch, flops, nbytes):
    return pl.pallas_call(
        kernel,
        grid_spec=pltpu.PrefetchScalarGridSpec(
            num_scalar_prefetch=1,
            grid=grid,
            in_specs=in_specs,
            out_specs=out_specs,
            scratch_shapes=scratch,
        ),
        out_shape=out_shape,
        compiler_params=pltpu.CompilerParams(vmem_limit_bytes=VMEM_LIMIT),
        cost_estimate=pl.CostEstimate(flops=flops, bytes_accessed=nbytes, transcendentals=0),
    )(meta, *args)


def whole(shape):
    return pl.BlockSpec(shape, lambda i, m: (0,) * len(shape))


def step(shape):
    return pl.BlockSpec(shape, lambda i, m: (i,) + (0,) * (len(shape) - 1))


def layer(level, index, width):
    return pl.BlockSpec((None, None, width, width), lambda i, m: (level, index, 0, 0))


def body(
    edge_state, directions, src_atom, dst_atom, rev_pos, counts, triplets, down_w, trip_w, edge_w
):
    n_src = lax.axis_size("src")
    n_dst = lax.axis_size("dst")
    n = n_src * n_dst
    rows, width = edge_state.shape
    trip = down_w.shape[2]
    cap = rows // n
    bps = SB // cap
    nsb = rows // SB
    nblock = rows // BLK
    group = n_dst // n_src
    dst_rows = ATOM_DEV * n_src
    region_rows = group * dst_rows
    prows = rows // 2
    both = ("src", "dst")

    s = lax.axis_index("src")

    flat = triplets.reshape(-1)
    block = flat % nblock
    pool_row = ((flat // nblock) ^ s) * prows + (block // SPB) * HALF + (block % (SPB // 2)) * BLK
    pool_half = (block % SPB) // (SPB // 2)
    meta = jnp.concatenate([s[None], counts.reshape(-1), pool_row, pool_half, flat * BLK])
    meta = meta.astype(jnp.int32)
    at_counts = 1
    at_row = at_counts + n
    at_half = at_row + nblock * PAIRS
    at_lane = at_half + nblock * PAIRS

    def counts_of(m):
        first = at_counts + pl.program_id(0) * bps
        return [m[first + i] for i in range(bps)]

    def lower_kernel(m, state_ref, down_ref, out_ref):
        low = silu(dot(state_ref[...], down_ref[...]))
        out_ref[...] = pack(masked(low, cap, counts_of(m)).astype(BF16))

    lowered = call(
        lower_kernel,
        meta,
        (edge_state, down_w),
        [step((SB, width)), pl.BlockSpec((None, width, trip), lambda i, m: (0, 0, 0))],
        jax.ShapeDtypeStruct((prows, 2 * trip), BF16),
        step((HALF, 2 * trip)),
        (nsb,),
        [],
        2 * rows * width * trip,
        rows * width * 2,
    )

    def src_perm(i):
        return [(a, a ^ i) for a in range(n_src)]

    def gather_src(x):
        slots = [None] * n_src
        slots[0] = x
        for i in range(2, n_src, 2):
            slots[i] = lax.ppermute(x, "src", src_perm(i))
        for i in range(0, n_src, 2):
            slots[i + 1] = lax.ppermute(slots[i], "src", src_perm(1))
        return slots

    dirs_pool = lax.all_gather(directions, "src", axis=1, tiled=True)

    def tiles_kernel(m, own_ref, pool_ref, out_ref):
        first = pl.program_id(0) * SPB
        own = jnp.concatenate([own_ref[...], jnp.zeros((5, SB), F32)], axis=0)
        col = own.T
        for c in range(SPB):
            col_c = col[c * BLK : (c + 1) * BLK]
            for q in range(PAIRS):
                lane = pl.multiple_of(m[at_lane + (first + c) * PAIRS + q], BLK)
                chosen = pool_ref[:, pl.ds(lane, BLK)]
                cosine = (
                    col_c[:, 0:1] * chosen[0:1]
                    + col_c[:, 1:2] * chosen[1:2]
                    + col_c[:, 2:3] * chosen[2:3]
                )
                for degree, tile in enumerate(legendre(cosine)):
                    out_ref[c, degree, :, q * BLK : (q + 1) * BLK] = tile.astype(BF16)

    tiles = call(
        tiles_kernel,
        meta,
        (directions, dirs_pool),
        [
            pl.BlockSpec((3, SB), lambda i, m: (0, i)),
            whole((3, n_src * rows)),
        ],
        jax.ShapeDtypeStruct((nblock, NSPH, BLK, PAIRS * BLK), BF16),
        step((SPB, NSPH, BLK, PAIRS * BLK)),
        (nsb,),
        [],
        nblock * BLK * PAIRS * BLK * 2000,
        nblock * NSPH * BLK * PAIRS * BLK * 2,
    )

    rev_row = rev_pos.reshape(nsb, 1, SB)
    dst_row = dst_atom.reshape(nsb, 1, SB)
    src_row = src_atom.reshape(nsb, 1, SB)
    row_spec = step((None, 1, SB))
    tri_scale = (BLK * PAIRS) ** (-0.5)
    chunks = range(SB // HALF)

    def split(value):
        return [value[h * HALF : (h + 1) * HALF] for h in chunks]

    def message_call(level, state, pool):
        def kernel(m, tiles_ref, state_ref, w_ref, up_ref, rev_ref, *refs):
            pool_refs, (mine_ref, send_ref, pool_all) = refs[:n_src], refs[n_src:]
            first = pl.program_id(0) * SPB

            @pl.when(pl.program_id(0) == 0)
            def _():
                for i in range(n_src):
                    pool_all[i * prows : (i + 1) * prows, :] = pool_refs[i][...]

            blocks = []
            for c in range(SPB):
                chosen = []
                for q in range(PAIRS):
                    which = (first + c) * PAIRS + q
                    x = pool_all[pl.ds(pl.multiple_of(m[at_row + which], BLK), BLK), :]
                    chosen.append(jnp.where(m[at_half + which] == 1, x[:, trip:], x[:, :trip]))
                summed = dot(
                    tiles_ref[c].reshape(NSPH * BLK, PAIRS * BLK), jnp.concatenate(chosen, axis=0)
                )
                summed = (summed * tri_scale).astype(BF16)
                blocks.append(
                    jnp.concatenate(
                        [summed[l * BLK : (l + 1) * BLK] for l in range(NSPH)], axis=1
                    )
                )
            triple = jnp.concatenate(blocks, axis=0)
            counts_here = counts_of(m)
            per = HALF // cap
            target_row = lax.broadcasted_iota(jnp.int32, (HALF, HALF), 0)
            base = lax.broadcasted_iota(jnp.int32, (1, HALF), 1) // cap * cap
            pre = [
                dot(x, w_ref[...]) + dot(t, up_ref[...])
                for x, t in zip(split(state_ref[...]), split(triple))
            ]
            for h in chunks:
                message = masked(silu(pre[h]), cap, counts_here[h * per : (h + 1) * per])
                message = message.astype(BF16)
                at = slice(h * HALF, (h + 1) * HALF)
                mine_ref[at, :] = message
                pick = jnp.where(target_row == rev_ref[:, at] + base, 1.0, 0.0).astype(BF16)
                send_ref[at, :] = dot(pick, message).astype(BF16)

        return call(
            kernel,
            meta,
            (tiles, state, edge_w, trip_w, rev_row, *pool),
            [
                step((SPB, NSPH, BLK, PAIRS * BLK)),
                step((SB, width)),
                layer(level, 0, width),
                pl.BlockSpec((None, NSPH * trip, width), lambda i, m: (level, 0, 0)),
                row_spec,
            ]
            + [whole((prows, 2 * trip))] * n_src,
            [jax.ShapeDtypeStruct((rows, width), BF16)] * 2,
            [step((SB, width))] * 2,
            (nsb,),
            [pltpu.VMEM((n_src * prows, 2 * trip), BF16)],
            2 * rows * width * (width + 2 * NSPH * trip) + 2 * rows * NSPH * 512 * 256,
            16 * 2**20,
        )

    def refine_call(level, mine, theirs):
        def kernel(m, dst_ref, w1_ref, w2_ref, mine_ref, theirs_ref, out_ref, *refs):
            sum_refs, total = refs[:n_src], refs[n_src]
            g = pl.program_id(0)
            symmetric = [
                (a.astype(F32) + b.astype(F32)).astype(BF16)
                for a, b in zip(split(mine_ref[...]), split(theirs_ref[...]))
            ]
            inner = [silu(dot(x, w1_ref[...])).astype(BF16) for x in symmetric]
            for h in chunks:
                out = (symmetric[h].astype(F32) + dot(inner[h], w2_ref[...])).astype(BF16)
                out_ref[h * HALF : (h + 1) * HALF, :] = out
            atoms = lax.broadcasted_iota(jnp.int32, (dst_rows, SB), 0)
            onehot = jnp.where(atoms == dst_ref[...], 1.0, 0.0).astype(BF16)
            part = dot(onehot, out_ref[...])

            @pl.when(g == 0)
            def _():
                total[...] = part

            @pl.when(g > 0)
            def _():
                total[...] += part

            @pl.when(g == nsb - 1)
            def _():
                for i in range(n_src):
                    start = pl.multiple_of((m[0] ^ i) * ATOM_DEV, ATOM_DEV)
                    sum_refs[i][...] = total[pl.ds(start, ATOM_DEV), :].astype(BF16)

        out = call(
            kernel,
            meta,
            (dst_row, edge_w, edge_w, mine, theirs),
            [row_spec, layer(level, 1, width), layer(level, 2, width)] + [step((SB, width))] * 2,
            [jax.ShapeDtypeStruct((rows, width), BF16)]
            + [jax.ShapeDtypeStruct((ATOM_DEV, width), BF16)] * n_src,
            [step((SB, width))] + [whole((ATOM_DEV, width))] * n_src,
            (nsb,),
            [pltpu.VMEM((dst_rows, width), F32)],
            2 * rows * width * (2 * width + dst_rows),
            8 * 2**20,
        )
        return out[0], out[1:]

    def update_call(level, state, refined, pieces):
        last = level == NBLK - 1

        def kernel(m, src_ref, state_ref, refined_ref, w3_ref, w4_ref, w5_ref, down_ref, *refs):
            pieces_ref, out_ref, region = refs[0], refs[1], refs[-1]

            @pl.when(pl.program_id(0) == 0)
            def _():
                for i in range(n_dst):
                    region[i * ATOM_DEV : (i + 1) * ATOM_DEV, :] = pieces_ref[
                        :, i * width : (i + 1) * width
                    ]

            atom = src_ref[...]
            where = (atom % dst_rows) // ATOM_DEV * group + atom // dst_rows
            where = where * ATOM_DEV + atom % ATOM_DEV
            lines = lax.broadcasted_iota(jnp.int32, (region_rows, SB), 0)
            pick = jnp.where(lines == where, 1.0, 0.0).astype(BF16)
            feed = split(dot_first(pick, region[...]))
            refined_v = [x.astype(F32) for x in split(refined_ref[...])]
            joined = [(a + b).astype(BF16) for a, b in zip(refined_v, feed)]
            one = [silu(dot(x, w3_ref[...])).astype(BF16) for x in joined]
            two = [silu(dot(x, w4_ref[...])).astype(BF16) for x in one]
            counts_here = counts_of(m)
            per = HALF // cap
            low = []
            for h in chunks:
                at = slice(h * HALF, (h + 1) * HALF)
                new = state_ref[at, :].astype(F32) + refined_v[h] + dot(two[h], w5_ref[...])
                new = masked(new * (0.5**0.5), cap, counts_here[h * per : (h + 1) * per])
                new = new.astype(BF16)
                out_ref[at, :] = new
                if not last:
                    value = silu(dot(new, down_ref[...]))
                    low.append(masked(value, cap, counts_here[h * per : (h + 1) * per]))
            if not last:
                refs[2][...] = jnp.concatenate(low, axis=1).astype(BF16)

        out_shape = [jax.ShapeDtypeStruct((rows, width), BF16)]
        out_specs = [step((SB, width))]
        if not last:
            out_shape.append(jax.ShapeDtypeStruct((prows, 2 * trip), BF16))
            out_specs.append(step((HALF, 2 * trip)))
        return call(
            kernel,
            meta,
            (src_row, state, refined, edge_w, edge_w, edge_w, down_w, pieces),
            [
                row_spec,
                step((SB, width)),
                step((SB, width)),
                layer(level, 3, width),
                layer(level, 4, width),
                layer(level, 5, width),
                pl.BlockSpec(
                    (None, width, trip), lambda i, m: (min(level + 1, NBLK - 1), 0, 0)
                ),
                whole((ATOM_DEV, n_dst * width)),
            ],
            out_shape,
            out_specs,
            (nsb,),
            [pltpu.VMEM((region_rows, width), BF16)],
            2 * rows * width * (3 * width + region_rows + trip),
            8 * 2**20,
        )

    state = edge_state
    for level in range(NBLK):
        pool = gather_src(lowered)
        mine, send = message_call(level, state, pool)
        theirs = lax.all_to_all(
            send.reshape(n, cap, width), both, split_axis=0, concat_axis=0, tiled=True
        )
        refined, sums = refine_call(level, mine, theirs.reshape(rows, width))
        parts = []
        for i in range(n_src):
            perm = []
            for a in range(n):
                sa, ua, ja = a // n_dst, (a % n_dst) // group, a % group
                perm.append((a, ua * n_dst + (sa ^ i) * group + ja))
            parts.append(lax.ppermute(sums[i], both, perm))
        total = functools.reduce(lambda a, b: a + b, [p.astype(F32) for p in parts])
        piece = (total * DEGREE ** (-0.5)).astype(BF16)
        pieces = lax.all_gather(piece, "dst", axis=1, tiled=True)
        out = update_call(level, state, refined, pieces)
        state = out[0]
        if level < NBLK - 1:
            lowered = out[1]
    return state


def solution(mesh):
    placed = (
        P(("src", "dst"), None),
        P(None, ("src", "dst")),
        P(("src", "dst")),
        P(("src", "dst")),
        P(("src", "dst")),
        P(("src", "dst"), None),
        P(("src", "dst"), None),
        P(),
        P(),
        P(),
    )
    return jax.shard_map(
        body, mesh=mesh, in_specs=placed, out_specs=P(("src", "dst"), None), check_vma=False
    )
```

```python
import functools

import jax
import jax.numpy as jnp
from jax import lax
from jax.experimental import pallas as pl
from jax.experimental.pallas import tpu as pltpu
from jax.sharding import PartitionSpec as P

BLK = 128
PAIRS = 4
NBLK = 2
NSPH = 4
ATOM_DEV = 32
DEGREE = 64
VMEM_LIMIT = 28 * 1024 * 1024

F32 = jnp.float32
BF16 = jnp.bfloat16


def silu(value):
    half = 0.5 * value
    return half + half * jnp.tanh(half)


def dot(a, b):
    return jnp.dot(a, b, preferred_element_type=F32)


def dot_last(a, b):
    return lax.dot_general(a, b, (((1,), (1,)), ((), ())), preferred_element_type=F32)


def dot_first(a, b):
    return lax.dot_general(a, b, (((0,), (0,)), ((), ())), preferred_element_type=F32)


def legendre(cosine):
    square = cosine * cosine
    return [
        cosine,
        1.5 * square - 0.5,
        (2.5 * square - 1.5) * cosine,
        (35.0 * square * square - 30.0 * square + 3.0) * 0.125,
    ]


def masked(value, cap, counts):
    position = lax.broadcasted_iota(jnp.int32, (cap, value.shape[1]), 0)
    parts = [
        jnp.where(position < count, value[i * cap : (i + 1) * cap], 0.0)
        for i, count in enumerate(counts)
    ]
    return jnp.concatenate(parts, axis=0)


def pack(low):
    half = low.shape[0] // 2
    return jnp.concatenate([low[:half], low[half:]], axis=1)


def call(
    kernel, meta, args, in_specs, out_shape, out_specs, grid, scratch, flops, nbytes,
    aliases=None, limit=VMEM_LIMIT,
):
    return pl.pallas_call(
        kernel,
        grid_spec=pltpu.PrefetchScalarGridSpec(
            num_scalar_prefetch=len(meta),
            grid=grid,
            in_specs=in_specs,
            out_specs=out_specs,
            scratch_shapes=scratch,
        ),
        out_shape=out_shape,
        input_output_aliases=aliases or {},
        compiler_params=pltpu.CompilerParams(vmem_limit_bytes=limit),
        cost_estimate=pl.CostEstimate(flops=flops, bytes_accessed=nbytes, transcendentals=0),
    )(*meta, *args)


def whole(shape):
    return pl.BlockSpec(shape, lambda i, *m: (0,) * len(shape))


def step(shape):
    return pl.BlockSpec(shape, lambda i, *m: (i,) + (0,) * (len(shape) - 1))


def layer(level, index, width):
    return pl.BlockSpec((None, None, width, width), lambda i, *m: (level, index, 0, 0))


def body(
    edge_state, directions, src_atom, dst_atom, rev_pos, counts, triplets, down_w, trip_w, edge_w
):
    n_src = lax.axis_size("src")
    n_dst = lax.axis_size("dst")
    n = n_src * n_dst
    rows, width = edge_state.shape
    trip = down_w.shape[2]
    cap = rows // n
    sb = rows // n_src
    spb = sb // BLK
    half = sb // 2
    chunk = min(sb, 256)
    groups = n_src // 2
    nblock = rows // BLK
    ratio = n_dst // n_src
    dst_rows = ATOM_DEV * n_src
    region_rows = ratio * dst_rows
    prows = rows // 2
    both = ("src", "dst")
    chunks = range(sb // chunk)
    per = chunk // cap

    s = lax.axis_index("src")
    d = lax.axis_index("dst")

    cnt = counts.reshape(-1)
    flat = triplets.T.reshape(-1)
    block = flat % nblock
    pool_row = ((flat // nblock) ^ s) * prows + block // spb * half + block % (spb // 2) * BLK
    pool_half = (block % spb) // (spb // 2)
    meta = jnp.concatenate([jnp.stack([s, d]), pool_row, pool_half, flat * BLK]).astype(jnp.int32)
    at_row = 2
    at_half = at_row + nblock * PAIRS
    at_lane = at_half + nblock * PAIRS
    down_t = jnp.swapaxes(down_w, 1, 2)

    def counts_at(cnt_ref, block, h=None):
        first = block * n_dst + (0 if h is None else h * per)
        return [cnt_ref[first + i] for i in range(n_dst if h is None else per)]

    def split(value):
        return [value[h * chunk : (h + 1) * chunk] for h in chunks]

    def lower_kernel(cnt_ref, state_ref, down_ref, out_ref):
        low = silu(dot_last(state_ref[...], down_ref[...]))
        low = masked(low, cap, counts_at(cnt_ref, pl.program_id(0)))
        out_ref[...] = pack(low.astype(BF16))

    lowered = call(
        lower_kernel,
        (cnt,),
        (edge_state, down_t),
        [step((sb, width)), pl.BlockSpec((None, trip, width), lambda i, *m: (0, 0, 0))],
        jax.ShapeDtypeStruct((prows, 2 * trip), BF16),
        step((half, 2 * trip)),
        (n_src,),
        [],
        2 * rows * width * trip,
        rows * width * 2,
        limit=60 * 2**20,
    )

    def src_perm(i):
        return [(a, a ^ i) for a in range(n_src)]

    def gather_src(x):
        slots = [None] * n_src
        slots[0] = x
        for i in range(2, n_src, 2):
            slots[i] = lax.ppermute(x, "src", src_perm(i))
        for i in range(0, n_src, 2):
            slots[i + 1] = lax.ppermute(slots[i], "src", src_perm(1))
        return slots

    own_dirs, _ = lax.optimization_barrier((directions, lowered))
    dirs_pool = lax.all_gather(own_dirs, "src", axis=1, tiled=True)

    def tiles_kernel(m, own_ref, pool_ref, out_ref):
        first = pl.program_id(0) * spb
        own = jnp.concatenate([own_ref[...], jnp.zeros((5, sb), F32)], axis=0)
        col = own.T
        for c in range(spb):
            col_c = col[c * BLK : (c + 1) * BLK]
            for q in range(PAIRS):
                lane = pl.multiple_of(m[at_lane + q * nblock + first + c], BLK)
                chosen = pool_ref[:, pl.ds(lane, BLK)]
                cosine = (
                    col_c[:, 0:1] * chosen[0:1]
                    + col_c[:, 1:2] * chosen[1:2]
                    + col_c[:, 2:3] * chosen[2:3]
                )
                for degree, tile in enumerate(legendre(cosine)):
                    out_ref[c, degree, :, q * BLK : (q + 1) * BLK] = tile.astype(BF16)

    tiles = call(
        tiles_kernel,
        (meta,),
        (directions, dirs_pool),
        [pl.BlockSpec((3, sb), lambda i, *m: (0, i)), whole((3, n_src * rows))],
        jax.ShapeDtypeStruct((nblock, NSPH, BLK, PAIRS * BLK), BF16),
        step((spb, NSPH, BLK, PAIRS * BLK)),
        (n_src,),
        [],
        nblock * BLK * PAIRS * BLK * 2000,
        nblock * NSPH * BLK * PAIRS * BLK * 2,
        limit=60 * 2**20,
    )

    rev_row = rev_pos.reshape(n_src, 1, sb)
    dst_row = dst_atom.reshape(n_src, 1, sb)
    src_row = src_atom.reshape(n_src, 1, sb)
    tri_scale = (BLK * PAIRS) ** (-0.5)

    def here(m, x, i):
        return m[0] ^ (2 * x) ^ 1 ^ i

    def message_call(level, x, state, pool):
        def kernel(cnt_ref, m, tiles_ref, state_ref, w_ref, up_ref, rev_ref, *refs):
            pool_refs, refs = refs[:n_src], refs[n_src:]
            mine_ref, give_ref, keep_ref, pool_all, hold = refs
            i = pl.program_id(0)
            at_block = here(m, x, i)

            @pl.when(i == 0)
            def _():
                for k in range(n_src):
                    pool_all[k * prows : (k + 1) * prows, :] = pool_refs[k][...]

            blocks = []
            for c in range(spb):
                chosen = []
                for q in range(PAIRS):
                    which = q * nblock + at_block * spb + c
                    v = pool_all[pl.ds(pl.multiple_of(m[at_row + which], BLK), BLK), :]
                    chosen.append(jnp.where(m[at_half + which] == 1, v[:, trip:], v[:, :trip]))
                summed = dot(
                    tiles_ref[c].reshape(NSPH * BLK, PAIRS * BLK), jnp.concatenate(chosen, axis=0)
                )
                summed = (summed * tri_scale).astype(BF16)
                blocks.append(
                    jnp.concatenate(
                        [summed[l * BLK : (l + 1) * BLK] for l in range(NSPH)], axis=1
                    )
                )
            triple = jnp.concatenate(blocks, axis=0)
            target_row = lax.broadcasted_iota(jnp.int32, (chunk, chunk), 0)
            base = lax.broadcasted_iota(jnp.int32, (1, chunk), 1) // cap * cap
            pre = [
                dot(v, w_ref[...]) + dot(t, up_ref[...])
                for v, t in zip(split(state_ref[...]), split(triple))
            ]
            for h in chunks:
                message = masked(silu(pre[h]), cap, counts_at(cnt_ref, at_block, h)).astype(BF16)
                at = slice(h * chunk, (h + 1) * chunk)
                mine_ref[at, :] = message
                pick = jnp.where(target_row == rev_ref[:, at] + base, 1.0, 0.0).astype(BF16)
                hold[at, :] = dot(pick, message).astype(BF16)
            for out_ref, when in ((give_ref, 0), (keep_ref, 1)):

                @pl.when(i == when)
                def _(out_ref=out_ref):
                    for j in range(n_dst):
                        start = pl.multiple_of((m[1] ^ j) * cap, cap)
                        out_ref[j * cap : (j + 1) * cap, :] = hold[pl.ds(start, cap), :]

        return call(
            kernel,
            (cnt, meta),
            (tiles, state, edge_w, trip_w, rev_row, *pool),
            [
                pl.BlockSpec(
                    (spb, NSPH, BLK, PAIRS * BLK), lambda i, c, m: (here(m, x, i), 0, 0, 0)
                ),
                pl.BlockSpec((sb, width), lambda i, c, m: (here(m, x, i), 0)),
                layer(level, 0, width),
                pl.BlockSpec((None, NSPH * trip, width), lambda i, *m: (level, 0, 0)),
                pl.BlockSpec((None, 1, sb), lambda i, c, m: (here(m, x, i), 0, 0)),
            ]
            + [whole((prows, 2 * trip))] * n_src,
            [jax.ShapeDtypeStruct((2 * sb, width), BF16)]
            + [jax.ShapeDtypeStruct((sb, width), BF16)] * 2,
            [pl.BlockSpec((sb, width), lambda i, c, m: (here(m, x, i) & 1, 0))]
            + [whole((sb, width))] * 2,
            (2,),
            [pltpu.VMEM((n_src * prows, 2 * trip), BF16), pltpu.VMEM((sb, width), BF16)],
            4 * sb * width * (width + 2 * NSPH * trip) + 4 * sb * NSPH * 512 * 256,
            9 * 2**20,
        )

    def join_call(keep, received):
        def kernel(keep_ref, received_ref, *out_refs):
            for j, out_ref in enumerate(out_refs):
                out_ref[:cap, :] = keep_ref[j * cap : (j + 1) * cap, :]
                out_ref[cap:, :] = received_ref[j * cap : (j + 1) * cap, :]

        return call(
            kernel,
            (),
            (keep, received),
            [whole((sb, width))] * 2,
            [jax.ShapeDtypeStruct((2 * cap, width), BF16)] * n_dst,
            [whole((2 * cap, width))] * n_dst,
            (1,),
            [],
            0,
            4 * sb * width * 2,
        )

    def refine_call(level, x, mine, theirs, refined, sums):
        first, last = x == 0, x == groups - 1

        def kernel(m, dst_ref, w1_ref, w2_ref, mine_ref, *refs):
            their_refs, refs = refs[:n_dst], refs[n_dst:]
            if not first:
                sums_ref, refs = refs[1], refs[2:]
            out_ref, sum_refs, arrived, total = refs[0], refs[1:-2], refs[-2], refs[-1]
            i = pl.program_id(0)
            core = (here(m, x, i) ^ m[0]) & 1

            @pl.when(i == 0)
            def _():
                for j in range(n_dst):
                    arrived[2 * j * cap : 2 * (j + 1) * cap, :] = their_refs[j][...]
                total[...] = jnp.zeros_like(total) if first else sums_ref[...]

            symmetric = []
            for h in chunks:
                theirs_h = []
                for j in range(h * per, (h + 1) * per):
                    start = pl.multiple_of(((j ^ m[1]) * 2 + core) * cap, cap)
                    theirs_h.append(arrived[pl.ds(start, cap), :])
                theirs_h = jnp.concatenate(theirs_h, axis=0)
                mine_h = mine_ref[h * chunk : (h + 1) * chunk, :]
                symmetric.append((mine_h.astype(F32) + theirs_h.astype(F32)).astype(BF16))
            inner = [silu(dot(v, w1_ref[...])).astype(BF16) for v in symmetric]
            for h in chunks:
                out = (symmetric[h].astype(F32) + dot(inner[h], w2_ref[...])).astype(BF16)
                out_ref[h * chunk : (h + 1) * chunk, :] = out
            atoms = lax.broadcasted_iota(jnp.int32, (dst_rows, sb), 0)
            onehot = jnp.where(atoms == dst_ref[...], 1.0, 0.0).astype(BF16)
            total[...] += dot(onehot, out_ref[...])

            @pl.when(i == 1)
            def _():
                if last:
                    for k in range(n_src):
                        start = pl.multiple_of((m[0] ^ k) * ATOM_DEV, ATOM_DEV)
                        sum_refs[k][...] = total[pl.ds(start, ATOM_DEV), :].astype(BF16)
                else:
                    sum_refs[0][...] = total[...]

        args = (dst_row, edge_w, edge_w, mine, *theirs)
        in_specs = [
            pl.BlockSpec((None, 1, sb), lambda i, m: (here(m, x, i), 0, 0)),
            layer(level, 1, width),
            layer(level, 2, width),
            pl.BlockSpec((sb, width), lambda i, m: (here(m, x, i) & 1, 0)),
        ] + [whole((2 * cap, width))] * n_dst
        aliases = {}
        if not first:
            aliases = {1 + len(args): 0}
            args = (*args, refined, sums)
            in_specs = in_specs + [pl.BlockSpec(memory_space=pl.ANY), whole((dst_rows, width))]
        if last:
            sum_shape = [jax.ShapeDtypeStruct((ATOM_DEV, width), BF16)] * n_src
            sum_specs = [whole((ATOM_DEV, width))] * n_src
        else:
            sum_shape = [jax.ShapeDtypeStruct((dst_rows, width), F32)]
            sum_specs = [whole((dst_rows, width))]
        out = call(
            kernel,
            (meta,),
            args,
            in_specs,
            [jax.ShapeDtypeStruct((rows, width), BF16)] + sum_shape,
            [pl.BlockSpec((sb, width), lambda i, m: (here(m, x, i), 0))] + sum_specs,
            (2,),
            [pltpu.VMEM((2 * sb, width), BF16), pltpu.VMEM((dst_rows, width), F32)],
            4 * sb * width * (2 * width + dst_rows),
            6 * 2**20,
            aliases,
        )
        return out[0], (out[1:] if last else out[1])

    def update_call(level, state, refined, region):
        last = level == NBLK - 1

        def kernel(
            cnt_ref, src_ref, state_ref, refined_ref, w3_ref, w4_ref, w5_ref, down_ref,
            region_ref, out_ref, *low_refs
        ):
            atom = src_ref[...]
            where = (atom % dst_rows) // ATOM_DEV * ratio + atom // dst_rows
            where = where * ATOM_DEV + atom % ATOM_DEV
            lines = lax.broadcasted_iota(jnp.int32, (region_rows, sb), 0)
            pick = jnp.where(lines == where, 1.0, 0.0).astype(BF16)
            feed = split(dot_first(pick, region_ref[...]))
            refined_v = [v.astype(F32) for v in split(refined_ref[...])]
            joined = [(a + b).astype(BF16) for a, b in zip(refined_v, feed)]
            one = [silu(dot(v, w3_ref[...])).astype(BF16) for v in joined]
            two = [silu(dot(v, w4_ref[...])).astype(BF16) for v in one]
            low = []
            for h in chunks:
                at = slice(h * chunk, (h + 1) * chunk)
                counts_h = counts_at(cnt_ref, pl.program_id(0), h)
                new = state_ref[at, :].astype(F32) + refined_v[h] + dot(two[h], w5_ref[...])
                new = masked(new * (0.5**0.5), cap, counts_h).astype(BF16)
                out_ref[at, :] = new
                if not last:
                    low.append(masked(silu(dot_last(new, down_ref[...])), cap, counts_h))
            if not last:
                low_refs[0][...] = pack(jnp.concatenate(low, axis=0).astype(BF16))

        out_shape = [jax.ShapeDtypeStruct((rows, width), BF16)]
        out_specs = [step((sb, width))]
        if not last:
            out_shape.append(jax.ShapeDtypeStruct((prows, 2 * trip), BF16))
            out_specs.append(step((half, 2 * trip)))
        return call(
            kernel,
            (cnt,),
            (src_row, state, refined, edge_w, edge_w, edge_w, down_t, region),
            [
                step((None, 1, sb)),
                step((sb, width)),
                step((sb, width)),
                layer(level, 3, width),
                layer(level, 4, width),
                layer(level, 5, width),
                pl.BlockSpec(
                    (None, trip, width), lambda i, *m: (min(level + 1, NBLK - 1), 0, 0)
                ),
                whole((region_rows, width)),
            ],
            out_shape,
            out_specs,
            (n_src,),
            [],
            2 * rows * width * (3 * width + region_rows + trip),
            8 * 2**20,
        )

    def chip_order():
        return list(range(n_dst // 2, n_dst)) + list(range(n_dst // 2 - 1, -1, -1))

    state = edge_state
    for level in range(NBLK):
        pool = gather_src(lowered)
        mine, theirs = [], []
        for x in range(groups):
            own, give, keep = message_call(level, x, state, pool)
            received = lax.ppermute(give, "src", src_perm(1))
            joined = join_call(keep, received)
            arrived = [None] * n_dst
            for j in chip_order():
                if x == 0 and j == 0:
                    arrived[j] = joined[j]
                    continue
                offset = 2 * x * n_dst + j
                arrived[j] = lax.ppermute(joined[j], both, [(a, a ^ offset) for a in range(n)])
            mine.append(own)
            theirs.append(arrived)
        refined, sums = None, None
        for x in range(groups):
            refined, sums = refine_call(level, x, mine[x], theirs[x], refined, sums)
        parts = []
        for i in range(n_src):
            perm = []
            for a in range(n):
                sa, ua, ja = a // n_dst, (a % n_dst) // ratio, a % ratio
                perm.append((a, ua * n_dst + (sa ^ i) * ratio + ja))
            parts.append(lax.ppermute(sums[i], both, perm))
        total = functools.reduce(lambda a, b: a + b, [p.astype(F32) for p in parts])
        piece = (total * DEGREE ** (-0.5)).astype(BF16)
        region = lax.all_to_all(
            jnp.broadcast_to(piece[None], (n_dst, ATOM_DEV, width)),
            "dst",
            split_axis=0,
            concat_axis=0,
            tiled=True,
        )
        out = update_call(level, state, refined, region.reshape(region_rows, width))
        state = out[0]
        if level < NBLK - 1:
            lowered = out[1]
    return state


def solution(mesh):
    placed = (
        P(("src", "dst"), None),
        P(None, ("src", "dst")),
        P(("src", "dst")),
        P(("src", "dst")),
        P(("src", "dst")),
        P(("src", "dst"), None),
        P(("src", "dst"), None),
        P(),
        P(),
        P(),
    )
    return jax.shard_map(
        body, mesh=mesh, in_specs=placed, out_specs=P(("src", "dst"), None), check_vma=False
    )
```

```python
import functools

import jax
import jax.numpy as jnp
from jax import lax
from jax.experimental import pallas as pl
from jax.experimental.pallas import tpu as pltpu
from jax.sharding import PartitionSpec as P

BLK = 128
PAIRS = 4
NBLK = 2
NSPH = 4
ATOM_DEV = 32
DEGREE = 64
VMEM_LIMIT = 28 * 1024 * 1024

F32 = jnp.float32
BF16 = jnp.bfloat16


def silu(value):
    half = 0.5 * value
    return half + half * jnp.tanh(half)


def dot(a, b):
    return jnp.dot(a, b, preferred_element_type=F32)


def dot_last(a, b):
    return lax.dot_general(a, b, (((1,), (1,)), ((), ())), preferred_element_type=F32)


def dot_first(a, b):
    return lax.dot_general(a, b, (((0,), (0,)), ((), ())), preferred_element_type=F32)


def legendre(cosine):
    square = cosine * cosine
    return [
        cosine,
        1.5 * square - 0.5,
        (2.5 * square - 1.5) * cosine,
        (35.0 * square * square - 30.0 * square + 3.0) * 0.125,
    ]


def masked(value, cap, counts):
    position = lax.broadcasted_iota(jnp.int32, (cap, value.shape[1]), 0)
    parts = [
        jnp.where(position < count, value[i * cap : (i + 1) * cap], 0.0)
        for i, count in enumerate(counts)
    ]
    return jnp.concatenate(parts, axis=0)


def pack(low):
    half = low.shape[0] // 2
    return jnp.concatenate([low[:half], low[half:]], axis=1)


def call(
    kernel, meta, args, in_specs, out_shape, out_specs, grid, scratch, flops, nbytes,
    aliases=None, limit=VMEM_LIMIT,
):
    return pl.pallas_call(
        kernel,
        grid_spec=pltpu.PrefetchScalarGridSpec(
            num_scalar_prefetch=len(meta),
            grid=grid,
            in_specs=in_specs,
            out_specs=out_specs,
            scratch_shapes=scratch,
        ),
        out_shape=out_shape,
        input_output_aliases=aliases or {},
        compiler_params=pltpu.CompilerParams(vmem_limit_bytes=limit),
        cost_estimate=pl.CostEstimate(flops=flops, bytes_accessed=nbytes, transcendentals=0),
    )(*meta, *args)


def whole(shape):
    return pl.BlockSpec(shape, lambda i, *m: (0,) * len(shape))


def step(shape):
    return pl.BlockSpec(shape, lambda i, *m: (i,) + (0,) * (len(shape) - 1))


def layer(level, index, width):
    return pl.BlockSpec((None, None, width, width), lambda i, *m: (level, index, 0, 0))


def body(
    edge_state, directions, src_atom, dst_atom, rev_pos, counts, triplets, down_w, trip_w, edge_w
):
    n_src = lax.axis_size("src")
    n_dst = lax.axis_size("dst")
    n = n_src * n_dst
    rows, width = edge_state.shape
    trip = down_w.shape[2]
    cap = rows // n
    sb = rows // n_src
    spb = sb // BLK
    half = sb // 2
    chunk = min(sb, 256)
    groups = n_src // 2
    nblock = rows // BLK
    ratio = n_dst // n_src
    dst_rows = ATOM_DEV * n_src
    region_rows = ratio * dst_rows
    prows = rows // 2
    both = ("src", "dst")
    chunks = range(sb // chunk)
    per = chunk // cap

    s = lax.axis_index("src")
    d = lax.axis_index("dst")

    cnt = counts.reshape(-1)
    flat = triplets.T.reshape(-1)
    block = flat % nblock
    pool_row = ((flat // nblock) ^ s) * prows + block // spb * half + block % (spb // 2) * BLK
    pool_half = (block % spb) // (spb // 2)
    meta = jnp.concatenate([jnp.stack([s, d]), pool_row, pool_half, flat * BLK]).astype(jnp.int32)
    at_row = 2
    at_half = at_row + nblock * PAIRS
    at_lane = at_half + nblock * PAIRS
    down_t = jnp.swapaxes(down_w, 1, 2)

    def counts_at(cnt_ref, block, h=None):
        first = block * n_dst + (0 if h is None else h * per)
        return [cnt_ref[first + i] for i in range(n_dst if h is None else per)]

    def split(value):
        return [value[h * chunk : (h + 1) * chunk] for h in chunks]

    def lower_kernel(cnt_ref, state_ref, down_ref, out_ref):
        low = silu(dot_last(state_ref[...], down_ref[...]))
        low = masked(low, cap, counts_at(cnt_ref, pl.program_id(0)))
        out_ref[...] = pack(low.astype(BF16))

    lowered = call(
        lower_kernel,
        (cnt,),
        (edge_state, down_t),
        [step((sb, width)), pl.BlockSpec((None, trip, width), lambda i, *m: (0, 0, 0))],
        jax.ShapeDtypeStruct((prows, 2 * trip), BF16),
        step((half, 2 * trip)),
        (n_src,),
        [],
        2 * rows * width * trip,
        rows * width * 2,
    )

    def src_perm(i):
        return [(a, a ^ i) for a in range(n_src)]

    def gather_src(x, before=None):
        slots = [None] * n_src
        slots[0] = x
        for i in range(2, n_src, 2):
            slots[i] = lax.ppermute(x, "src", src_perm(i))
        slots[1] = lax.ppermute(x, "src", src_perm(1))
        for i in range(2, n_src, 2):
            if before is not None:
                slots[i], _ = lax.optimization_barrier((slots[i], before))
            slots[i + 1] = lax.ppermute(slots[i], "src", src_perm(1))
        return slots

    own_dirs, _ = lax.optimization_barrier((directions, lowered))
    dirs_pool = lax.all_gather(own_dirs, "src", axis=1, tiled=True)

    def tiles_kernel(m, own_ref, pool_ref, out_ref):
        first = pl.program_id(0) * spb
        own = jnp.concatenate([own_ref[...], jnp.zeros((5, sb), F32)], axis=0)
        col = own.T
        for c in range(spb):
            col_c = col[c * BLK : (c + 1) * BLK]
            for q in range(PAIRS):
                lane = pl.multiple_of(m[at_lane + q * nblock + first + c], BLK)
                chosen = pool_ref[:, pl.ds(lane, BLK)]
                cosine = (
                    col_c[:, 0:1] * chosen[0:1]
                    + col_c[:, 1:2] * chosen[1:2]
                    + col_c[:, 2:3] * chosen[2:3]
                )
                for degree, tile in enumerate(legendre(cosine)):
                    out_ref[c, degree, :, q * BLK : (q + 1) * BLK] = tile.astype(BF16)

    tiles = call(
        tiles_kernel,
        (meta,),
        (directions, dirs_pool),
        [pl.BlockSpec((3, sb), lambda i, *m: (0, i)), whole((3, n_src * rows))],
        jax.ShapeDtypeStruct((nblock, NSPH, BLK, PAIRS * BLK), BF16),
        step((spb, NSPH, BLK, PAIRS * BLK)),
        (n_src,),
        [],
        nblock * BLK * PAIRS * BLK * 2000,
        nblock * NSPH * BLK * PAIRS * BLK * 2,
    )

    rev_row = rev_pos.reshape(n_src, 1, sb)
    dst_row = dst_atom.reshape(n_src, 1, sb)
    src_row = src_atom.reshape(n_src, 1, sb)
    tri_scale = (BLK * PAIRS) ** (-0.5)

    def here(m, x, i):
        return m[0] ^ (2 * x) ^ 1 ^ i

    def message_call(level, x, state, pool):
        def kernel(cnt_ref, m, tiles_ref, state_ref, w_ref, up_ref, rev_ref, *refs):
            pool_refs, refs = refs[:n_src], refs[n_src:]
            mine_ref, give_ref, keep_ref, pool_all, hold = refs
            i = pl.program_id(0)
            at_block = here(m, x, i)

            @pl.when(i == 0)
            def _():
                for k in range(n_src):
                    pool_all[k * prows : (k + 1) * prows, :] = pool_refs[k][...]

            blocks = []
            for c in range(spb):
                chosen = []
                for q in range(PAIRS):
                    which = q * nblock + at_block * spb + c
                    v = pool_all[pl.ds(pl.multiple_of(m[at_row + which], BLK), BLK), :]
                    chosen.append(jnp.where(m[at_half + which] == 1, v[:, trip:], v[:, :trip]))
                summed = dot(
                    tiles_ref[c].reshape(NSPH * BLK, PAIRS * BLK), jnp.concatenate(chosen, axis=0)
                )
                summed = (summed * tri_scale).astype(BF16)
                blocks.append(
                    jnp.concatenate(
                        [summed[l * BLK : (l + 1) * BLK] for l in range(NSPH)], axis=1
                    )
                )
            triple = jnp.concatenate(blocks, axis=0)
            target_row = lax.broadcasted_iota(jnp.int32, (chunk, chunk), 0)
            base = lax.broadcasted_iota(jnp.int32, (1, chunk), 1) // cap * cap
            pre = [
                dot(v, w_ref[...]) + dot(t, up_ref[...])
                for v, t in zip(split(state_ref[...]), split(triple))
            ]
            for h in chunks:
                message = masked(silu(pre[h]), cap, counts_at(cnt_ref, at_block, h)).astype(BF16)
                at = slice(h * chunk, (h + 1) * chunk)
                mine_ref[at, :] = message
                pick = jnp.where(target_row == rev_ref[:, at] + base, 1.0, 0.0).astype(BF16)
                hold[at, :] = dot(pick, message).astype(BF16)
            for out_ref, when in ((give_ref, 0), (keep_ref, 1)):

                @pl.when(i == when)
                def _(out_ref=out_ref):
                    for j in range(n_dst):
                        start = pl.multiple_of((m[1] ^ j) * cap, cap)
                        out_ref[j * cap : (j + 1) * cap, :] = hold[pl.ds(start, cap), :]

        return call(
            kernel,
            (cnt, meta),
            (tiles, state, edge_w, trip_w, rev_row, *pool),
            [
                pl.BlockSpec(
                    (spb, NSPH, BLK, PAIRS * BLK), lambda i, c, m: (here(m, x, i), 0, 0, 0)
                ),
                pl.BlockSpec((sb, width), lambda i, c, m: (here(m, x, i), 0)),
                layer(level, 0, width),
                pl.BlockSpec((None, NSPH * trip, width), lambda i, *m: (level, 0, 0)),
                pl.BlockSpec((None, 1, sb), lambda i, c, m: (here(m, x, i), 0, 0)),
            ]
            + [whole((prows, 2 * trip))] * n_src,
            [jax.ShapeDtypeStruct((2 * sb, width), BF16)]
            + [jax.ShapeDtypeStruct((sb, width), BF16)] * 2,
            [pl.BlockSpec((sb, width), lambda i, c, m: (here(m, x, i) & 1, 0))]
            + [whole((sb, width))] * 2,
            (2,),
            [pltpu.VMEM((n_src * prows, 2 * trip), BF16), pltpu.VMEM((sb, width), BF16)],
            4 * sb * width * (width + 2 * NSPH * trip) + 4 * sb * NSPH * 512 * 256,
            9 * 2**20,
        )

    def join_call(keep, received):
        def kernel(keep_ref, received_ref, *out_refs):
            for j, out_ref in enumerate(out_refs):
                out_ref[:cap, :] = keep_ref[j * cap : (j + 1) * cap, :]
                out_ref[cap:, :] = received_ref[j * cap : (j + 1) * cap, :]

        return call(
            kernel,
            (),
            (keep, received),
            [whole((sb, width))] * 2,
            [jax.ShapeDtypeStruct((2 * cap, width), BF16)] * n_dst,
            [whole((2 * cap, width))] * n_dst,
            (1,),
            [],
            0,
            4 * sb * width * 2,
        )

    def refine_call(level, x, mine, theirs, refined, sums):
        first, last = x == 0, x == groups - 1

        def kernel(m, dst_ref, w1_ref, w2_ref, mine_ref, *refs):
            their_refs, refs = refs[:n_dst], refs[n_dst:]
            if not first:
                sums_ref, refs = refs[1], refs[2:]
            out_ref, sum_refs, arrived, total = refs[0], refs[1:-2], refs[-2], refs[-1]
            i = pl.program_id(0)
            core = (here(m, x, i) ^ m[0]) & 1

            @pl.when(i == 0)
            def _():
                for j in range(n_dst):
                    arrived[2 * j * cap : 2 * (j + 1) * cap, :] = their_refs[j][...]
                total[...] = jnp.zeros_like(total) if first else sums_ref[...]

            symmetric = []
            for h in chunks:
                theirs_h = []
                for j in range(h * per, (h + 1) * per):
                    start = pl.multiple_of(((j ^ m[1]) * 2 + core) * cap, cap)
                    theirs_h.append(arrived[pl.ds(start, cap), :])
                theirs_h = jnp.concatenate(theirs_h, axis=0)
                mine_h = mine_ref[h * chunk : (h + 1) * chunk, :]
                symmetric.append((mine_h.astype(F32) + theirs_h.astype(F32)).astype(BF16))
            inner = [silu(dot(v, w1_ref[...])).astype(BF16) for v in symmetric]
            for h in chunks:
                out = (symmetric[h].astype(F32) + dot(inner[h], w2_ref[...])).astype(BF16)
                out_ref[h * chunk : (h + 1) * chunk, :] = out
            atoms = lax.broadcasted_iota(jnp.int32, (dst_rows, sb), 0)
            onehot = jnp.where(atoms == dst_ref[...], 1.0, 0.0).astype(BF16)
            total[...] += dot(onehot, out_ref[...])

            @pl.when(i == 1)
            def _():
                if last:
                    for k in range(n_src):
                        start = pl.multiple_of((m[0] ^ k) * ATOM_DEV, ATOM_DEV)
                        sum_refs[k][...] = total[pl.ds(start, ATOM_DEV), :].astype(BF16)
                else:
                    sum_refs[0][...] = total[...]

        args = (dst_row, edge_w, edge_w, mine, *theirs)
        in_specs = [
            pl.BlockSpec((None, 1, sb), lambda i, m: (here(m, x, i), 0, 0)),
            layer(level, 1, width),
            layer(level, 2, width),
            pl.BlockSpec((sb, width), lambda i, m: (here(m, x, i) & 1, 0)),
        ] + [whole((2 * cap, width))] * n_dst
        aliases = {}
        if not first:
            aliases = {1 + len(args): 0}
            args = (*args, refined, sums)
            in_specs = in_specs + [pl.BlockSpec(memory_space=pl.ANY), whole((dst_rows, width))]
        if last:
            sum_shape = [jax.ShapeDtypeStruct((ATOM_DEV, width), BF16)] * n_src
            sum_specs = [whole((ATOM_DEV, width))] * n_src
        else:
            sum_shape = [jax.ShapeDtypeStruct((dst_rows, width), F32)]
            sum_specs = [whole((dst_rows, width))]
        out = call(
            kernel,
            (meta,),
            args,
            in_specs,
            [jax.ShapeDtypeStruct((rows, width), BF16)] + sum_shape,
            [pl.BlockSpec((sb, width), lambda i, m: (here(m, x, i), 0))] + sum_specs,
            (2,),
            [pltpu.VMEM((2 * sb, width), BF16), pltpu.VMEM((dst_rows, width), F32)],
            4 * sb * width * (2 * width + dst_rows),
            6 * 2**20,
            aliases,
        )
        return out[0], (out[1:] if last else out[1])

    def update_call(level, state, refined, region):
        last = level == NBLK - 1

        def kernel(
            cnt_ref, m, src_ref, state_ref, refined_ref, w3_ref, w4_ref, w5_ref, down_ref, *refs
        ):
            region_refs, out_ref = refs[: n_dst // 2], refs[n_dst // 2]
            low_refs, region = refs[n_dst // 2 + 1 : -1], refs[-1]

            @pl.when(pl.program_id(0) == 0)
            def _():
                for k, region_ref in enumerate(region_refs):
                    region[k * 2 * ATOM_DEV : (k + 1) * 2 * ATOM_DEV, :] = region_ref[...]

            atom = src_ref[...]
            where = (atom % dst_rows) // ATOM_DEV * ratio + atom // dst_rows
            where = (where ^ m[1]) * ATOM_DEV + atom % ATOM_DEV
            lines = lax.broadcasted_iota(jnp.int32, (region_rows, sb), 0)
            pick = jnp.where(lines == where, 1.0, 0.0).astype(BF16)
            feed = split(dot_first(pick, region[...]))
            refined_v = [v.astype(F32) for v in split(refined_ref[...])]
            joined = [(a + b).astype(BF16) for a, b in zip(refined_v, feed)]
            one = [silu(dot(v, w3_ref[...])).astype(BF16) for v in joined]
            two = [silu(dot(v, w4_ref[...])).astype(BF16) for v in one]
            low = []
            for h in chunks:
                at = slice(h * chunk, (h + 1) * chunk)
                counts_h = counts_at(cnt_ref, pl.program_id(0), h)
                new = state_ref[at, :].astype(F32) + refined_v[h] + dot(two[h], w5_ref[...])
                new = masked(new * (0.5**0.5), cap, counts_h).astype(BF16)
                out_ref[at, :] = new
                if not last:
                    low.append(masked(silu(dot_last(new, down_ref[...])), cap, counts_h))
            if not last:
                low_refs[0][...] = pack(jnp.concatenate(low, axis=0).astype(BF16))

        out_shape = [jax.ShapeDtypeStruct((rows, width), BF16)]
        out_specs = [step((sb, width))]
        if not last:
            out_shape.append(jax.ShapeDtypeStruct((prows, 2 * trip), BF16))
            out_specs.append(step((half, 2 * trip)))
        return call(
            kernel,
            (cnt, meta),
            (src_row, state, refined, edge_w, edge_w, edge_w, down_t, *region),
            [
                step((None, 1, sb)),
                step((sb, width)),
                step((sb, width)),
                layer(level, 3, width),
                layer(level, 4, width),
                layer(level, 5, width),
                pl.BlockSpec(
                    (None, trip, width), lambda i, *m: (min(level + 1, NBLK - 1), 0, 0)
                ),
            ]
            + [whole((2 * ATOM_DEV, width))] * (n_dst // 2),
            out_shape,
            out_specs,
            (n_src,),
            [pltpu.VMEM((region_rows, width), BF16)],
            2 * rows * width * (3 * width + region_rows + trip),
            8 * 2**20,
        )

    def chip_order():
        mid = n_dst // 2
        return [j for pair in zip(range(mid, n_dst), range(mid - 1, -1, -1)) for j in pair]

    state = edge_state
    for level in range(NBLK):
        pool = gather_src(lowered, dirs_pool if level == 0 else None)
        mine, theirs = [], []
        for x in range(groups):
            own, give, keep = message_call(level, x, state, pool)
            received = lax.ppermute(give, "src", src_perm(1))
            joined = join_call(keep, received)
            arrived = [None] * n_dst
            for j in chip_order():
                if x == 0 and j == 0:
                    arrived[j] = joined[j]
                    continue
                offset = 2 * x * n_dst + j
                arrived[j] = lax.ppermute(joined[j], both, [(a, a ^ offset) for a in range(n)])
            mine.append(own)
            theirs.append(arrived)
        refined, sums = None, None
        for x in range(groups):
            refined, sums = refine_call(level, x, mine[x], theirs[x], refined, sums)
        parts = []
        for i in range(n_src):
            perm = []
            for a in range(n):
                sa, ua, ja = a // n_dst, (a % n_dst) // ratio, a % ratio
                perm.append((a, ua * n_dst + (sa ^ i) * ratio + ja))
            parts.append(lax.ppermute(sums[i], both, perm))
        total = functools.reduce(lambda a, b: a + b, [p.astype(F32) for p in parts])
        piece = (total * DEGREE ** (-0.5)).astype(BF16)
        beside = lax.ppermute(piece, "dst", [(a, a ^ 1) for a in range(n_dst)])
        pair = jnp.concatenate([piece, beside], axis=0)
        region = [pair] + [
            lax.ppermute(pair, "dst", [(a, a ^ i) for a in range(n_dst)])
            for i in range(2, n_dst, 2)
        ]
        out = update_call(level, state, refined, region)
        state = out[0]
        if level < NBLK - 1:
            lowered = out[1]
    return state


def solution(mesh):
    placed = (
        P(("src", "dst"), None),
        P(None, ("src", "dst")),
        P(("src", "dst")),
        P(("src", "dst")),
        P(("src", "dst")),
        P(("src", "dst"), None),
        P(("src", "dst"), None),
        P(),
        P(),
        P(),
    )
    return jax.shard_map(
        body, mesh=mesh, in_specs=placed, out_specs=P(("src", "dst"), None), check_vma=False
    )
```

```python
import functools

import jax
import jax.numpy as jnp
from jax import lax
from jax.experimental import pallas as pl
from jax.experimental.pallas import tpu as pltpu
from jax.sharding import PartitionSpec as P

BLK = 128
PAIRS = 4
NBLK = 2
NSPH = 4
ATOM_DEV = 32
DEGREE = 64
VMEM_LIMIT = 28 * 1024 * 1024

F32 = jnp.float32
BF16 = jnp.bfloat16


def silu(value):
    half = 0.5 * value
    return half + half * jnp.tanh(half)


def dot(a, b):
    return jnp.dot(a, b, preferred_element_type=F32)


def dot_last(a, b):
    return lax.dot_general(a, b, (((1,), (1,)), ((), ())), preferred_element_type=F32)


def dot_first(a, b):
    return lax.dot_general(a, b, (((0,), (0,)), ((), ())), preferred_element_type=F32)


def legendre(cosine):
    square = cosine * cosine
    return [
        cosine,
        1.5 * square - 0.5,
        (2.5 * square - 1.5) * cosine,
        (35.0 * square * square - 30.0 * square + 3.0) * 0.125,
    ]


def masked(value, cap, counts):
    position = lax.broadcasted_iota(jnp.int32, (cap, value.shape[1]), 0)
    parts = [
        jnp.where(position < count, value[i * cap : (i + 1) * cap], 0.0)
        for i, count in enumerate(counts)
    ]
    return jnp.concatenate(parts, axis=0)


def pack(low):
    half = low.shape[0] // 2
    return jnp.concatenate([low[:half], low[half:]], axis=1)


def call(
    kernel, meta, args, in_specs, out_shape, out_specs, grid, scratch, flops, nbytes,
    aliases=None, limit=VMEM_LIMIT,
):
    return pl.pallas_call(
        kernel,
        grid_spec=pltpu.PrefetchScalarGridSpec(
            num_scalar_prefetch=len(meta),
            grid=grid,
            in_specs=in_specs,
            out_specs=out_specs,
            scratch_shapes=scratch,
        ),
        out_shape=out_shape,
        input_output_aliases=aliases or {},
        compiler_params=pltpu.CompilerParams(vmem_limit_bytes=limit),
        cost_estimate=pl.CostEstimate(flops=flops, bytes_accessed=nbytes, transcendentals=0),
    )(*meta, *args)


def whole(shape):
    return pl.BlockSpec(shape, lambda i, *m: (0,) * len(shape))


def step(shape):
    return pl.BlockSpec(shape, lambda i, *m: (i,) + (0,) * (len(shape) - 1))


def layer(level, index, width):
    return pl.BlockSpec((None, None, width, width), lambda i, *m: (level, index, 0, 0))


def body(
    edge_state, directions, src_atom, dst_atom, rev_pos, counts, triplets, down_w, trip_w, edge_w
):
    n_src = lax.axis_size("src")
    n_dst = lax.axis_size("dst")
    n = n_src * n_dst
    rows, width = edge_state.shape
    trip = down_w.shape[2]
    cap = rows // n
    sb = rows // n_src
    spb = sb // BLK
    half = sb // 2
    chunk = min(sb, 256)
    groups = n_src // 2
    nblock = rows // BLK
    ratio = n_dst // n_src
    dst_rows = ATOM_DEV * n_src
    region_rows = ratio * dst_rows
    prows = rows // 2
    both = ("src", "dst")
    chunks = range(sb // chunk)
    per = chunk // cap

    s = lax.axis_index("src")
    d = lax.axis_index("dst")

    cnt = counts.reshape(-1)
    flat = triplets.T.reshape(-1)
    block = flat % nblock
    pool_row = ((flat // nblock) ^ s) * prows + block // spb * half + block % (spb // 2) * BLK
    pool_half = (block % spb) // (spb // 2)
    meta = jnp.concatenate([jnp.stack([s, d]), pool_row, pool_half, flat * BLK]).astype(jnp.int32)
    at_row = 2
    at_half = at_row + nblock * PAIRS
    at_lane = at_half + nblock * PAIRS
    down_t = jnp.swapaxes(down_w, 1, 2)

    def counts_at(cnt_ref, block, h=None):
        first = block * n_dst + (0 if h is None else h * per)
        return [cnt_ref[first + i] for i in range(n_dst if h is None else per)]

    def split(value):
        return [value[h * chunk : (h + 1) * chunk] for h in chunks]

    def lower_kernel(cnt_ref, state_ref, down_ref, out_ref):
        low = silu(dot_last(state_ref[...], down_ref[...]))
        low = masked(low, cap, counts_at(cnt_ref, pl.program_id(0)))
        out_ref[...] = pack(low.astype(BF16))

    lowered = call(
        lower_kernel,
        (cnt,),
        (edge_state, down_t),
        [step((sb, width)), pl.BlockSpec((None, trip, width), lambda i, *m: (0, 0, 0))],
        jax.ShapeDtypeStruct((prows, 2 * trip), BF16),
        step((half, 2 * trip)),
        (n_src,),
        [],
        2 * rows * width * trip,
        rows * width * 2,
    )

    def src_perm(i):
        return [(a, a ^ i) for a in range(n_src)]

    def gather_src(x, before=None):
        slots = [None] * n_src
        slots[0] = x
        for i in range(2, n_src, 2):
            slots[i] = lax.ppermute(x, "src", src_perm(i))
        slots[1] = lax.ppermute(x, "src", src_perm(1))
        for i in range(2, n_src, 2):
            if before is not None:
                slots[i], _ = lax.optimization_barrier((slots[i], before))
            slots[i + 1] = lax.ppermute(slots[i], "src", src_perm(1))
        return slots

    own_dirs, _ = lax.optimization_barrier((directions, lowered))
    dirs_pool = lax.all_gather(own_dirs, "src", axis=1, tiled=True)

    def tiles_kernel(m, own_ref, pool_ref, out_ref):
        first = pl.program_id(0) * spb
        own = jnp.concatenate([own_ref[...], jnp.zeros((5, sb), F32)], axis=0)
        col = own.T
        for c in range(spb):
            col_c = col[c * BLK : (c + 1) * BLK]
            for q in range(PAIRS):
                lane = pl.multiple_of(m[at_lane + q * nblock + first + c], BLK)
                chosen = pool_ref[:, pl.ds(lane, BLK)]
                cosine = (
                    col_c[:, 0:1] * chosen[0:1]
                    + col_c[:, 1:2] * chosen[1:2]
                    + col_c[:, 2:3] * chosen[2:3]
                )
                for degree, tile in enumerate(legendre(cosine)):
                    out_ref[c, degree, :, q * BLK : (q + 1) * BLK] = tile.astype(BF16)

    tiles = call(
        tiles_kernel,
        (meta,),
        (directions, dirs_pool),
        [pl.BlockSpec((3, sb), lambda i, *m: (0, i)), whole((3, n_src * rows))],
        jax.ShapeDtypeStruct((nblock, NSPH, BLK, PAIRS * BLK), BF16),
        step((spb, NSPH, BLK, PAIRS * BLK)),
        (n_src,),
        [],
        nblock * BLK * PAIRS * BLK * 2000,
        nblock * NSPH * BLK * PAIRS * BLK * 2,
    )

    rev_row = rev_pos.reshape(n_src, 1, sb)
    dst_row = dst_atom.reshape(n_src, 1, sb)
    src_row = src_atom.reshape(n_src, 1, sb)
    tri_scale = (BLK * PAIRS) ** (-0.5)

    def here(m, x, i):
        return m[0] ^ (2 * x) ^ 1 ^ i

    def message_call(level, x, state, pool):
        def kernel(cnt_ref, m, tiles_ref, state_ref, w_ref, up_ref, rev_ref, *refs):
            pool_refs, refs = refs[:n_src], refs[n_src:]
            mine_ref, give_ref, keep_ref, pool_all, hold = refs
            i = pl.program_id(0)
            at_block = here(m, x, i)

            @pl.when(i == 0)
            def _():
                for k in range(n_src):
                    pool_all[k * prows : (k + 1) * prows, :] = pool_refs[k][...]

            blocks = []
            for c in range(spb):
                chosen = []
                for q in range(PAIRS):
                    which = q * nblock + at_block * spb + c
                    v = pool_all[pl.ds(pl.multiple_of(m[at_row + which], BLK), BLK), :]
                    chosen.append(jnp.where(m[at_half + which] == 1, v[:, trip:], v[:, :trip]))
                summed = dot(
                    tiles_ref[c].reshape(NSPH * BLK, PAIRS * BLK), jnp.concatenate(chosen, axis=0)
                )
                summed = (summed * tri_scale).astype(BF16)
                blocks.append(
                    jnp.concatenate(
                        [summed[l * BLK : (l + 1) * BLK] for l in range(NSPH)], axis=1
                    )
                )
            triple = jnp.concatenate(blocks, axis=0)
            target_row = lax.broadcasted_iota(jnp.int32, (chunk, chunk), 0)
            base = lax.broadcasted_iota(jnp.int32, (1, chunk), 1) // cap * cap
            pre = [
                dot(v, w_ref[...]) + dot(t, up_ref[...])
                for v, t in zip(split(state_ref[...]), split(triple))
            ]
            for h in chunks:
                message = masked(silu(pre[h]), cap, counts_at(cnt_ref, at_block, h)).astype(BF16)
                at = slice(h * chunk, (h + 1) * chunk)
                mine_ref[at, :] = message
                pick = jnp.where(target_row == rev_ref[:, at] + base, 1.0, 0.0).astype(BF16)
                hold[at, :] = dot(pick, message).astype(BF16)
            for out_ref, when in ((give_ref, 0), (keep_ref, 1)):

                @pl.when(i == when)
                def _(out_ref=out_ref):
                    for j in range(n_dst):
                        start = pl.multiple_of((m[1] ^ j) * cap, cap)
                        out_ref[j * cap : (j + 1) * cap, :] = hold[pl.ds(start, cap), :]

        return call(
            kernel,
            (cnt, meta),
            (tiles, state, edge_w, trip_w, rev_row, *pool),
            [
                pl.BlockSpec(
                    (spb, NSPH, BLK, PAIRS * BLK), lambda i, c, m: (here(m, x, i), 0, 0, 0)
                ),
                pl.BlockSpec((sb, width), lambda i, c, m: (here(m, x, i), 0)),
                layer(level, 0, width),
                pl.BlockSpec((None, NSPH * trip, width), lambda i, *m: (level, 0, 0)),
                pl.BlockSpec((None, 1, sb), lambda i, c, m: (here(m, x, i), 0, 0)),
            ]
            + [whole((prows, 2 * trip))] * n_src,
            [jax.ShapeDtypeStruct((2 * sb, width), BF16)]
            + [jax.ShapeDtypeStruct((sb, width), BF16)] * 2,
            [pl.BlockSpec((sb, width), lambda i, c, m: (here(m, x, i) & 1, 0))]
            + [whole((sb, width))] * 2,
            (2,),
            [pltpu.VMEM((n_src * prows, 2 * trip), BF16), pltpu.VMEM((sb, width), BF16)],
            4 * sb * width * (width + 2 * NSPH * trip) + 4 * sb * NSPH * 512 * 256,
            9 * 2**20,
        )

    def join_call(keep, received):
        def kernel(keep_ref, received_ref, *out_refs):
            for j, out_ref in enumerate(out_refs):
                out_ref[:cap, :] = keep_ref[j * cap : (j + 1) * cap, :]
                out_ref[cap:, :] = received_ref[j * cap : (j + 1) * cap, :]

        return call(
            kernel,
            (),
            (keep, received),
            [whole((sb, width))] * 2,
            [jax.ShapeDtypeStruct((2 * cap, width), BF16)] * n_dst,
            [whole((2 * cap, width))] * n_dst,
            (1,),
            [],
            0,
            4 * sb * width * 2,
        )

    def refine_call(level, x, mine, theirs, refined, sums):
        first, last = x == 0, x == groups - 1

        def kernel(m, dst_ref, w1_ref, w2_ref, mine_ref, *refs):
            their_refs, refs = refs[:n_dst], refs[n_dst:]
            if not first:
                sums_ref, refs = refs[1], refs[2:]
            out_ref, sum_refs, arrived, total = refs[0], refs[1:-2], refs[-2], refs[-1]
            i = pl.program_id(0)
            core = (here(m, x, i) ^ m[0]) & 1

            @pl.when(i == 0)
            def _():
                for j in range(n_dst):
                    arrived[2 * j * cap : 2 * (j + 1) * cap, :] = their_refs[j][...]
                total[...] = jnp.zeros_like(total) if first else sums_ref[...]

            symmetric = []
            for h in chunks:
                theirs_h = []
                for j in range(h * per, (h + 1) * per):
                    start = pl.multiple_of(((j ^ m[1]) * 2 + core) * cap, cap)
                    theirs_h.append(arrived[pl.ds(start, cap), :])
                theirs_h = jnp.concatenate(theirs_h, axis=0)
                mine_h = mine_ref[h * chunk : (h + 1) * chunk, :]
                symmetric.append((mine_h.astype(F32) + theirs_h.astype(F32)).astype(BF16))
            inner = [silu(dot(v, w1_ref[...])).astype(BF16) for v in symmetric]
            for h in chunks:
                out = (symmetric[h].astype(F32) + dot(inner[h], w2_ref[...])).astype(BF16)
                out_ref[h * chunk : (h + 1) * chunk, :] = out
            atoms = lax.broadcasted_iota(jnp.int32, (dst_rows, sb), 0)
            onehot = jnp.where(atoms == dst_ref[...], 1.0, 0.0).astype(BF16)
            total[...] += dot(onehot, out_ref[...])

            @pl.when(i == 1)
            def _():
                if last:
                    for k in range(n_src):
                        start = pl.multiple_of((m[0] ^ k) * ATOM_DEV, ATOM_DEV)
                        piece = total[pl.ds(start, ATOM_DEV), :].astype(BF16)
                        if level == 0:
                            sum_refs[k][...] = piece
                        elif k % 2 == 0:
                            sum_refs[k // 2][...] = piece
                        else:
                            sum_refs[-1][k // 2 * ATOM_DEV : (k // 2 + 1) * ATOM_DEV, :] = piece
                else:
                    sum_refs[0][...] = total[...]

        args = (dst_row, edge_w, edge_w, mine, *theirs)
        in_specs = [
            pl.BlockSpec((None, 1, sb), lambda i, m: (here(m, x, i), 0, 0)),
            layer(level, 1, width),
            layer(level, 2, width),
            pl.BlockSpec((sb, width), lambda i, m: (here(m, x, i) & 1, 0)),
        ] + [whole((2 * cap, width))] * n_dst
        aliases = {}
        if not first:
            aliases = {1 + len(args): 0}
            args = (*args, refined, sums)
            in_specs = in_specs + [pl.BlockSpec(memory_space=pl.ANY), whole((dst_rows, width))]
        if last:
            sizes = [ATOM_DEV] * n_src if level == 0 else [ATOM_DEV] * groups + [ATOM_DEV * groups]
            sum_shape = [jax.ShapeDtypeStruct((size, width), BF16) for size in sizes]
            sum_specs = [whole((size, width)) for size in sizes]
        else:
            sum_shape = [jax.ShapeDtypeStruct((dst_rows, width), F32)]
            sum_specs = [whole((dst_rows, width))]
        out = call(
            kernel,
            (meta,),
            args,
            in_specs,
            [jax.ShapeDtypeStruct((rows, width), BF16)] + sum_shape,
            [pl.BlockSpec((sb, width), lambda i, m: (here(m, x, i), 0))] + sum_specs,
            (2,),
            [pltpu.VMEM((2 * sb, width), BF16), pltpu.VMEM((dst_rows, width), F32)],
            4 * sb * width * (2 * width + dst_rows),
            6 * 2**20,
            aliases,
        )
        return out[0], (out[1:] if last else out[1])

    def update_call(level, state, refined, pieces):
        last = level == NBLK - 1
        size = pieces[0].shape[0]

        def kernel(
            cnt_ref, m, src_ref, state_ref, refined_ref, w3_ref, w4_ref, w5_ref, down_ref, *refs
        ):
            region_refs, out_ref = refs[: len(pieces)], refs[len(pieces)]
            low_refs, region = refs[len(pieces) + 1 : -1], refs[-1]

            @pl.when(pl.program_id(0) == 0)
            def _():
                for k, region_ref in enumerate(region_refs):
                    region[k * size : (k + 1) * size, :] = region_ref[...]

            atom = src_ref[...]
            where = (atom % dst_rows) // ATOM_DEV * ratio + atom // dst_rows
            if len(pieces) > 1:
                where = where ^ m[1]
            where = where * ATOM_DEV + atom % ATOM_DEV
            lines = lax.broadcasted_iota(jnp.int32, (region_rows, sb), 0)
            pick = jnp.where(lines == where, 1.0, 0.0).astype(BF16)
            feed = split(dot_first(pick, region[...]))
            refined_v = [v.astype(F32) for v in split(refined_ref[...])]
            joined = [(a + b).astype(BF16) for a, b in zip(refined_v, feed)]
            one = [silu(dot(v, w3_ref[...])).astype(BF16) for v in joined]
            two = [silu(dot(v, w4_ref[...])).astype(BF16) for v in one]
            low = []
            for h in chunks:
                at = slice(h * chunk, (h + 1) * chunk)
                counts_h = counts_at(cnt_ref, pl.program_id(0), h)
                new = state_ref[at, :].astype(F32) + refined_v[h] + dot(two[h], w5_ref[...])
                new = masked(new * (0.5**0.5), cap, counts_h).astype(BF16)
                out_ref[at, :] = new
                if not last:
                    low.append(masked(silu(dot_last(new, down_ref[...])), cap, counts_h))
            if not last:
                low_refs[0][...] = pack(jnp.concatenate(low, axis=0).astype(BF16))

        out_shape = [jax.ShapeDtypeStruct((rows, width), BF16)]
        out_specs = [step((sb, width))]
        if not last:
            out_shape.append(jax.ShapeDtypeStruct((prows, 2 * trip), BF16))
            out_specs.append(step((half, 2 * trip)))
        return call(
            kernel,
            (cnt, meta),
            (src_row, state, refined, edge_w, edge_w, edge_w, down_t, *pieces),
            [
                step((None, 1, sb)),
                step((sb, width)),
                step((sb, width)),
                layer(level, 3, width),
                layer(level, 4, width),
                layer(level, 5, width),
                pl.BlockSpec(
                    (None, trip, width), lambda i, *m: (min(level + 1, NBLK - 1), 0, 0)
                ),
            ]
            + [whole((size, width))] * len(pieces),
            out_shape,
            out_specs,
            (n_src,),
            [pltpu.VMEM((region_rows, width), BF16)],
            2 * rows * width * (3 * width + region_rows + trip),
            8 * 2**20,
        )

    def exchange(joined, window):
        mid = n_dst // 2
        order = [j for pair in zip(range(mid, n_dst), range(mid - 1, -1, -1)) for j in pair]
        arrived = [[None] * n_dst for _ in range(groups)]
        arrived[0][0] = joined[0][0]
        sent = []
        for x in range(groups):
            for j in order:
                if arrived[x][j] is not None:
                    continue
                operand, offset = joined[x][j], 2 * x * n_dst + j
                if len(sent) >= window:
                    operand, _ = lax.optimization_barrier((operand, sent[-window]))
                sent.append(lax.ppermute(operand, both, [(a, a ^ offset) for a in range(n)]))
                arrived[x][j] = sent[-1]
        return arrived

    def to_owner(x, i):
        perm = []
        for a in range(n):
            sa, ua, ja = a // n_dst, (a % n_dst) // ratio, a % ratio
            perm.append((a, ua * n_dst + (sa ^ i) * ratio + ja))
        return lax.ppermute(x, both, perm)

    state = edge_state
    for level in range(NBLK):
        pool = gather_src(lowered, dirs_pool if level == 0 else None)
        mine, joined = [], []
        for x in range(groups):
            fresh = state
            if level > 0 and x > 0:
                fresh, _ = lax.optimization_barrier((state, joined[-1][0]))
            own, give, keep = message_call(level, x, fresh, pool)
            mine.append(own)
            joined.append(join_call(keep, lax.ppermute(give, "src", src_perm(1))))
        theirs = exchange(joined, 4 if level == 0 else 5)
        refined, sums = None, None
        for x in range(groups):
            refined, sums = refine_call(level, x, mine[x], theirs[x], refined, sums)
        if level == 0:
            parts = [to_owner(sums[i], i) for i in range(n_src)]
        else:
            received = lax.ppermute(sums[-1], "src", src_perm(1))
            parts = []
            for i in range(groups):
                other = received[i * ATOM_DEV : (i + 1) * ATOM_DEV].astype(F32)
                parts.append(to_owner((sums[i].astype(F32) + other).astype(BF16), 2 * i))
        total = functools.reduce(lambda a, b: a + b, [p.astype(F32) for p in parts])
        piece = (total * DEGREE ** (-0.5)).astype(BF16)
        if level == 0:
            region = [lax.all_gather(piece, "dst", axis=0, tiled=True)]
        else:
            region = [piece] + [
                lax.ppermute(piece, "dst", [(a, a ^ i) for a in range(n_dst)])
                for i in range(1, n_dst)
            ]
        out = update_call(level, state, refined, region)
        state = out[0]
        if level < NBLK - 1:
            lowered = out[1]
    return state


def solution(mesh):
    placed = (
        P(("src", "dst"), None),
        P(None, ("src", "dst")),
        P(("src", "dst")),
        P(("src", "dst")),
        P(("src", "dst")),
        P(("src", "dst"), None),
        P(("src", "dst"), None),
        P(),
        P(),
        P(),
    )
    return jax.shard_map(
        body, mesh=mesh, in_specs=placed, out_specs=P(("src", "dst"), None), check_vma=False
    )
```

```python
import functools

import jax
import jax.numpy as jnp
from jax import lax
from jax.experimental import pallas as pl
from jax.experimental.pallas import tpu as pltpu
from jax.sharding import PartitionSpec as P

BLK = 128
PAIRS = 4
NBLK = 2
NSPH = 4
ATOM_DEV = 32
DEGREE = 64
VMEM_LIMIT = 20 * 1024 * 1024

F32 = jnp.float32
BF16 = jnp.bfloat16


def silu(value):
    half = 0.5 * value
    return half + half * jnp.tanh(half)


def dot(a, b):
    return jnp.dot(a, b, preferred_element_type=F32)


def dot_last(a, b):
    return lax.dot_general(a, b, (((1,), (1,)), ((), ())), preferred_element_type=F32)


def dot_first(a, b):
    return lax.dot_general(a, b, (((0,), (0,)), ((), ())), preferred_element_type=F32)


def legendre(cosine):
    square = cosine * cosine
    return [
        cosine,
        1.5 * square - 0.5,
        (2.5 * square - 1.5) * cosine,
        (35.0 * square * square - 30.0 * square + 3.0) * 0.125,
    ]


def masked(value, cap, counts):
    position = lax.broadcasted_iota(jnp.int32, (cap, value.shape[1]), 0)
    parts = [
        jnp.where(position < count, value[i * cap : (i + 1) * cap], 0.0)
        for i, count in enumerate(counts)
    ]
    return jnp.concatenate(parts, axis=0)


def pack(low):
    half = low.shape[0] // 2
    return jnp.concatenate([low[:half], low[half:]], axis=1)


SMEM = pl.BlockSpec(memory_space=pltpu.SMEM)
VMEM = pl.BlockSpec(memory_space=pltpu.VMEM)
ANY = pl.BlockSpec(memory_space=pl.ANY)


def call(kernel, scalars, args, out_shape, scratch=(), flops=0, nbytes=0, aliases=None, out_specs=None):
    several = isinstance(out_shape, list)
    return pl.pallas_call(
        kernel,
        in_specs=[SMEM] * len(scalars) + [VMEM] * len(args),
        out_specs=out_specs or ([VMEM] * len(out_shape) if several else VMEM),
        out_shape=out_shape,
        scratch_shapes=list(scratch),
        input_output_aliases=aliases or {},
        compiler_params=pltpu.CompilerParams(vmem_limit_bytes=VMEM_LIMIT),
        cost_estimate=pl.CostEstimate(flops=flops, bytes_accessed=nbytes, transcendentals=0),
    )(*scalars, *args)


def array(shape, kind=BF16):
    return jax.ShapeDtypeStruct(shape, kind)


def span(start, size):
    return pl.ds(pl.multiple_of(start * size, size), size)


def body(
    edge_state, directions, src_atom, dst_atom, rev_pos, counts, triplets, down_w, trip_w, edge_w
):
    n_src = lax.axis_size("src")
    n_dst = lax.axis_size("dst")
    n = n_src * n_dst
    rows, width = edge_state.shape
    trip = down_w.shape[2]
    cap = rows // n
    sb = rows // n_src
    spb = sb // BLK
    half = sb // 2
    chunk = min(sb, 256)
    groups = n_src // 2
    nblock = rows // BLK
    ratio = n_dst // n_src
    dst_rows = ATOM_DEV * n_src
    region_rows = ratio * dst_rows
    prows = rows // 2
    both = ("src", "dst")
    chunks = range(sb // chunk)
    per = chunk // cap

    s = lax.axis_index("src")
    d = lax.axis_index("dst")

    cnt = counts.reshape(-1)
    flat = triplets.T.reshape(-1)
    block = flat % nblock
    pool_row = ((flat // nblock) ^ s) * prows + block // spb * half + block % (spb // 2) * BLK
    pool_half = (block % spb) // (spb // 2)
    meta = jnp.concatenate([jnp.stack([s, d]), pool_row, pool_half, flat]).astype(jnp.int32)
    at_row = 2
    at_half = at_row + nblock * PAIRS
    at_block = at_half + nblock * PAIRS
    down_t = jnp.swapaxes(down_w, 1, 2)

    def counts_at(cnt_ref, block, h=None):
        first = block * n_dst + (0 if h is None else h * per)
        return [cnt_ref[first + i] for i in range(n_dst if h is None else per)]

    def split(value):
        return [value[h * chunk : (h + 1) * chunk] for h in chunks]

    def lower_kernel(cnt_ref, state_ref, down_ref, out_ref):
        @pl.loop(0, n_src)
        def _(i):
            low = silu(dot_last(state_ref[span(i, sb), :], down_ref[0]))
            out_ref[span(i, half), :] = pack(masked(low, cap, counts_at(cnt_ref, i)).astype(BF16))

    lowered = call(
        lower_kernel,
        (cnt,),
        (edge_state, down_t),
        array((prows, 2 * trip)),
        (),
        2 * rows * width * trip,
        rows * width * 2,
    )

    def src_perm(i):
        return [(a, a ^ i) for a in range(n_src)]

    def gather_src(x, before=None):
        slots = [None] * n_src
        slots[0] = x
        for i in range(2, n_src, 2):
            slots[i] = lax.ppermute(x, "src", src_perm(i))
        slots[1] = lax.ppermute(x, "src", src_perm(1))
        for i in range(2, n_src, 2):
            if before is not None:
                slots[i], _ = lax.optimization_barrier((slots[i], before))
            slots[i + 1] = lax.ppermute(slots[i], "src", src_perm(1))
        return slots

    own_dirs, _ = lax.optimization_barrier((directions, lowered))
    dirs_pool = lax.all_gather(own_dirs, "src", axis=1, tiled=True)

    def tiles_kernel(m, own_ref, pool_ref, out_ref):
        @pl.loop(0, nblock)
        def _(c):
            own = own_ref[:, span(c, BLK)]
            col = jnp.concatenate([own, jnp.zeros((5, BLK), F32)], axis=0).T
            for q in range(PAIRS):
                chosen = pool_ref[:, span(m[at_block + q * nblock + c], BLK)]
                cosine = (
                    col[:, 0:1] * chosen[0:1]
                    + col[:, 1:2] * chosen[1:2]
                    + col[:, 2:3] * chosen[2:3]
                )
                for degree, tile in enumerate(legendre(cosine)):
                    out_ref[c, degree, :, q * BLK : (q + 1) * BLK] = tile.astype(BF16)

    tiles = call(
        tiles_kernel,
        (meta,),
        (directions, dirs_pool),
        array((nblock, NSPH, BLK, PAIRS * BLK)),
        (),
        nblock * BLK * PAIRS * BLK * 2000,
        nblock * NSPH * BLK * PAIRS * BLK * 2,
    )

    rev_row = rev_pos.reshape(n_src, 1, sb)
    dst_row = dst_atom.reshape(n_src, 1, sb)
    src_row = src_atom.reshape(n_src, 1, sb)
    tri_scale = (BLK * PAIRS) ** (-0.5)

    def here(m, x, i):
        return m[0] ^ (2 * x) ^ 1 ^ i

    def message_call(level, x, state, pool):
        def kernel(cnt_ref, m, tiles_ref, state_ref, w_ref, up_ref, rev_ref, *refs):
            pool_refs, refs = refs[:n_src], refs[n_src:]
            mine_ref, give_ref, keep_ref, pool_all, hold = refs
            for k in range(n_src):
                pool_all[k * prows : (k + 1) * prows, :] = pool_refs[k][...]
            target_row = lax.broadcasted_iota(jnp.int32, (chunk, chunk), 0)
            base = lax.broadcasted_iota(jnp.int32, (1, chunk), 1) // cap * cap
            for i, out_ref in enumerate((give_ref, keep_ref)):
                at_src = here(m, x, i)
                triple = []
                for c in range(spb):
                    chosen = []
                    for q in range(PAIRS):
                        which = q * nblock + at_src * spb + c
                        v = pool_all[pl.ds(pl.multiple_of(m[at_row + which], BLK), BLK), :]
                        chosen.append(jnp.where(m[at_half + which] == 1, v[:, trip:], v[:, :trip]))
                    summed = dot(
                        tiles_ref[at_src * spb + c].reshape(NSPH * BLK, PAIRS * BLK),
                        jnp.concatenate(chosen, axis=0),
                    )
                    summed = (summed * tri_scale).astype(BF16)
                    triple.append(
                        jnp.concatenate(
                            [summed[l * BLK : (l + 1) * BLK] for l in range(NSPH)], axis=1
                        )
                    )
                triple = split(jnp.concatenate(triple, axis=0))
                per_src = sb // chunk
                pre = [
                    dot(state_ref[span(at_src * per_src + h, chunk), :], w_ref[level, 0])
                    + dot(triple[h], up_ref[level])
                    for h in chunks
                ]
                for h in chunks:
                    message = masked(silu(pre[h]), cap, counts_at(cnt_ref, at_src, h)).astype(BF16)
                    mine_ref[span((at_src & 1) * per_src + h, chunk), :] = message
                    rev = rev_ref[at_src, :, h * chunk : (h + 1) * chunk]
                    pick = jnp.where(target_row == rev + base, 1.0, 0.0).astype(BF16)
                    hold[h * chunk : (h + 1) * chunk, :] = dot(pick, message).astype(BF16)
                for j in range(n_dst):
                    out_ref[j * cap : (j + 1) * cap, :] = hold[span(m[1] ^ j, cap), :]

        return call(
            kernel,
            (cnt, meta),
            (tiles, state, edge_w, trip_w, rev_row, *pool),
            [array((2 * sb, width)), array((sb, width)), array((sb, width))],
            [pltpu.VMEM((n_src * prows, 2 * trip), BF16), pltpu.VMEM((sb, width), BF16)],
            4 * sb * width * (width + 2 * NSPH * trip) + 4 * sb * NSPH * 512 * 256,
            9 * 2**20,
        )

    def join_call(keep, received):
        def kernel(keep_ref, received_ref, *out_refs):
            for j, out_ref in enumerate(out_refs):
                out_ref[:cap, :] = keep_ref[j * cap : (j + 1) * cap, :]
                out_ref[cap:, :] = received_ref[j * cap : (j + 1) * cap, :]

        return call(
            kernel,
            (),
            (keep, received),
            [array((2 * cap, width))] * n_dst,
            (),
            0,
            4 * sb * width * 2,
        )

    def refine_call(level, x, mine, theirs, refined, sums):
        first, last = x == 0, x == groups - 1

        def kernel(m, dst_ref, w_ref, mine_ref, *refs):
            their_refs, refs = refs[:n_dst], refs[n_dst:]
            if not first:
                sums_ref, refs = refs[1], refs[2:]
            out_ref, sum_refs, arrived, total = refs[0], refs[1:-2], refs[-2], refs[-1]
            for j in range(n_dst):
                arrived[2 * j * cap : 2 * (j + 1) * cap, :] = their_refs[j][...]
            total[...] = jnp.zeros_like(total) if first else sums_ref[...]
            atoms = lax.broadcasted_iota(jnp.int32, (dst_rows, chunk), 0)
            per_src = sb // chunk
            for i in range(2):
                at_src = here(m, x, i)
                symmetric = []
                for h in chunks:
                    theirs_h = jnp.concatenate(
                        [
                            arrived[span((j ^ m[1]) * 2 + 1 - i, cap), :]
                            for j in range(h * per, (h + 1) * per)
                        ],
                        axis=0,
                    )
                    mine_h = mine_ref[span((at_src & 1) * per_src + h, chunk), :]
                    symmetric.append((mine_h.astype(F32) + theirs_h.astype(F32)).astype(BF16))
                inner = [silu(dot(v, w_ref[level, 1])).astype(BF16) for v in symmetric]
                for h in chunks:
                    out = symmetric[h].astype(F32) + dot(inner[h], w_ref[level, 2])
                    out = out.astype(BF16)
                    out_ref[span(at_src * per_src + h, chunk), :] = out
                    targets = dst_ref[at_src, :, h * chunk : (h + 1) * chunk]
                    onehot = jnp.where(atoms == targets, 1.0, 0.0).astype(BF16)
                    total[...] += dot(onehot, out)
            if last:
                for k in range(n_src):
                    sum_refs[k][...] = total[span(m[0] ^ k, ATOM_DEV), :].astype(BF16)
            else:
                sum_refs[0][...] = total[...]

        args = (dst_row, edge_w, mine, *theirs)
        aliases = {}
        if not first:
            aliases = {1 + len(args): 0}
            args = (*args, refined, sums)
        out = call(
            kernel,
            (meta,),
            args,
            [array((rows, width))]
            + ([array((ATOM_DEV, width))] * n_src if last else [array((dst_rows, width), F32)]),
            [pltpu.VMEM((2 * sb, width), BF16), pltpu.VMEM((dst_rows, width), F32)],
            4 * sb * width * (2 * width + dst_rows),
            6 * 2**20,
            aliases,
        )
        return out[0], (out[1:] if last else out[1])

    def update_call(level, state, refined, pieces):
        last = level == NBLK - 1

        def kernel(cnt_ref, m, src_ref, state_ref, refined_ref, w_ref, down_ref, *refs):
            piece_refs, out_ref, refs = refs[:n_dst], refs[n_dst], refs[n_dst + 1 :]
            region = refs[1] if not last else refs[0]
            for k, piece_ref in enumerate(piece_refs):
                region[k * ATOM_DEV : (k + 1) * ATOM_DEV, :] = piece_ref[...]
            per_src = sb // chunk
            lines = lax.broadcasted_iota(jnp.int32, (region_rows, sb), 0)

            @pl.loop(0, n_src)
            def _(i):
                atom = src_ref[i]
                where = (atom % dst_rows) // ATOM_DEV * ratio + atom // dst_rows
                where = (where ^ m[1]) * ATOM_DEV + atom % ATOM_DEV
                pick = jnp.where(lines == where, 1.0, 0.0).astype(BF16)
                feed = split(dot_first(pick, region[...]))
                refined_v = [
                    refined_ref[span(i * per_src + h, chunk), :].astype(F32) for h in chunks
                ]
                joined = [(a + b).astype(BF16) for a, b in zip(refined_v, feed)]
                one = [silu(dot(v, w_ref[level, 3])).astype(BF16) for v in joined]
                two = [silu(dot(v, w_ref[level, 4])).astype(BF16) for v in one]
                low = []
                for h in chunks:
                    at = span(i * per_src + h, chunk)
                    counts_h = counts_at(cnt_ref, i, h)
                    new = state_ref[at, :].astype(F32) + refined_v[h] + dot(two[h], w_ref[level, 5])
                    new = masked(new * (0.5**0.5), cap, counts_h).astype(BF16)
                    if last:
                        refs[1][at, :] = new
                    else:
                        out_ref[at, :] = new
                        low.append(masked(silu(dot_last(new, down_ref[level + 1])), cap, counts_h))
                if last:
                    pltpu.make_async_copy(
                        refs[1].at[span(i, sb)], out_ref.at[span(i, sb)], refs[2].at[i]
                    ).start()
                else:
                    refs[0][span(i, half), :] = pack(jnp.concatenate(low, axis=0).astype(BF16))

            if last:
                for i in range(n_src):
                    at = slice(i * sb, (i + 1) * sb)
                    pltpu.make_async_copy(refs[1].at[at], out_ref.at[at], refs[2].at[i]).wait()

        scratch = [pltpu.VMEM((region_rows, width), BF16)]
        if last:
            out_shape, out_specs = [array((rows, width))], [ANY]
            scratch += [pltpu.VMEM((rows, width), BF16), pltpu.SemaphoreType.DMA((n_src,))]
        else:
            out_shape, out_specs = [array((rows, width)), array((prows, 2 * trip))], None
        return call(
            kernel,
            (cnt, meta),
            (src_row, state, refined, edge_w, down_t, *pieces),
            out_shape,
            scratch,
            2 * rows * width * (3 * width + region_rows + trip),
            8 * 2**20,
            None,
            out_specs,
        )

    def exchange(joined, window):
        mid = n_dst // 2
        order = [j for pair in zip(range(mid, n_dst), range(mid - 1, -1, -1)) for j in pair]
        arrived = [[None] * n_dst for _ in range(groups)]
        arrived[0][0] = joined[0][0]
        sent = []
        for x in range(groups):
            for j in order:
                if arrived[x][j] is not None:
                    continue
                operand, offset = joined[x][j], 2 * x * n_dst + j
                if len(sent) >= window:
                    operand, _ = lax.optimization_barrier((operand, sent[-window]))
                sent.append(lax.ppermute(operand, both, [(a, a ^ offset) for a in range(n)]))
                arrived[x][j] = sent[-1]
        return arrived

    def to_owner(x, i):
        perm = []
        for a in range(n):
            sa, ua, ja = a // n_dst, (a % n_dst) // ratio, a % ratio
            perm.append((a, ua * n_dst + (sa ^ i) * ratio + ja))
        return lax.ppermute(x, both, perm)

    state = edge_state
    for level in range(NBLK):
        pool = gather_src(lowered, dirs_pool if level == 0 else None)
        mine, joined = [], []
        for x in range(groups):
            fresh = state
            if x > 0:
                fresh, _ = lax.optimization_barrier((state, joined[-1][0]))
            own, give, keep = message_call(level, x, fresh, pool)
            mine.append(own)
            joined.append(join_call(keep, lax.ppermute(give, "src", src_perm(1))))
        theirs = exchange(joined, 5)
        refined, sums = None, None
        for x in range(groups):
            refined, sums = refine_call(level, x, mine[x], theirs[x], refined, sums)
        parts = [to_owner(sums[i], i) for i in range(n_src)]
        total = functools.reduce(lambda a, b: a + b, [p.astype(F32) for p in parts])
        piece = (total * DEGREE ** (-0.5)).astype(BF16)
        region = [piece] + [
            lax.ppermute(piece, "dst", [(a, a ^ i) for a in range(n_dst)]) for i in range(1, n_dst)
        ]
        out = update_call(level, state, refined, region)
        state = out[0]
        if level < NBLK - 1:
            lowered = out[1]
    return state


def solution(mesh):
    placed = (
        P(("src", "dst"), None),
        P(None, ("src", "dst")),
        P(("src", "dst")),
        P(("src", "dst")),
        P(("src", "dst")),
        P(("src", "dst"), None),
        P(("src", "dst"), None),
        P(),
        P(),
        P(),
    )
    return jax.shard_map(
        body, mesh=mesh, in_specs=placed, out_specs=P(("src", "dst"), None), check_vma=False
    )
```

```python
import functools

import jax
import jax.numpy as jnp
from jax import lax
from jax.experimental import pallas as pl
from jax.experimental.pallas import tpu as pltpu
from jax.sharding import PartitionSpec as P

BLK = 128
PAIRS = 4
NBLK = 2
NSPH = 4
ATOM_DEV = 32
DEGREE = 64
VMEM_LIMIT = 20 * 1024 * 1024

F32 = jnp.float32
BF16 = jnp.bfloat16


def silu(value):
    half = 0.5 * value
    return half + half * jnp.tanh(half)


def dot(a, b):
    return jnp.dot(a, b, preferred_element_type=F32)


def dot_last(a, b):
    return lax.dot_general(a, b, (((1,), (1,)), ((), ())), preferred_element_type=F32)


def dot_first(a, b):
    return lax.dot_general(a, b, (((0,), (0,)), ((), ())), preferred_element_type=F32)


def legendre(cosine):
    square = cosine * cosine
    return [
        cosine,
        1.5 * square - 0.5,
        (2.5 * square - 1.5) * cosine,
        (4.375 * square - 3.75) * square + 0.375,
    ]


def masked(value, cap, counts):
    position = lax.broadcasted_iota(jnp.int32, (cap, value.shape[1]), 0)
    parts = [
        jnp.where(position < count, value[i * cap : (i + 1) * cap], 0.0)
        for i, count in enumerate(counts)
    ]
    return jnp.concatenate(parts, axis=0)


def pack(low):
    half = low.shape[0] // 2
    return jnp.concatenate([low[:half], low[half:]], axis=1)


SMEM = pl.BlockSpec(memory_space=pltpu.SMEM)
VMEM = pl.BlockSpec(memory_space=pltpu.VMEM)
ANY = pl.BlockSpec(memory_space=pl.ANY)


def call(kernel, scalars, args, out_shape, scratch=(), flops=0, nbytes=0, aliases=None, out_specs=None):
    several = isinstance(out_shape, list)
    return pl.pallas_call(
        kernel,
        in_specs=[SMEM] * len(scalars) + [VMEM] * len(args),
        out_specs=out_specs or ([VMEM] * len(out_shape) if several else VMEM),
        out_shape=out_shape,
        scratch_shapes=list(scratch),
        input_output_aliases=aliases or {},
        compiler_params=pltpu.CompilerParams(vmem_limit_bytes=VMEM_LIMIT),
        cost_estimate=pl.CostEstimate(flops=flops, bytes_accessed=nbytes, transcendentals=0),
    )(*scalars, *args)


def array(shape, kind=BF16):
    return jax.ShapeDtypeStruct(shape, kind)


def span(start, size):
    return pl.ds(pl.multiple_of(start * size, size), size)


def body(
    edge_state, directions, src_atom, dst_atom, rev_pos, counts, triplets, down_w, trip_w, edge_w
):
    n_src = lax.axis_size("src")
    n_dst = lax.axis_size("dst")
    n = n_src * n_dst
    rows, width = edge_state.shape
    trip = down_w.shape[2]
    cap = rows // n
    sb = rows // n_src
    spb = sb // BLK
    half = sb // 2
    chunk = min(sb, 256)
    groups = n_src // 2
    nblock = rows // BLK
    ratio = n_dst // n_src
    dst_rows = ATOM_DEV * n_src
    region_rows = ratio * dst_rows
    prows = rows // 2
    both = ("src", "dst")
    chunks = range(sb // chunk)
    per = chunk // cap

    s = lax.axis_index("src")
    d = lax.axis_index("dst")

    cnt = counts.reshape(-1)
    flat = triplets.T.reshape(-1)
    block = flat % nblock
    rel = (flat // nblock) ^ s
    pool_row = rel * prows + block // spb * half + block % (spb // 2) * BLK
    pool_half = (block % spb) // (spb // 2)
    meta = jnp.concatenate([jnp.stack([s, d]), pool_row, pool_half, rel * nblock + block]).astype(jnp.int32)
    at_row = 2
    at_half = at_row + nblock * PAIRS
    at_block = at_half + nblock * PAIRS
    down_t = jnp.swapaxes(down_w, 1, 2)

    def counts_at(cnt_ref, block, h=None):
        first = block * n_dst + (0 if h is None else h * per)
        return [cnt_ref[first + i] for i in range(n_dst if h is None else per)]

    def split(value):
        return [value[h * chunk : (h + 1) * chunk] for h in chunks]

    def lower_kernel(cnt_ref, state_ref, down_ref, out_ref):
        @pl.loop(0, n_src)
        def _(i):
            low = silu(dot_last(state_ref[span(i, sb), :], down_ref[0]))
            out_ref[span(i, half), :] = pack(masked(low, cap, counts_at(cnt_ref, i)).astype(BF16))

    lowered = call(
        lower_kernel,
        (cnt,),
        (edge_state, down_t),
        array((prows, 2 * trip)),
        (),
        2 * rows * width * trip,
        rows * width * 2,
    )

    def src_perm(i):
        return [(a, a ^ i) for a in range(n_src)]

    def gather_src(x):
        slots = [None] * n_src
        slots[0] = x
        for i in range(2, n_src, 2):
            slots[i] = lax.ppermute(x, "src", src_perm(i))
        for i in range(0, n_src, 2):
            slots[i + 1] = lax.ppermute(slots[i], "src", src_perm(1))
        return slots

    dirs_pool = gather_src(directions)

    def tiles_kernel(m, *refs):
        own_ref, out_ref, pool_ref = refs[0], refs[n_src], refs[n_src + 1]
        for k in range(n_src):
            pool_ref[:, k * rows : (k + 1) * rows] = refs[k][...]

        @pl.loop(0, nblock)
        def _(c):
            own = own_ref[:, span(c, BLK)]
            col = jnp.concatenate([own, jnp.zeros((5, BLK), F32)], axis=0).T
            for q in range(PAIRS):
                chosen = pool_ref[:, span(m[at_block + q * nblock + c], BLK)]
                cosine = (
                    col[:, 0:1] * chosen[0:1]
                    + col[:, 1:2] * chosen[1:2]
                    + col[:, 2:3] * chosen[2:3]
                )
                for degree, tile in enumerate(legendre(cosine)):
                    out_ref[c, degree, :, q * BLK : (q + 1) * BLK] = tile.astype(BF16)

    tiles = call(
        tiles_kernel,
        (meta,),
        dirs_pool,
        array((nblock, NSPH, BLK, PAIRS * BLK)),
        [pltpu.VMEM((3, n_src * rows), F32)],
        nblock * BLK * PAIRS * BLK * 2000,
        nblock * NSPH * BLK * PAIRS * BLK * 2,
    )

    rev_row = rev_pos.reshape(n_src, 1, sb)
    dst_row = dst_atom.reshape(n_src, 1, sb)
    src_row = src_atom.reshape(n_src, 1, sb)
    tri_scale = (BLK * PAIRS) ** (-0.5)

    def here(m, x, i):
        return m[0] ^ (2 * x) ^ 1 ^ i

    def message_call(level, x, state, pool):
        def kernel(cnt_ref, m, tiles_ref, state_ref, w_ref, up_ref, rev_ref, *refs):
            pool_refs, refs = refs[:n_src], refs[n_src:]
            mine_ref, give_ref, keep_ref, pool_all, hold = refs
            for k in range(n_src):
                pool_all[k * prows : (k + 1) * prows, :] = pool_refs[k][...]
            target_row = lax.broadcasted_iota(jnp.int32, (chunk, chunk), 0)
            base = lax.broadcasted_iota(jnp.int32, (1, chunk), 1) // cap * cap
            for i, out_ref in enumerate((give_ref, keep_ref)):
                at_src = here(m, x, i)
                triple = []
                for c in range(spb):
                    chosen = []
                    for q in range(PAIRS):
                        which = q * nblock + at_src * spb + c
                        v = pool_all[pl.ds(pl.multiple_of(m[at_row + which], BLK), BLK), :]
                        chosen.append(jnp.where(m[at_half + which] == 1, v[:, trip:], v[:, :trip]))
                    summed = dot(
                        tiles_ref[at_src * spb + c].reshape(NSPH * BLK, PAIRS * BLK),
                        jnp.concatenate(chosen, axis=0),
                    )
                    summed = (summed * tri_scale).astype(BF16)
                    triple.append(
                        jnp.concatenate(
                            [summed[l * BLK : (l + 1) * BLK] for l in range(NSPH)], axis=1
                        )
                    )
                triple = jnp.concatenate(triple, axis=0)
                size = sb if x == 0 else chunk
                message = []
                for h in range(sb // size):
                    pre = dot(state_ref[span(at_src * (sb // size) + h, size), :], w_ref[level, 0])
                    pre = pre + dot(triple[h * size : (h + 1) * size], up_ref[level])
                    counts_h = counts_at(cnt_ref, at_src)[h * size // cap : (h + 1) * size // cap]
                    message.append(masked(silu(pre), cap, counts_h).astype(BF16))
                message = jnp.concatenate(message, axis=0)
                mine_ref[span(at_src & 1, sb), :] = message
                for h in chunks:
                    at = slice(h * chunk, (h + 1) * chunk)
                    pick = jnp.where(target_row == rev_ref[at_src, :, at] + base, 1.0, 0.0)
                    hold[at, :] = dot(pick.astype(BF16), message[at]).astype(BF16)
                for j in range(n_dst):
                    out_ref[j * cap : (j + 1) * cap, :] = hold[span(m[1] ^ j, cap), :]

        return call(
            kernel,
            (cnt, meta),
            (tiles, state, edge_w, trip_w, rev_row, *pool),
            [array((2 * sb, width)), array((sb, width)), array((sb, width))],
            [pltpu.VMEM((n_src * prows, 2 * trip), BF16), pltpu.VMEM((sb, width), BF16)],
            4 * sb * width * (width + 2 * NSPH * trip) + 4 * sb * NSPH * 512 * 256,
            9 * 2**20,
        )

    def join_call(keep, received):
        def kernel(keep_ref, received_ref, *out_refs):
            for j, out_ref in enumerate(out_refs):
                out_ref[:cap, :] = keep_ref[j * cap : (j + 1) * cap, :]
                out_ref[cap:, :] = received_ref[j * cap : (j + 1) * cap, :]

        return call(
            kernel,
            (),
            (keep, received),
            [array((2 * cap, width))] * n_dst,
            (),
            0,
            4 * sb * width * 2,
        )

    def refine_call(level, x, mine, theirs, refined, sums):
        first, last = x == 0, x == groups - 1

        def kernel(m, dst_ref, w_ref, mine_ref, *refs):
            their_refs, refs = refs[:n_dst], refs[n_dst:]
            if not first:
                sums_ref, refs = refs[1], refs[2:]
            out_ref, sum_refs, arrived, total = refs[0], refs[1:-2], refs[-2], refs[-1]
            for j in range(n_dst):
                arrived[2 * j * cap : 2 * (j + 1) * cap, :] = their_refs[j][...]
            total[...] = jnp.zeros_like(total) if first else sums_ref[...]
            for steps in ([(0,), (1,)] if first else [(0, 1)]):
                symmetric = []
                for i in steps:
                    theirs_i = [
                        arrived[span((j ^ m[1]) * 2 + 1 - i, cap), :] for j in range(n_dst)
                    ]
                    theirs_i = jnp.concatenate(theirs_i, axis=0).astype(F32)
                    mine_i = mine_ref[span(here(m, x, i) & 1, sb), :].astype(F32)
                    symmetric.append((mine_i + theirs_i).astype(BF16))
                symmetric = jnp.concatenate(symmetric, axis=0)
                inner = silu(dot(symmetric, w_ref[level, 1])).astype(BF16)
                out = symmetric.astype(F32) + dot(inner, w_ref[level, 2])
                out = out.astype(BF16)
                targets = []
                for k, i in enumerate(steps):
                    out_ref[span(here(m, x, i), sb), :] = out[k * sb : (k + 1) * sb]
                    targets.append(dst_ref[here(m, x, i)])
                atoms = lax.broadcasted_iota(jnp.int32, (dst_rows, len(steps) * sb), 0)
                onehot = jnp.where(atoms == jnp.concatenate(targets, axis=1), 1.0, 0.0)
                total[...] += dot(onehot.astype(BF16), out)
            if last:
                for k in range(n_src):
                    sum_refs[k][...] = total[span(m[0] ^ k, ATOM_DEV), :].astype(BF16)
            else:
                sum_refs[0][...] = total[...]

        args = (dst_row, edge_w, mine, *theirs)
        aliases = {}
        if not first:
            aliases = {1 + len(args): 0}
            args = (*args, refined, sums)
        out = call(
            kernel,
            (meta,),
            args,
            [array((rows, width))]
            + ([array((ATOM_DEV, width))] * n_src if last else [array((dst_rows, width), F32)]),
            [pltpu.VMEM((2 * sb, width), BF16), pltpu.VMEM((dst_rows, width), F32)],
            4 * sb * width * (2 * width + dst_rows),
            6 * 2**20,
            aliases,
        )
        return out[0], (out[1:] if last else out[1])

    def update_call(level, state, refined, pieces):
        last = level == NBLK - 1

        def kernel(cnt_ref, m, src_ref, state_ref, refined_ref, w_ref, down_ref, *refs):
            piece_refs, refs = refs[: len(pieces)], refs[len(pieces) :]
            out_ref, refs = refs[0], refs[1:]
            region = refs[1] if not last else refs[0]
            filled = 0
            for piece_ref in piece_refs:
                region[filled : filled + piece_ref.shape[0], :] = piece_ref[...]
                filled += piece_ref.shape[0]
            many = 2 if last else 1
            size = many * sb
            lines = lax.broadcasted_iota(jnp.int32, (region_rows, size), 0)

            @pl.loop(0, n_src // many)
            def _(i):
                atom = jnp.concatenate([src_ref[i * many + k] for k in range(many)], axis=1)
                where = (atom % dst_rows) // ATOM_DEV * ratio + atom // dst_rows
                where = where ^ m[1]
                where = (where % 2 * (n_dst // 2) + where // 2) * ATOM_DEV + atom % ATOM_DEV
                pick = jnp.where(lines == where, 1.0, 0.0).astype(BF16)
                at = span(i, size)
                refined_v = refined_ref[at, :].astype(F32)
                joined = (refined_v + dot_first(pick, region[...])).astype(BF16)
                one = silu(dot(joined, w_ref[level, 3])).astype(BF16)
                two = silu(dot(one, w_ref[level, 4])).astype(BF16)
                counts_i = []
                for k in range(many):
                    counts_i += counts_at(cnt_ref, i * many + k)
                new = state_ref[at, :].astype(F32) + refined_v + dot(two, w_ref[level, 5])
                new = masked(new * (0.5**0.5), cap, counts_i).astype(BF16)
                if last:
                    refs[1][at, :] = new
                    pltpu.make_async_copy(refs[1].at[at], out_ref.at[at], refs[2].at[i]).start()
                else:
                    out_ref[at, :] = new
                    low = masked(silu(dot_last(new, down_ref[level + 1])), cap, counts_i)
                    refs[0][span(i, half), :] = pack(low.astype(BF16))

            if last:
                for i in range(n_src // many):
                    at = slice(i * size, (i + 1) * size)
                    pltpu.make_async_copy(refs[1].at[at], out_ref.at[at], refs[2].at[i]).wait()

        scratch = [pltpu.VMEM((region_rows, width), BF16)]
        if last:
            out_shape, out_specs = [array((rows, width))], [ANY]
            scratch += [pltpu.VMEM((rows, width), BF16), pltpu.SemaphoreType.DMA((n_src,))]
        else:
            out_shape, out_specs = [array((rows, width)), array((prows, 2 * trip))], None
        return call(
            kernel,
            (cnt, meta),
            (src_row, state, refined, edge_w, down_t, *pieces),
            out_shape,
            scratch,
            2 * rows * width * (3 * width + region_rows + trip),
            8 * 2**20,
            None,
            out_specs,
        )

    def exchange_order():
        mid = n_dst // 2
        over = [(k + 1.5 * x, x, j) for x in range(groups) for k, j in enumerate(range(mid, n_dst))]
        near = [
            (k + 1.5 * x, x, j)
            for x in range(groups)
            for k, j in enumerate(range(mid - 1, -1, -1))
            if (x, j) != (0, 0)
        ]
        order = []
        for k, (_, x, j) in enumerate(sorted(over)):
            order.append((x, j))
            if k < len(near):
                order.append(sorted(near)[k][1:])
        return order

    def exchange(level, state, pool, window):
        mine, joined, arrived = [], [], [[None] * n_dst for _ in range(groups)]
        sent = []

        def prepare(x):
            own, give, keep = message_call(level, x, state, pool)
            mine.append(own)
            joined.append(join_call(keep, lax.ppermute(give, "src", src_perm(1))))

        prepare(0)
        arrived[0][0] = joined[0][0]
        for x, j in exchange_order():
            while len(joined) <= x:
                prepare(len(joined))
            operand, offset = joined[x][j], 2 * x * n_dst + j
            if len(sent) >= window:
                operand, _ = lax.optimization_barrier((operand, sent[-window]))
            sent.append(lax.ppermute(operand, both, [(a, a ^ offset) for a in range(n)]))
            arrived[x][j] = sent[-1]
        return mine, arrived

    def to_owner(x, i):
        perm = []
        for a in range(n):
            sa, ua, ja = a // n_dst, (a % n_dst) // ratio, a % ratio
            perm.append((a, ua * n_dst + (sa ^ i) * ratio + ja))
        return lax.ppermute(x, both, perm)

    state = edge_state
    for level in range(NBLK):
        pool = gather_src(lowered)
        mine, theirs = exchange(level, state, pool, 5)
        refined, sums = None, None
        for x in range(groups):
            refined, sums = refine_call(level, x, mine[x], theirs[x], refined, sums)
        parts = [to_owner(sums[i], i) for i in range(n_src)]
        total = functools.reduce(lambda a, b: a + b, [p.astype(F32) for p in parts])
        piece = (total * DEGREE ** (-0.5)).astype(BF16)
        along = [
            lax.ppermute(piece, "dst", [(a, a ^ i) for a in range(n_dst)])
            for i in range(2, n_dst, 2)
        ]
        beside = lax.ppermute(piece, "dst", [(a, a ^ 1) for a in range(n_dst)])
        rest = lax.ppermute(
            jnp.concatenate(along, axis=0), "dst", [(a, a ^ 1) for a in range(n_dst)]
        )
        region = [piece, *along, beside, rest]
        out = update_call(level, state, refined, region)
        state = out[0]
        if level < NBLK - 1:
            lowered = out[1]
    return state


def solution(mesh):
    placed = (
        P(("src", "dst"), None),
        P(None, ("src", "dst")),
        P(("src", "dst")),
        P(("src", "dst")),
        P(("src", "dst")),
        P(("src", "dst"), None),
        P(("src", "dst"), None),
        P(),
        P(),
        P(),
    )
    return jax.shard_map(
        body, mesh=mesh, in_specs=placed, out_specs=P(("src", "dst"), None), check_vma=False
    )
```

```python
import functools

import jax
import jax.numpy as jnp
from jax import lax
from jax.experimental import pallas as pl
from jax.experimental.pallas import tpu as pltpu
from jax.sharding import PartitionSpec as P

BLK = 128
PAIRS = 4
NBLK = 2
NSPH = 4
ATOM_DEV = 32
DEGREE = 64
VMEM_LIMIT = 20 * 1024 * 1024

F32 = jnp.float32
BF16 = jnp.bfloat16


def silu(value):
    half = 0.5 * value
    return half + half * jnp.tanh(half)


def dot(a, b):
    return jnp.dot(a, b, preferred_element_type=F32)


def dot_last(a, b):
    return lax.dot_general(a, b, (((1,), (1,)), ((), ())), preferred_element_type=F32)


def dot_first(a, b):
    return lax.dot_general(a, b, (((0,), (0,)), ((), ())), preferred_element_type=F32)


def legendre(cosine):
    square = cosine * cosine
    return [
        cosine,
        1.5 * square - 0.5,
        (2.5 * square - 1.5) * cosine,
        (4.375 * square - 3.75) * square + 0.375,
    ]


def masked(value, cap, counts):
    position = lax.broadcasted_iota(jnp.int32, (cap, value.shape[1]), 0)
    parts = [
        jnp.where(position < count, value[i * cap : (i + 1) * cap], 0.0)
        for i, count in enumerate(counts)
    ]
    return jnp.concatenate(parts, axis=0)


def pack(low):
    half = low.shape[0] // 2
    return jnp.concatenate([low[:half], low[half:]], axis=1)


SMEM = pl.BlockSpec(memory_space=pltpu.SMEM)
VMEM = pl.BlockSpec(memory_space=pltpu.VMEM)
ANY = pl.BlockSpec(memory_space=pl.ANY)


def call(kernel, scalars, args, out_shape, scratch=(), flops=0, nbytes=0, aliases=None, out_specs=None):
    several = isinstance(out_shape, list)
    return pl.pallas_call(
        kernel,
        in_specs=[SMEM] * len(scalars) + [VMEM] * len(args),
        out_specs=out_specs or ([VMEM] * len(out_shape) if several else VMEM),
        out_shape=out_shape,
        scratch_shapes=list(scratch),
        input_output_aliases=aliases or {},
        compiler_params=pltpu.CompilerParams(vmem_limit_bytes=VMEM_LIMIT),
        cost_estimate=pl.CostEstimate(flops=flops, bytes_accessed=nbytes, transcendentals=0),
    )(*scalars, *args)


def array(shape, kind=BF16):
    return jax.ShapeDtypeStruct(shape, kind)


def span(start, size):
    return pl.ds(pl.multiple_of(start * size, size), size)


def body(
    edge_state, directions, src_atom, dst_atom, rev_pos, counts, triplets, down_w, trip_w, edge_w
):
    n_src = lax.axis_size("src")
    n_dst = lax.axis_size("dst")
    n = n_src * n_dst
    rows, width = edge_state.shape
    trip = down_w.shape[2]
    cap = rows // n
    sb = rows // n_src
    spb = sb // BLK
    half = sb // 2
    chunk = min(sb, 256)
    groups = n_src // 2
    nblock = rows // BLK
    ratio = n_dst // n_src
    dst_rows = ATOM_DEV * n_src
    region_rows = ratio * dst_rows
    prows = rows // 2
    both = ("src", "dst")
    chunks = range(sb // chunk)
    per = chunk // cap

    s = lax.axis_index("src")
    d = lax.axis_index("dst")

    cnt = counts.reshape(-1)
    flat = triplets.T.reshape(-1)
    block = flat % nblock
    rel = (flat // nblock) ^ s
    pool_row = rel * prows + block // spb * half + block % (spb // 2) * BLK
    pool_half = (block % spb) // (spb // 2)
    meta = jnp.concatenate([jnp.stack([s, d]), pool_row, pool_half, rel * nblock + block]).astype(jnp.int32)
    at_row = 2
    at_half = at_row + nblock * PAIRS
    at_block = at_half + nblock * PAIRS
    down_t = jnp.swapaxes(down_w, 1, 2)

    def counts_at(cnt_ref, block, h=None):
        first = block * n_dst + (0 if h is None else h * per)
        return [cnt_ref[first + i] for i in range(n_dst if h is None else per)]

    def split(value):
        return [value[h * chunk : (h + 1) * chunk] for h in chunks]

    def lower_kernel(cnt_ref, state_ref, down_ref, out_ref):
        @pl.loop(0, n_src)
        def _(i):
            low = silu(dot_last(state_ref[span(i, sb), :], down_ref[0]))
            out_ref[span(i, half), :] = pack(masked(low, cap, counts_at(cnt_ref, i)).astype(BF16))

    lowered = call(
        lower_kernel,
        (cnt,),
        (edge_state, down_t),
        array((prows, 2 * trip)),
        (),
        2 * rows * width * trip,
        rows * width * 2,
    )

    def src_perm(i):
        return [(a, a ^ i) for a in range(n_src)]

    def gather_src(x, before=None):
        slots = [None] * n_src
        slots[0] = x
        for i in range(2, n_src, 2):
            slots[i] = lax.ppermute(x, "src", src_perm(i))
        for i in range(0, n_src, 2):
            if i and before is not None:
                slots[i], _ = lax.optimization_barrier((slots[i], before))
            slots[i + 1] = lax.ppermute(slots[i], "src", src_perm(1))
        return slots

    dirs_pool = gather_src(directions)

    def tiles_kernel(m, *refs):
        own_ref, out_ref, pool_ref = refs[0], refs[n_src], refs[n_src + 1]
        for k in range(n_src):
            pool_ref[:, k * rows : (k + 1) * rows] = refs[k][...]

        @pl.loop(0, nblock)
        def _(c):
            own = own_ref[:, span(c, BLK)]
            col = jnp.concatenate([own, jnp.zeros((5, BLK), F32)], axis=0).T
            for q in range(PAIRS):
                chosen = pool_ref[:, span(m[at_block + q * nblock + c], BLK)]
                cosine = (
                    col[:, 0:1] * chosen[0:1]
                    + col[:, 1:2] * chosen[1:2]
                    + col[:, 2:3] * chosen[2:3]
                )
                for degree, tile in enumerate(legendre(cosine)):
                    out_ref[c, degree, :, q * BLK : (q + 1) * BLK] = tile.astype(BF16)

    tiles = call(
        tiles_kernel,
        (meta,),
        dirs_pool,
        array((nblock, NSPH, BLK, PAIRS * BLK)),
        [pltpu.VMEM((3, n_src * rows), F32)],
        nblock * BLK * PAIRS * BLK * 2000,
        nblock * NSPH * BLK * PAIRS * BLK * 2,
    )

    rev_row = rev_pos.reshape(n_src, 1, sb)
    dst_row = dst_atom.reshape(n_src, 1, sb)
    src_row = src_atom.reshape(n_src, 1, sb)
    tri_scale = (BLK * PAIRS) ** (-0.5)

    def here(m, x, i):
        return m[0] ^ (2 * x) ^ 1 ^ i

    def message_call(level, x, state, pool):
        def kernel(cnt_ref, m, tiles_ref, state_ref, w_ref, up_ref, rev_ref, *refs):
            pool_refs, refs = refs[:n_src], refs[n_src:]
            mine_ref, give_ref, keep_ref, pool_all, hold = refs
            for k in range(n_src):
                pool_all[k * prows : (k + 1) * prows, :] = pool_refs[k][...]
            target_row = lax.broadcasted_iota(jnp.int32, (chunk, chunk), 0)
            base = lax.broadcasted_iota(jnp.int32, (1, chunk), 1) // cap * cap
            for i, out_ref in enumerate((give_ref, keep_ref)):
                at_src = here(m, x, i)
                triple = []
                for c in range(spb):
                    chosen = []
                    for q in range(PAIRS):
                        which = q * nblock + at_src * spb + c
                        v = pool_all[pl.ds(pl.multiple_of(m[at_row + which], BLK), BLK), :]
                        chosen.append(jnp.where(m[at_half + which] == 1, v[:, trip:], v[:, :trip]))
                    summed = dot(
                        tiles_ref[at_src * spb + c].reshape(NSPH * BLK, PAIRS * BLK),
                        jnp.concatenate(chosen, axis=0),
                    )
                    summed = (summed * tri_scale).astype(BF16)
                    triple.append(
                        jnp.concatenate(
                            [summed[l * BLK : (l + 1) * BLK] for l in range(NSPH)], axis=1
                        )
                    )
                triple = jnp.concatenate(triple, axis=0)
                size = chunk
                message = []
                for h in range(sb // size):
                    pre = dot(state_ref[span(at_src * (sb // size) + h, size), :], w_ref[level, 0])
                    pre = pre + dot(triple[h * size : (h + 1) * size], up_ref[level])
                    counts_h = counts_at(cnt_ref, at_src)[h * size // cap : (h + 1) * size // cap]
                    message.append(masked(silu(pre), cap, counts_h).astype(BF16))
                message = jnp.concatenate(message, axis=0)
                mine_ref[span(at_src & 1, sb), :] = message
                for h in chunks:
                    at = slice(h * chunk, (h + 1) * chunk)
                    pick = jnp.where(target_row == rev_ref[at_src, :, at] + base, 1.0, 0.0)
                    hold[at, :] = dot(pick.astype(BF16), message[at]).astype(BF16)
                for j in range(n_dst):
                    out_ref[j * cap : (j + 1) * cap, :] = hold[span(m[1] ^ j, cap), :]

        return call(
            kernel,
            (cnt, meta),
            (tiles, state, edge_w, trip_w, rev_row, *pool),
            [array((2 * sb, width)), array((sb, width)), array((sb, width))],
            [pltpu.VMEM((n_src * prows, 2 * trip), BF16), pltpu.VMEM((sb, width), BF16)],
            4 * sb * width * (width + 2 * NSPH * trip) + 4 * sb * NSPH * 512 * 256,
            9 * 2**20,
        )

    def join_call(keep, received):
        def kernel(keep_ref, received_ref, *out_refs):
            for j, out_ref in enumerate(out_refs):
                out_ref[:cap, :] = keep_ref[j * cap : (j + 1) * cap, :]
                out_ref[cap:, :] = received_ref[j * cap : (j + 1) * cap, :]

        return call(
            kernel,
            (),
            (keep, received),
            [array((2 * cap, width))] * n_dst,
            (),
            0,
            4 * sb * width * 2,
        )

    def refine_call(level, x, mine, theirs, refined, sums):
        first, last = x == 0, x == groups - 1

        def kernel(m, dst_ref, w_ref, mine_ref, *refs):
            their_refs, refs = refs[:n_dst], refs[n_dst:]
            if not first:
                sums_ref, refs = refs[1], refs[2:]
            out_ref, sum_refs, arrived, total = refs[0], refs[1:-2], refs[-2], refs[-1]
            for j in range(n_dst):
                arrived[2 * j * cap : 2 * (j + 1) * cap, :] = their_refs[j][...]
            total[...] = jnp.zeros_like(total) if first else sums_ref[...]
            for steps in ([(0,), (1,)] if first else [(0, 1)]):
                symmetric = []
                for i in steps:
                    theirs_i = [
                        arrived[span((j ^ m[1]) * 2 + 1 - i, cap), :] for j in range(n_dst)
                    ]
                    theirs_i = jnp.concatenate(theirs_i, axis=0).astype(F32)
                    mine_i = mine_ref[span(here(m, x, i) & 1, sb), :].astype(F32)
                    symmetric.append((mine_i + theirs_i).astype(BF16))
                symmetric = jnp.concatenate(symmetric, axis=0)
                inner = silu(dot(symmetric, w_ref[level, 1])).astype(BF16)
                out = symmetric.astype(F32) + dot(inner, w_ref[level, 2])
                out = out.astype(BF16)
                targets = []
                for k, i in enumerate(steps):
                    out_ref[span(here(m, x, i), sb), :] = out[k * sb : (k + 1) * sb]
                    targets.append(dst_ref[here(m, x, i)])
                atoms = lax.broadcasted_iota(jnp.int32, (dst_rows, len(steps) * sb), 0)
                onehot = jnp.where(atoms == jnp.concatenate(targets, axis=1), 1.0, 0.0)
                total[...] += dot(onehot.astype(BF16), out)
            sum_refs[0][...] = total[...].astype(sum_refs[0].dtype)

        args = (dst_row, edge_w, mine, *theirs)
        aliases = {}
        if not first:
            aliases = {1 + len(args): 0}
            args = (*args, refined, sums)
        out = call(
            kernel,
            (meta,),
            args,
            [array((rows, width)), array((dst_rows, width), BF16 if last else F32)],
            [pltpu.VMEM((2 * sb, width), BF16), pltpu.VMEM((dst_rows, width), F32)],
            4 * sb * width * (2 * width + dst_rows),
            6 * 2**20,
            aliases,
        )
        return out[0], out[1]

    def update_call(level, state, refined, pieces):
        last = level == NBLK - 1

        def kernel(cnt_ref, m, src_ref, state_ref, refined_ref, w_ref, down_ref, *refs):
            piece_refs, refs = refs[: len(pieces)], refs[len(pieces) :]
            out_ref, refs = refs[0], refs[1:]
            region = refs[1] if not last else refs[0]
            filled = 0
            for piece_ref in piece_refs:
                region[filled : filled + piece_ref.shape[0], :] = piece_ref[...]
                filled += piece_ref.shape[0]
            many = 2 if last else 1
            size = many * sb
            lines = lax.broadcasted_iota(jnp.int32, (region_rows, size), 0)

            @pl.loop(0, n_src // many)
            def _(i):
                atom = jnp.concatenate([src_ref[i * many + k] for k in range(many)], axis=1)
                where = (atom // dst_rows ^ m[1] % ratio) * dst_rows + atom % dst_rows
                pick = jnp.where(lines == where, 1.0, 0.0).astype(BF16)
                at = span(i, size)
                refined_v = refined_ref[at, :].astype(F32)
                joined = (refined_v + dot_first(pick, region[...])).astype(BF16)
                one = silu(dot(joined, w_ref[level, 3])).astype(BF16)
                two = silu(dot(one, w_ref[level, 4])).astype(BF16)
                counts_i = []
                for k in range(many):
                    counts_i += counts_at(cnt_ref, i * many + k)
                new = state_ref[at, :].astype(F32) + refined_v + dot(two, w_ref[level, 5])
                new = masked(new * (0.5**0.5), cap, counts_i).astype(BF16)
                if last:
                    refs[1][at, :] = new
                    pltpu.make_async_copy(refs[1].at[at], out_ref.at[at], refs[2].at[i]).start()
                else:
                    out_ref[at, :] = new
                    low = masked(silu(dot_last(new, down_ref[level + 1])), cap, counts_i)
                    refs[0][span(i, half), :] = pack(low.astype(BF16))

            if last:
                for i in range(n_src // many):
                    at = slice(i * size, (i + 1) * size)
                    pltpu.make_async_copy(refs[1].at[at], out_ref.at[at], refs[2].at[i]).wait()

        scratch = [pltpu.VMEM((region_rows, width), BF16)]
        if last:
            out_shape, out_specs = [array((rows, width))], [ANY]
            scratch += [pltpu.VMEM((rows, width), BF16), pltpu.SemaphoreType.DMA((n_src,))]
        else:
            out_shape, out_specs = [array((rows, width)), array((prows, 2 * trip))], None
        return call(
            kernel,
            (cnt, meta),
            (src_row, state, refined, edge_w, down_t, *pieces),
            out_shape,
            scratch,
            2 * rows * width * (3 * width + region_rows + trip),
            8 * 2**20,
            None,
            out_specs,
        )

    def exchange_order():
        mid = n_dst // 2
        over = [(k + 1.5 * x, x, j) for x in range(groups) for k, j in enumerate(range(mid, n_dst))]
        near = [
            (k + 1.5 * x, x, j)
            for x in range(groups)
            for k, j in enumerate(range(mid - 1, -1, -1))
            if (x, j) != (0, 0)
        ]
        order = []
        for k, (_, x, j) in enumerate(sorted(over)):
            order.append((x, j))
            if k < len(near):
                order.append(sorted(near)[k][1:])
        return order

    def exchange(level, state, pool, window):
        mine, joined, arrived = [], [], [[None] * n_dst for _ in range(groups)]
        sent = []

        def prepare(x):
            own, give, keep = message_call(level, x, state, pool)
            mine.append(own)
            joined.append(join_call(keep, lax.ppermute(give, "src", src_perm(1))))

        prepare(0)
        arrived[0][0] = joined[0][0]
        for x, j in exchange_order():
            while len(joined) <= x:
                prepare(len(joined))
            operand, offset = joined[x][j], 2 * x * n_dst + j
            if len(sent) >= window:
                operand, _ = lax.optimization_barrier((operand, sent[-window]))
            sent.append(lax.ppermute(operand, both, [(a, a ^ offset) for a in range(n)]))
            arrived[x][j] = sent[-1]
        return mine, arrived

    def atoms_of(sums):
        other = lax.ppermute(sums, "src", src_perm(1))
        sums = (sums.astype(F32) + other.astype(F32)).astype(BF16)
        total = sums.astype(F32)
        for i in range(2, n_src, 2):
            total = total + lax.ppermute(sums, "src", src_perm(i)).astype(F32)
        return (total * DEGREE ** (-0.5)).astype(BF16)

    def to_sources(atoms):
        slots = []
        for r in range(ratio):
            perm = []
            for a in range(n):
                v, u, j = a // n_dst, a % n_dst // ratio, a % ratio
                perm.append((a, u * n_dst + v * ratio + (j ^ r)))
            slots.append(lax.ppermute(atoms, both, perm))
        return slots

    state = edge_state
    for level in range(NBLK):
        pool = gather_src(lowered, tiles if level == 0 else None)
        mine, theirs = exchange(level, state, pool, 5)
        refined, sums = None, None
        for x in range(groups):
            refined, sums = refine_call(level, x, mine[x], theirs[x], refined, sums)
        region = to_sources(atoms_of(sums))
        out = update_call(level, state, refined, region)
        state = out[0]
        if level < NBLK - 1:
            lowered = out[1]
    return state


def solution(mesh):
    placed = (
        P(("src", "dst"), None),
        P(None, ("src", "dst")),
        P(("src", "dst")),
        P(("src", "dst")),
        P(("src", "dst")),
        P(("src", "dst"), None),
        P(("src", "dst"), None),
        P(),
        P(),
        P(),
    )
    return jax.shard_map(
        body, mesh=mesh, in_specs=placed, out_specs=P(("src", "dst"), None), check_vma=False
    )
```

```python
import functools

import jax
import jax.numpy as jnp
from jax import lax
from jax.experimental import pallas as pl
from jax.experimental.pallas import tpu as pltpu
from jax.sharding import PartitionSpec as P

BLK = 128
PAIRS = 4
NBLK = 2
NSPH = 4
ATOM_DEV = 32
DEGREE = 64
VMEM_LIMIT = 20 * 1024 * 1024

F32 = jnp.float32
BF16 = jnp.bfloat16


def silu(value):
    half = 0.5 * value
    return half + half * jnp.tanh(half)


def dot(a, b):
    return jnp.dot(a, b, preferred_element_type=F32)


def dot_last(a, b):
    return lax.dot_general(a, b, (((1,), (1,)), ((), ())), preferred_element_type=F32)


def dot_first(a, b):
    return lax.dot_general(a, b, (((0,), (0,)), ((), ())), preferred_element_type=F32)


def legendre(cosine):
    square = cosine * cosine
    return [
        cosine,
        1.5 * square - 0.5,
        (2.5 * square - 1.5) * cosine,
        (4.375 * square - 3.75) * square + 0.375,
    ]


def masked(value, cap, counts):
    position = lax.broadcasted_iota(jnp.int32, (cap, value.shape[1]), 0)
    parts = [
        jnp.where(position < count, value[i * cap : (i + 1) * cap], 0.0)
        for i, count in enumerate(counts)
    ]
    return jnp.concatenate(parts, axis=0)


def pack(low):
    half = low.shape[0] // 2
    return jnp.concatenate([low[:half], low[half:]], axis=1)


SMEM = pl.BlockSpec(memory_space=pltpu.SMEM)
VMEM = pl.BlockSpec(memory_space=pltpu.VMEM)
ANY = pl.BlockSpec(memory_space=pl.ANY)


def call(
    kernel, scalars, args, out_shape, scratch=(), flops=0, nbytes=0, aliases=None, out_specs=None,
    in_specs=None,
):
    several = isinstance(out_shape, list)
    return pl.pallas_call(
        kernel,
        in_specs=[SMEM] * len(scalars) + (in_specs or [VMEM] * len(args)),
        out_specs=out_specs or ([VMEM] * len(out_shape) if several else VMEM),
        out_shape=out_shape,
        scratch_shapes=list(scratch),
        input_output_aliases=aliases or {},
        compiler_params=pltpu.CompilerParams(vmem_limit_bytes=VMEM_LIMIT),
        cost_estimate=pl.CostEstimate(flops=flops, bytes_accessed=nbytes, transcendentals=0),
    )(*scalars, *args)


def array(shape, kind=BF16):
    return jax.ShapeDtypeStruct(shape, kind)


def span(start, size):
    return pl.ds(pl.multiple_of(start * size, size), size)


def body(
    edge_state, directions, src_atom, dst_atom, rev_pos, counts, triplets, down_w, trip_w, edge_w
):
    n_src = lax.axis_size("src")
    n_dst = lax.axis_size("dst")
    n = n_src * n_dst
    rows, width = edge_state.shape
    trip = down_w.shape[2]
    cap = rows // n
    sb = rows // n_src
    spb = sb // BLK
    half = sb // 2
    chunk = min(sb, 256)
    groups = n_src // 2
    nblock = rows // BLK
    ratio = n_dst // n_src
    dst_rows = ATOM_DEV * n_src
    region_rows = ratio * dst_rows
    prows = rows // 2
    both = ("src", "dst")
    chunks = range(sb // chunk)
    per = chunk // cap

    s = lax.axis_index("src")
    d = lax.axis_index("dst")

    cnt = counts.reshape(-1)
    flat = triplets.T.reshape(-1)
    block = flat % nblock
    rel = (flat // nblock) ^ s
    pool_row = rel * prows + block // spb * half + block % (spb // 2) * BLK
    pool_half = (block % spb) // (spb // 2)
    meta = jnp.concatenate([jnp.stack([s, d]), pool_row, pool_half, rel * nblock + block]).astype(jnp.int32)
    at_row = 2
    at_half = at_row + nblock * PAIRS
    at_block = at_half + nblock * PAIRS
    down_t = jnp.swapaxes(down_w, 1, 2)

    def counts_at(cnt_ref, block, h=None):
        first = block * n_dst + (0 if h is None else h * per)
        return [cnt_ref[first + i] for i in range(n_dst if h is None else per)]

    def split(value):
        return [value[h * chunk : (h + 1) * chunk] for h in chunks]

    def lower_kernel(cnt_ref, state_hbm, down_hbm, out_ref, state_ref, down_ref, sems):
        down = pltpu.make_async_copy(down_hbm.at[0], down_ref, sems.at[n_src])
        down.start()
        parts = [
            pltpu.make_async_copy(
                state_hbm.at[pl.ds(i * sb, sb)], state_ref.at[pl.ds(i * sb, sb)], sems.at[i]
            )
            for i in range(n_src)
        ]
        for part in parts:
            part.start()
        down.wait()
        for i, part in enumerate(parts):
            part.wait()
            low = silu(dot_last(state_ref[i * sb : (i + 1) * sb, :], down_ref[...]))
            low = masked(low, cap, counts_at(cnt_ref, i)).astype(BF16)
            out_ref[i * half : (i + 1) * half, :] = pack(low)

    lowered = call(
        lower_kernel,
        (cnt,),
        (edge_state, down_t),
        array((prows, 2 * trip)),
        [
            pltpu.VMEM((rows, width), BF16),
            pltpu.VMEM((trip, width), BF16),
            pltpu.SemaphoreType.DMA((n_src + 1,)),
        ],
        2 * rows * width * trip,
        rows * width * 2,
        in_specs=[ANY] * 2,
    )

    def project(level, index, x):
        def kernel(x_ref, w_ref, out_ref):
            @pl.loop(0, n_src)
            def _(i):
                out_ref[span(i, sb), :] = dot(x_ref[span(i, sb), :], w_ref[level, index])

        return call(
            kernel, (), (x, edge_w), array((rows, width), F32), (),
            2 * rows * width * width, 6 * rows * width,
        )

    def src_perm(i):
        return [(a, a ^ i) for a in range(n_src)]

    def gather_src(x, before=None):
        slots = [None] * n_src
        slots[0] = x
        for i in range(2, n_src, 2):
            slots[i] = lax.ppermute(x, "src", src_perm(i))
        for i in range(0, n_src, 2):
            if i and before is not None:
                slots[i], _ = lax.optimization_barrier((slots[i], before))
            slots[i + 1] = lax.ppermute(slots[i], "src", src_perm(1))
        return slots

    dirs_pool = gather_src(directions)

    def tiles_kernel(m, *refs):
        own_ref, out_ref, pool_ref = refs[0], refs[n_src], refs[n_src + 1]
        for k in range(n_src):
            pool_ref[:, k * rows : (k + 1) * rows] = refs[k][...]

        @pl.loop(0, nblock)
        def _(c):
            own = own_ref[:, span(c, BLK)]
            col = jnp.concatenate([own, jnp.zeros((5, BLK), F32)], axis=0).T
            for q in range(PAIRS):
                chosen = pool_ref[:, span(m[at_block + q * nblock + c], BLK)]
                cosine = (
                    col[:, 0:1] * chosen[0:1]
                    + col[:, 1:2] * chosen[1:2]
                    + col[:, 2:3] * chosen[2:3]
                )
                for degree, tile in enumerate(legendre(cosine)):
                    out_ref[c, degree, :, q * BLK : (q + 1) * BLK] = tile.astype(BF16)

    tiles = call(
        tiles_kernel,
        (meta,),
        dirs_pool,
        array((nblock, NSPH, BLK, PAIRS * BLK)),
        [pltpu.VMEM((3, n_src * rows), F32)],
        nblock * BLK * PAIRS * BLK * 2000,
        nblock * NSPH * BLK * PAIRS * BLK * 2,
    )

    rev_row = rev_pos.reshape(n_src, 1, sb)
    dst_row = dst_atom.reshape(n_src, 1, sb)
    src_row = src_atom.reshape(n_src, 1, sb)
    tri_scale = (BLK * PAIRS) ** (-0.5)

    def here(m, x, i):
        return m[0] ^ (2 * x) ^ 1 ^ i

    def message_call(level, x, projected, pool):
        def kernel(cnt_ref, m, tiles_ref, projected_ref, up_ref, rev_ref, *refs):
            pool_refs, refs = refs[:n_src], refs[n_src:]
            mine_ref, give_ref, keep_ref, pool_all, hold = refs
            for k in range(n_src):
                pool_all[k * prows : (k + 1) * prows, :] = pool_refs[k][...]
            target_row = lax.broadcasted_iota(jnp.int32, (chunk, chunk), 0)
            base = lax.broadcasted_iota(jnp.int32, (1, chunk), 1) // cap * cap
            for i, out_ref in enumerate((give_ref, keep_ref)):
                at_src = here(m, x, i)
                triple = []
                for c in range(spb):
                    chosen = []
                    for q in range(PAIRS):
                        which = q * nblock + at_src * spb + c
                        v = pool_all[pl.ds(pl.multiple_of(m[at_row + which], BLK), BLK), :]
                        chosen.append(jnp.where(m[at_half + which] == 1, v[:, trip:], v[:, :trip]))
                    summed = dot(
                        tiles_ref[at_src * spb + c].reshape(NSPH * BLK, PAIRS * BLK),
                        jnp.concatenate(chosen, axis=0),
                    )
                    summed = (summed * tri_scale).astype(BF16)
                    triple.append(
                        jnp.concatenate(
                            [summed[l * BLK : (l + 1) * BLK] for l in range(NSPH)], axis=1
                        )
                    )
                triple = jnp.concatenate(triple, axis=0)
                size = chunk
                message = []
                for h in range(sb // size):
                    pre = projected_ref[span(at_src * (sb // size) + h, size), :]
                    pre = pre + dot(triple[h * size : (h + 1) * size], up_ref[level])
                    counts_h = counts_at(cnt_ref, at_src)[h * size // cap : (h + 1) * size // cap]
                    message.append(masked(silu(pre), cap, counts_h).astype(BF16))
                message = jnp.concatenate(message, axis=0)
                mine_ref[span(at_src & 1, sb), :] = message
                for h in chunks:
                    at = slice(h * chunk, (h + 1) * chunk)
                    pick = jnp.where(target_row == rev_ref[at_src, :, at] + base, 1.0, 0.0)
                    hold[at, :] = dot(pick.astype(BF16), message[at]).astype(BF16)
                for j in range(n_dst):
                    out_ref[j * cap : (j + 1) * cap, :] = hold[span(m[1] ^ j, cap), :]

        return call(
            kernel,
            (cnt, meta),
            (tiles, projected, trip_w, rev_row, *pool),
            [array((2 * sb, width)), array((sb, width)), array((sb, width))],
            [pltpu.VMEM((n_src * prows, 2 * trip), BF16), pltpu.VMEM((sb, width), BF16)],
            4 * sb * width * (width + 2 * NSPH * trip) + 4 * sb * NSPH * 512 * 256,
            9 * 2**20,
        )

    def join_call(keep, received):
        def kernel(keep_ref, received_ref, *out_refs):
            for j, out_ref in enumerate(out_refs):
                out_ref[:cap, :] = keep_ref[j * cap : (j + 1) * cap, :]
                out_ref[cap:, :] = received_ref[j * cap : (j + 1) * cap, :]

        return call(
            kernel,
            (),
            (keep, received),
            [array((2 * cap, width))] * n_dst,
            (),
            0,
            4 * sb * width * 2,
        )

    def refine_call(level, x, mine, theirs, refined, sums):
        first, last = x == 0, x == groups - 1

        def kernel(m, dst_ref, w_ref, mine_ref, *refs):
            their_refs, refs = refs[:n_dst], refs[n_dst:]
            if not first:
                sums_ref, refs = refs[1], refs[2:]
            out_ref, sum_refs, arrived, total = refs[0], refs[1:-2], refs[-2], refs[-1]
            for j in range(n_dst):
                arrived[2 * j * cap : 2 * (j + 1) * cap, :] = their_refs[j][...]
            total[...] = jnp.zeros_like(total) if first else sums_ref[...]
            for steps in ([(0,), (1,)] if first else [(0, 1)]):
                symmetric = []
                for i in steps:
                    theirs_i = [
                        arrived[span((j ^ m[1]) * 2 + 1 - i, cap), :] for j in range(n_dst)
                    ]
                    theirs_i = jnp.concatenate(theirs_i, axis=0).astype(F32)
                    mine_i = mine_ref[span(here(m, x, i) & 1, sb), :].astype(F32)
                    symmetric.append((mine_i + theirs_i).astype(BF16))
                symmetric = jnp.concatenate(symmetric, axis=0)
                inner = silu(dot(symmetric, w_ref[level, 1])).astype(BF16)
                out = symmetric.astype(F32) + dot(inner, w_ref[level, 2])
                out = out.astype(BF16)
                targets = []
                for k, i in enumerate(steps):
                    out_ref[span(here(m, x, i), sb), :] = out[k * sb : (k + 1) * sb]
                    targets.append(dst_ref[here(m, x, i)])
                atoms = lax.broadcasted_iota(jnp.int32, (dst_rows, len(steps) * sb), 0)
                onehot = jnp.where(atoms == jnp.concatenate(targets, axis=1), 1.0, 0.0)
                total[...] += dot(onehot.astype(BF16), out)
            sum_refs[0][...] = total[...].astype(sum_refs[0].dtype)

        args = (dst_row, edge_w, mine, *theirs)
        aliases = {}
        if not first:
            aliases = {1 + len(args): 0}
            args = (*args, refined, sums)
        out = call(
            kernel,
            (meta,),
            args,
            [array((rows, width)), array((dst_rows, width), BF16 if last else F32)],
            [pltpu.VMEM((2 * sb, width), BF16), pltpu.VMEM((dst_rows, width), F32)],
            4 * sb * width * (2 * width + dst_rows),
            6 * 2**20,
            aliases,
        )
        return out[0], out[1]

    def update_call(level, state, refined, projected, pieces):
        last = level == NBLK - 1

        def kernel(cnt_ref, m, src_ref, state_ref, refined_ref, projected_ref, w_ref, down_ref, *refs):
            piece_refs, refs = refs[: len(pieces)], refs[len(pieces) :]
            out_ref, refs = refs[0], refs[1:]
            region = refs[1] if not last else refs[0]
            filled = 0
            for piece_ref in piece_refs:
                fed = dot(piece_ref[...], w_ref[level, 3]).astype(BF16)
                region[filled : filled + piece_ref.shape[0], :] = fed
                filled += piece_ref.shape[0]
            many = 2 if last else 1
            size = many * sb
            lines = lax.broadcasted_iota(jnp.int32, (region_rows, size), 0)

            @pl.loop(0, n_src // many)
            def _(i):
                atom = jnp.concatenate([src_ref[i * many + k] for k in range(many)], axis=1)
                where = (atom // dst_rows ^ m[1] % ratio) * dst_rows + atom % dst_rows
                pick = jnp.where(lines == where, 1.0, 0.0).astype(BF16)
                at = span(i, size)
                refined_v = refined_ref[at, :].astype(F32)
                one = silu(projected_ref[at, :] + dot_first(pick, region[...])).astype(BF16)
                two = silu(dot(one, w_ref[level, 4])).astype(BF16)
                counts_i = []
                for k in range(many):
                    counts_i += counts_at(cnt_ref, i * many + k)
                new = state_ref[at, :].astype(F32) + refined_v + dot(two, w_ref[level, 5])
                new = masked(new * (0.5**0.5), cap, counts_i).astype(BF16)
                if last:
                    refs[1][at, :] = new
                    pltpu.make_async_copy(refs[1].at[at], out_ref.at[at], refs[2].at[i]).start()
                else:
                    out_ref[at, :] = new
                    low = masked(silu(dot_last(new, down_ref[level + 1])), cap, counts_i)
                    refs[0][span(i, half), :] = pack(low.astype(BF16))

            if last:
                for i in range(n_src // many):
                    at = slice(i * size, (i + 1) * size)
                    pltpu.make_async_copy(refs[1].at[at], out_ref.at[at], refs[2].at[i]).wait()

        scratch = [pltpu.VMEM((region_rows, width), BF16)]
        if last:
            out_shape, out_specs = [array((rows, width))], [ANY]
            scratch += [pltpu.VMEM((rows, width), BF16), pltpu.SemaphoreType.DMA((n_src,))]
        else:
            out_shape, out_specs = [array((rows, width)), array((prows, 2 * trip))], None
        return call(
            kernel,
            (cnt, meta),
            (src_row, state, refined, projected, edge_w, down_t, *pieces),
            out_shape,
            scratch,
            2 * rows * width * (3 * width + region_rows + trip),
            8 * 2**20,
            None,
            out_specs,
        )

    def exchange_order():
        mid = n_dst // 2
        over = [(k + 1.5 * x, x, j) for x in range(groups) for k, j in enumerate(range(mid, n_dst))]
        near = [
            (k + 1.5 * x, x, j)
            for x in range(groups)
            for k, j in enumerate(range(mid - 1, -1, -1))
            if (x, j) != (0, 0)
        ]
        order = []
        for k, (_, x, j) in enumerate(sorted(over)):
            order.append((x, j))
            if k < len(near):
                order.append(sorted(near)[k][1:])
        return order

    def exchange(level, projected, pool, window):
        mine, joined, arrived = [], [], [[None] * n_dst for _ in range(groups)]
        sent = []

        def prepare(x):
            own, give, keep = message_call(level, x, projected, pool)
            mine.append(own)
            joined.append(join_call(keep, lax.ppermute(give, "src", src_perm(1))))

        prepare(0)
        arrived[0][0] = joined[0][0]
        for x, j in exchange_order():
            while len(joined) <= x:
                prepare(len(joined))
            operand, offset = joined[x][j], 2 * x * n_dst + j
            if len(sent) >= window:
                operand, _ = lax.optimization_barrier((operand, sent[-window]))
            sent.append(lax.ppermute(operand, both, [(a, a ^ offset) for a in range(n)]))
            arrived[x][j] = sent[-1]
        return mine, arrived

    def atoms_of(sums):
        other = lax.ppermute(sums, "src", src_perm(1))
        sums = (sums.astype(F32) + other.astype(F32)).astype(BF16)
        total = sums.astype(F32)
        for i in range(2, n_src, 2):
            total = total + lax.ppermute(sums, "src", src_perm(i)).astype(F32)
        return (total * DEGREE ** (-0.5)).astype(BF16)

    def to_sources(atoms):
        perm = []
        for a in range(n):
            v, u, j = a // n_dst, a % n_dst // ratio, a % ratio
            perm.append((a, u * n_dst + v * ratio + j))
        first = lax.ppermute(atoms, both, perm)
        return [first] + [
            lax.ppermute(first, "dst", [(a, a ^ r) for a in range(n_dst)])
            for r in range(1, ratio)
        ]

    state = edge_state
    for level in range(NBLK):
        pool = gather_src(lowered, tiles if level == 0 else None)
        mine, theirs = exchange(level, project(level, 0, state), pool, 5)
        refined, sums = None, None
        for x in range(groups):
            refined, sums = refine_call(level, x, mine[x], theirs[x], refined, sums)
        region = to_sources(atoms_of(sums))
        out = update_call(level, state, refined, project(level, 3, refined), region)
        state = out[0]
        if level < NBLK - 1:
            lowered = out[1]
    return state


def solution(mesh):
    placed = (
        P(("src", "dst"), None),
        P(None, ("src", "dst")),
        P(("src", "dst")),
        P(("src", "dst")),
        P(("src", "dst")),
        P(("src", "dst"), None),
        P(("src", "dst"), None),
        P(),
        P(),
        P(),
    )
    return jax.shard_map(
        body, mesh=mesh, in_specs=placed, out_specs=P(("src", "dst"), None), check_vma=False
    )
```

```python
import functools

import jax
import jax.numpy as jnp
from jax import lax
from jax.experimental import pallas as pl
from jax.experimental.pallas import tpu as pltpu
from jax.sharding import PartitionSpec as P

BLK = 128
PAIRS = 4
NBLK = 2
NSPH = 4
ATOM_DEV = 32
DEGREE = 64
VMEM_LIMIT = 20 * 1024 * 1024

F32 = jnp.float32
BF16 = jnp.bfloat16


def silu(value):
    half = 0.5 * value
    return half + half * jnp.tanh(half)


def dot(a, b):
    return jnp.dot(a, b, preferred_element_type=F32)


def dot_last(a, b):
    return lax.dot_general(a, b, (((1,), (1,)), ((), ())), preferred_element_type=F32)


def dot_first(a, b):
    return lax.dot_general(a, b, (((0,), (0,)), ((), ())), preferred_element_type=F32)


def legendre(cosine):
    square = cosine * cosine
    return [
        cosine,
        1.5 * square - 0.5,
        (2.5 * square - 1.5) * cosine,
        (4.375 * square - 3.75) * square + 0.375,
    ]


def masked(value, cap, counts):
    position = lax.broadcasted_iota(jnp.int32, (cap, value.shape[1]), 0)
    parts = [
        jnp.where(position < count, value[i * cap : (i + 1) * cap], 0.0)
        for i, count in enumerate(counts)
    ]
    return jnp.concatenate(parts, axis=0)


def pack(low):
    half = low.shape[0] // 2
    return jnp.concatenate([low[:half], low[half:]], axis=1)


SMEM = pl.BlockSpec(memory_space=pltpu.SMEM)
VMEM = pl.BlockSpec(memory_space=pltpu.VMEM)
ANY = pl.BlockSpec(memory_space=pl.ANY)


def call(kernel, scalars, args, out_shape, scratch=(), flops=0, nbytes=0, aliases=None, out_specs=None):
    several = isinstance(out_shape, list)
    return pl.pallas_call(
        kernel,
        in_specs=[SMEM] * len(scalars) + [VMEM] * len(args),
        out_specs=out_specs or ([VMEM] * len(out_shape) if several else VMEM),
        out_shape=out_shape,
        scratch_shapes=list(scratch),
        input_output_aliases=aliases or {},
        compiler_params=pltpu.CompilerParams(vmem_limit_bytes=VMEM_LIMIT),
        cost_estimate=pl.CostEstimate(flops=flops, bytes_accessed=nbytes, transcendentals=0),
    )(*scalars, *args)


def array(shape, kind=BF16):
    return jax.ShapeDtypeStruct(shape, kind)


def span(start, size):
    return pl.ds(pl.multiple_of(start * size, size), size)


def body(
    edge_state, directions, src_atom, dst_atom, rev_pos, counts, triplets, down_w, trip_w, edge_w
):
    n_src = lax.axis_size("src")
    n_dst = lax.axis_size("dst")
    n = n_src * n_dst
    rows, width = edge_state.shape
    trip = down_w.shape[2]
    cap = rows // n
    sb = rows // n_src
    spb = sb // BLK
    half = sb // 2
    chunk = min(sb, 256)
    groups = n_src // 2
    nblock = rows // BLK
    ratio = n_dst // n_src
    dst_rows = ATOM_DEV * n_src
    region_rows = ratio * dst_rows
    prows = rows // 2
    both = ("src", "dst")
    chunks = range(sb // chunk)
    per = chunk // cap

    s = lax.axis_index("src")
    d = lax.axis_index("dst")

    cnt = counts.reshape(-1)
    flat = triplets.T.reshape(-1)
    block = flat % nblock
    rel = (flat // nblock) ^ s
    pool_row = rel * prows + block // spb * half + block % (spb // 2) * BLK
    pool_half = (block % spb) // (spb // 2)
    meta = jnp.concatenate([jnp.stack([s, d]), pool_row, pool_half, rel * nblock + block]).astype(jnp.int32)
    at_row = 2
    at_half = at_row + nblock * PAIRS
    at_block = at_half + nblock * PAIRS
    down_t = jnp.swapaxes(down_w, 1, 2)

    def counts_at(cnt_ref, block, h=None):
        first = block * n_dst + (0 if h is None else h * per)
        return [cnt_ref[first + i] for i in range(n_dst if h is None else per)]

    def split(value):
        return [value[h * chunk : (h + 1) * chunk] for h in chunks]

    def lower_kernel(cnt_ref, state_ref, down_ref, out_ref):
        @pl.loop(0, n_src)
        def _(i):
            low = silu(dot_last(state_ref[span(i, sb), :], down_ref[0]))
            out_ref[span(i, half), :] = pack(masked(low, cap, counts_at(cnt_ref, i)).astype(BF16))

    lowered = call(
        lower_kernel,
        (cnt,),
        (edge_state, down_t),
        array((prows, 2 * trip)),
        (),
        2 * rows * width * trip,
        rows * width * 2,
    )

    def project(level, index, x):
        def kernel(x_ref, w_ref, out_ref):
            @pl.loop(0, n_src)
            def _(i):
                out_ref[span(i, sb), :] = dot(x_ref[span(i, sb), :], w_ref[level, index])

        return call(
            kernel, (), (x, edge_w), array((rows, width), F32), (),
            2 * rows * width * width, 6 * rows * width,
        )

    def src_perm(i):
        return [(a, a ^ i) for a in range(n_src)]

    def gather_src(x, before=None):
        slots = [None] * n_src
        slots[0] = x
        for i in range(2, n_src, 2):
            slots[i] = lax.ppermute(x, "src", src_perm(i))
        for i in range(0, n_src, 2):
            if i and before is not None:
                slots[i], _ = lax.optimization_barrier((slots[i], before))
            slots[i + 1] = lax.ppermute(slots[i], "src", src_perm(1))
        return slots

    dirs_pool = gather_src(directions)

    def tiles_kernel(m, *refs):
        own_ref, out_ref, pool_ref = refs[0], refs[n_src], refs[n_src + 1]
        for k in range(n_src):
            pool_ref[:, k * rows : (k + 1) * rows] = refs[k][...]

        @pl.loop(0, nblock)
        def _(c):
            own = own_ref[:, span(c, BLK)]
            col = jnp.concatenate([own, jnp.zeros((5, BLK), F32)], axis=0).T
            for q in range(PAIRS):
                chosen = pool_ref[:, span(m[at_block + q * nblock + c], BLK)]
                cosine = (
                    col[:, 0:1] * chosen[0:1]
                    + col[:, 1:2] * chosen[1:2]
                    + col[:, 2:3] * chosen[2:3]
                )
                for degree, tile in enumerate(legendre(cosine)):
                    out_ref[c, degree, :, q * BLK : (q + 1) * BLK] = tile.astype(BF16)

    tiles = call(
        tiles_kernel,
        (meta,),
        dirs_pool,
        array((nblock, NSPH, BLK, PAIRS * BLK)),
        [pltpu.VMEM((3, n_src * rows), F32)],
        nblock * BLK * PAIRS * BLK * 2000,
        nblock * NSPH * BLK * PAIRS * BLK * 2,
    )

    rev_row = rev_pos.reshape(n_src, 1, sb)
    dst_row = dst_atom.reshape(n_src, 1, sb)
    src_row = src_atom.reshape(n_src, 1, sb)
    tri_scale = (BLK * PAIRS) ** (-0.5)

    def here(m, x, i):
        return m[0] ^ (2 * x) ^ 1 ^ i

    def message_call(level, x, state, pool):
        def kernel(cnt_ref, m, tiles_ref, state_ref, w_ref, up_ref, rev_ref, *refs):
            pool_refs, refs = refs[:n_src], refs[n_src:]
            mine_ref, give_ref, keep_ref, pool_all, hold = refs
            for k in range(n_src):
                pool_all[k * prows : (k + 1) * prows, :] = pool_refs[k][...]
            target_row = lax.broadcasted_iota(jnp.int32, (chunk, chunk), 0)
            base = lax.broadcasted_iota(jnp.int32, (1, chunk), 1) // cap * cap
            for i, out_ref in enumerate((give_ref, keep_ref)):
                at_src = here(m, x, i)
                triple = []
                for c in range(spb):
                    chosen = []
                    for q in range(PAIRS):
                        which = q * nblock + at_src * spb + c
                        v = pool_all[pl.ds(pl.multiple_of(m[at_row + which], BLK), BLK), :]
                        chosen.append(jnp.where(m[at_half + which] == 1, v[:, trip:], v[:, :trip]))
                    summed = dot(
                        tiles_ref[at_src * spb + c].reshape(NSPH * BLK, PAIRS * BLK),
                        jnp.concatenate(chosen, axis=0),
                    )
                    summed = (summed * tri_scale).astype(BF16)
                    triple.append(
                        jnp.concatenate(
                            [summed[l * BLK : (l + 1) * BLK] for l in range(NSPH)], axis=1
                        )
                    )
                triple = jnp.concatenate(triple, axis=0)
                size = chunk
                message = []
                for h in range(sb // size):
                    pre = dot(state_ref[span(at_src * (sb // size) + h, size), :], w_ref[level, 0])
                    pre = pre + dot(triple[h * size : (h + 1) * size], up_ref[level])
                    counts_h = counts_at(cnt_ref, at_src)[h * size // cap : (h + 1) * size // cap]
                    message.append(masked(silu(pre), cap, counts_h).astype(BF16))
                message = jnp.concatenate(message, axis=0)
                mine_ref[span(at_src & 1, sb), :] = message
                for h in chunks:
                    at = slice(h * chunk, (h + 1) * chunk)
                    pick = jnp.where(target_row == rev_ref[at_src, :, at] + base, 1.0, 0.0)
                    hold[at, :] = dot(pick.astype(BF16), message[at]).astype(BF16)
                for j in range(n_dst):
                    out_ref[j * cap : (j + 1) * cap, :] = hold[span(m[1] ^ j, cap), :]

        return call(
            kernel,
            (cnt, meta),
            (tiles, state, edge_w, trip_w, rev_row, *pool),
            [array((2 * sb, width)), array((sb, width)), array((sb, width))],
            [pltpu.VMEM((n_src * prows, 2 * trip), BF16), pltpu.VMEM((sb, width), BF16)],
            4 * sb * width * (width + 2 * NSPH * trip) + 4 * sb * NSPH * 512 * 256,
            9 * 2**20,
        )

    def join_call(keep, received):
        def kernel(keep_ref, received_ref, *out_refs):
            for j, out_ref in enumerate(out_refs):
                out_ref[:cap, :] = keep_ref[j * cap : (j + 1) * cap, :]
                out_ref[cap:, :] = received_ref[j * cap : (j + 1) * cap, :]

        return call(
            kernel,
            (),
            (keep, received),
            [array((2 * cap, width))] * n_dst,
            (),
            0,
            4 * sb * width * 2,
        )

    def refine_call(level, x, mine, theirs, refined, sums):
        first, last = x == 0, x == groups - 1

        def kernel(m, dst_ref, w_ref, mine_ref, *refs):
            their_refs, refs = refs[:n_dst], refs[n_dst:]
            if not first:
                sums_ref, refs = refs[1], refs[2:]
            out_ref, sum_refs, arrived, total = refs[0], refs[1:-2], refs[-2], refs[-1]
            for j in range(n_dst):
                arrived[2 * j * cap : 2 * (j + 1) * cap, :] = their_refs[j][...]
            total[...] = jnp.zeros_like(total) if first else sums_ref[...]
            for steps in ([(0,), (1,)] if first else [(0, 1)]):
                symmetric = []
                for i in steps:
                    theirs_i = [
                        arrived[span((j ^ m[1]) * 2 + 1 - i, cap), :] for j in range(n_dst)
                    ]
                    theirs_i = jnp.concatenate(theirs_i, axis=0).astype(F32)
                    mine_i = mine_ref[span(here(m, x, i) & 1, sb), :].astype(F32)
                    symmetric.append((mine_i + theirs_i).astype(BF16))
                symmetric = jnp.concatenate(symmetric, axis=0)
                inner = silu(dot(symmetric, w_ref[level, 1])).astype(BF16)
                out = symmetric.astype(F32) + dot(inner, w_ref[level, 2])
                out = out.astype(BF16)
                targets = []
                for k, i in enumerate(steps):
                    out_ref[span(here(m, x, i), sb), :] = out[k * sb : (k + 1) * sb]
                    targets.append(dst_ref[here(m, x, i)])
                atoms = lax.broadcasted_iota(jnp.int32, (dst_rows, len(steps) * sb), 0)
                onehot = jnp.where(atoms == jnp.concatenate(targets, axis=1), 1.0, 0.0)
                total[...] += dot(onehot.astype(BF16), out)
            sum_refs[0][...] = total[...].astype(sum_refs[0].dtype)

        args = (dst_row, edge_w, mine, *theirs)
        aliases = {}
        if not first:
            aliases = {1 + len(args): 0}
            args = (*args, refined, sums)
        out = call(
            kernel,
            (meta,),
            args,
            [array((rows, width)), array((dst_rows, width), BF16 if last else F32)],
            [pltpu.VMEM((2 * sb, width), BF16), pltpu.VMEM((dst_rows, width), F32)],
            4 * sb * width * (2 * width + dst_rows),
            6 * 2**20,
            aliases,
        )
        return out[0], out[1]

    def update_call(level, state, refined, projected, pieces):
        last = level == NBLK - 1

        def kernel(cnt_ref, m, src_ref, state_ref, refined_ref, projected_ref, w_ref, down_ref, *refs):
            piece_refs, refs = refs[: len(pieces)], refs[len(pieces) :]
            out_ref, refs = refs[0], refs[1:]
            region = refs[1] if not last else refs[0]
            filled = 0
            for piece_ref in piece_refs:
                fed = dot(piece_ref[...], w_ref[level, 3]).astype(BF16)
                region[filled : filled + piece_ref.shape[0], :] = fed
                filled += piece_ref.shape[0]
            many = 2 if last else 1
            size = many * sb
            lines = lax.broadcasted_iota(jnp.int32, (region_rows, size), 0)

            @pl.loop(0, n_src // many)
            def _(i):
                atom = jnp.concatenate([src_ref[i * many + k] for k in range(many)], axis=1)
                where = (atom // dst_rows ^ m[1] % ratio) * dst_rows + atom % dst_rows
                pick = jnp.where(lines == where, 1.0, 0.0).astype(BF16)
                at = span(i, size)
                refined_v = refined_ref[at, :].astype(F32)
                one = silu(projected_ref[at, :] + dot_first(pick, region[...])).astype(BF16)
                two = silu(dot(one, w_ref[level, 4])).astype(BF16)
                counts_i = []
                for k in range(many):
                    counts_i += counts_at(cnt_ref, i * many + k)
                new = state_ref[at, :].astype(F32) + refined_v + dot(two, w_ref[level, 5])
                new = masked(new * (0.5**0.5), cap, counts_i).astype(BF16)
                if last:
                    refs[1][at, :] = new
                    pltpu.make_async_copy(refs[1].at[at], out_ref.at[at], refs[2].at[i]).start()
                else:
                    out_ref[at, :] = new
                    low = masked(silu(dot_last(new, down_ref[level + 1])), cap, counts_i)
                    refs[0][span(i, half), :] = pack(low.astype(BF16))

            if last:
                for i in range(n_src // many):
                    at = slice(i * size, (i + 1) * size)
                    pltpu.make_async_copy(refs[1].at[at], out_ref.at[at], refs[2].at[i]).wait()

        scratch = [pltpu.VMEM((region_rows, width), BF16)]
        if last:
            out_shape, out_specs = [array((rows, width))], [ANY]
            scratch += [pltpu.VMEM((rows, width), BF16), pltpu.SemaphoreType.DMA((n_src,))]
        else:
            out_shape, out_specs = [array((rows, width)), array((prows, 2 * trip))], None
        return call(
            kernel,
            (cnt, meta),
            (src_row, state, refined, projected, edge_w, down_t, *pieces),
            out_shape,
            scratch,
            2 * rows * width * (3 * width + region_rows + trip),
            8 * 2**20,
            None,
            out_specs,
        )

    def exchange_order():
        mid = n_dst // 2
        over = [(k + 1.5 * x, x, j) for x in range(groups) for k, j in enumerate(range(mid, n_dst))]
        near = [
            (k + 1.5 * x, x, j)
            for x in range(groups)
            for k, j in enumerate(range(mid - 1, -1, -1))
            if (x, j) != (0, 0)
        ]
        order = []
        for k, (_, x, j) in enumerate(sorted(over)):
            order.append((x, j))
            if k < len(near):
                order.append(sorted(near)[k][1:])
        return order

    def exchange(level, state, pool, window):
        mine, joined, arrived = [], [], [[None] * n_dst for _ in range(groups)]
        sent = []

        def prepare(x):
            own, give, keep = message_call(level, x, state, pool)
            mine.append(own)
            joined.append(join_call(keep, lax.ppermute(give, "src", src_perm(1))))

        prepare(0)
        arrived[0][0] = joined[0][0]
        for x, j in exchange_order():
            while len(joined) <= x:
                prepare(len(joined))
            operand, offset = joined[x][j], 2 * x * n_dst + j
            if len(sent) >= window:
                operand, _ = lax.optimization_barrier((operand, sent[-window]))
            sent.append(lax.ppermute(operand, both, [(a, a ^ offset) for a in range(n)]))
            arrived[x][j] = sent[-1]
        return mine, arrived

    def atoms_of(sums):
        other = lax.ppermute(sums, "src", src_perm(1))
        sums = (sums.astype(F32) + other.astype(F32)).astype(BF16)
        total = sums.astype(F32)
        for i in range(2, n_src, 2):
            total = total + lax.ppermute(sums, "src", src_perm(i)).astype(F32)
        return (total * DEGREE ** (-0.5)).astype(BF16)

    def to_sources(atoms):
        slots = []
        for r in range(ratio):
            perm = []
            for a in range(n):
                t, u, j = a // n_dst, a % n_dst // ratio, a % ratio
                v = t % groups * 2 + t // groups
                perm.append((a, u * n_dst + v * ratio + (j ^ r)))
            slots.append(lax.ppermute(atoms, both, perm))
        return slots

    state = edge_state
    for level in range(NBLK):
        pool = gather_src(lowered, tiles if level == 0 else None)
        mine, theirs = exchange(level, state, pool, 5)
        refined, sums = None, None
        for x in range(groups):
            refined, sums = refine_call(level, x, mine[x], theirs[x], refined, sums)
        region = to_sources(atoms_of(sums))
        out = update_call(level, state, refined, project(level, 3, refined), region)
        state = out[0]
        if level < NBLK - 1:
            lowered = out[1]
    return state


def solution(mesh):
    placed = (
        P(("src", "dst"), None),
        P(None, ("src", "dst")),
        P(("src", "dst")),
        P(("src", "dst")),
        P(("src", "dst")),
        P(("src", "dst"), None),
        P(("src", "dst"), None),
        P(),
        P(),
        P(),
    )
    return jax.shard_map(
        body, mesh=mesh, in_specs=placed, out_specs=P(("src", "dst"), None), check_vma=False
    )
```

```python
import functools

import jax
import jax.numpy as jnp
from jax import lax
from jax.experimental import pallas as pl
from jax.experimental.pallas import tpu as pltpu
from jax.sharding import PartitionSpec as P

BLK = 128
PAIRS = 4
NBLK = 2
NSPH = 4
ATOM_DEV = 32
DEGREE = 64
VMEM_LIMIT = 20 * 1024 * 1024

F32 = jnp.float32
BF16 = jnp.bfloat16


def silu(value):
    half = 0.5 * value
    return half + half * jnp.tanh(half)


def dot(a, b):
    return jnp.dot(a, b, preferred_element_type=F32)


def dot_last(a, b):
    return lax.dot_general(a, b, (((1,), (1,)), ((), ())), preferred_element_type=F32)


def dot_first(a, b):
    return lax.dot_general(a, b, (((0,), (0,)), ((), ())), preferred_element_type=F32)


def legendre(cosine):
    square = cosine * cosine
    return [
        cosine,
        1.5 * square - 0.5,
        (2.5 * square - 1.5) * cosine,
        (4.375 * square - 3.75) * square + 0.375,
    ]


def masked(value, cap, counts):
    position = lax.broadcasted_iota(jnp.int32, (cap, value.shape[1]), 0)
    parts = [
        jnp.where(position < count, value[i * cap : (i + 1) * cap], 0.0)
        for i, count in enumerate(counts)
    ]
    return jnp.concatenate(parts, axis=0)


def pack(low):
    half = low.shape[0] // 2
    return jnp.concatenate([low[:half], low[half:]], axis=1)


SMEM = pl.BlockSpec(memory_space=pltpu.SMEM)
VMEM = pl.BlockSpec(memory_space=pltpu.VMEM)
ANY = pl.BlockSpec(memory_space=pl.ANY)


def call(kernel, scalars, args, out_shape, scratch=(), flops=0, nbytes=0, aliases=None, out_specs=None):
    several = isinstance(out_shape, list)
    return pl.pallas_call(
        kernel,
        in_specs=[SMEM] * len(scalars) + [VMEM] * len(args),
        out_specs=out_specs or ([VMEM] * len(out_shape) if several else VMEM),
        out_shape=out_shape,
        scratch_shapes=list(scratch),
        input_output_aliases=aliases or {},
        compiler_params=pltpu.CompilerParams(vmem_limit_bytes=VMEM_LIMIT),
        cost_estimate=pl.CostEstimate(flops=flops, bytes_accessed=nbytes, transcendentals=0),
    )(*scalars, *args)


def array(shape, kind=BF16):
    return jax.ShapeDtypeStruct(shape, kind)


def span(start, size):
    return pl.ds(pl.multiple_of(start * size, size), size)


def body(
    edge_state, directions, src_atom, dst_atom, rev_pos, counts, triplets, down_w, trip_w, edge_w
):
    n_src = lax.axis_size("src")
    n_dst = lax.axis_size("dst")
    n = n_src * n_dst
    rows, width = edge_state.shape
    trip = down_w.shape[2]
    cap = rows // n
    sb = rows // n_src
    spb = sb // BLK
    half = sb // 2
    chunk = min(sb, 256)
    groups = n_src // 2
    nblock = rows // BLK
    ratio = n_dst // n_src
    dst_rows = ATOM_DEV * n_src
    region_rows = ratio * dst_rows
    prows = rows // 2
    both = ("src", "dst")
    chunks = range(sb // chunk)
    per = chunk // cap

    s = lax.axis_index("src")
    d = lax.axis_index("dst")

    cnt = counts.reshape(-1)
    flat = triplets.T.reshape(-1)
    block = flat % nblock
    rel = (flat // nblock) ^ s
    pool_row = rel * prows + block // spb * half + block % (spb // 2) * BLK
    pool_half = (block % spb) // (spb // 2)
    meta = jnp.concatenate([jnp.stack([s, d]), pool_row, pool_half, rel * nblock + block]).astype(jnp.int32)
    at_row = 2
    at_half = at_row + nblock * PAIRS
    at_block = at_half + nblock * PAIRS
    down_t = jnp.swapaxes(down_w, 1, 2)

    def counts_at(cnt_ref, block, h=None):
        first = block * n_dst + (0 if h is None else h * per)
        return [cnt_ref[first + i] for i in range(n_dst if h is None else per)]

    def split(value):
        return [value[h * chunk : (h + 1) * chunk] for h in chunks]

    def lower_kernel(cnt_ref, state_ref, down_ref, out_ref):
        @pl.loop(0, n_src)
        def _(i):
            low = silu(dot_last(state_ref[span(i, sb), :], down_ref[0]))
            out_ref[span(i, half), :] = pack(masked(low, cap, counts_at(cnt_ref, i)).astype(BF16))

    lowered = call(
        lower_kernel,
        (cnt,),
        (edge_state, down_t),
        array((prows, 2 * trip)),
        (),
        2 * rows * width * trip,
        rows * width * 2,
    )

    def project(level, index, x):
        def kernel(x_ref, w_ref, out_ref):
            @pl.loop(0, n_src)
            def _(i):
                out_ref[span(i, sb), :] = dot(x_ref[span(i, sb), :], w_ref[level, index])

        return call(
            kernel, (), (x, edge_w), array((rows, width), F32), (),
            2 * rows * width * width, 6 * rows * width,
        )

    def src_perm(i):
        return [(a, a ^ i) for a in range(n_src)]

    def gather_src(x, before=None):
        slots = [None] * n_src
        slots[0] = x
        for i in range(2, n_src, 2):
            slots[i] = lax.ppermute(x, "src", src_perm(i))
        for i in range(0, n_src, 2):
            if i and before is not None:
                slots[i], _ = lax.optimization_barrier((slots[i], before))
            slots[i + 1] = lax.ppermute(slots[i], "src", src_perm(1))
        return slots

    dirs_pool = gather_src(directions)

    def tiles_kernel(m, *refs):
        own_ref, out_ref, pool_ref = refs[0], refs[n_src], refs[n_src + 1]
        for k in range(n_src):
            pool_ref[:, k * rows : (k + 1) * rows] = refs[k][...]

        @pl.loop(0, nblock)
        def _(c):
            own = own_ref[:, span(c, BLK)]
            col = jnp.concatenate([own, jnp.zeros((5, BLK), F32)], axis=0).T
            for q in range(PAIRS):
                chosen = pool_ref[:, span(m[at_block + q * nblock + c], BLK)]
                cosine = (
                    col[:, 0:1] * chosen[0:1]
                    + col[:, 1:2] * chosen[1:2]
                    + col[:, 2:3] * chosen[2:3]
                )
                for degree, tile in enumerate(legendre(cosine)):
                    out_ref[c, degree, :, q * BLK : (q + 1) * BLK] = tile.astype(BF16)

    tiles = call(
        tiles_kernel,
        (meta,),
        dirs_pool,
        array((nblock, NSPH, BLK, PAIRS * BLK)),
        [pltpu.VMEM((3, n_src * rows), F32)],
        nblock * BLK * PAIRS * BLK * 2000,
        nblock * NSPH * BLK * PAIRS * BLK * 2,
    )

    rev_row = rev_pos.reshape(n_src, 1, sb)
    src_row = src_atom.reshape(n_src, 1, sb)
    tri_scale = (BLK * PAIRS) ** (-0.5)

    def here(m, x, i):
        return m[0] ^ (2 * x) ^ 1 ^ i

    def message_call(level, x, state, pool):
        def kernel(cnt_ref, m, tiles_ref, state_ref, w_ref, up_ref, rev_ref, *refs):
            pool_refs, refs = refs[:n_src], refs[n_src:]
            mine_ref, give_ref, keep_ref, pool_all, hold = refs
            for k in range(n_src):
                pool_all[k * prows : (k + 1) * prows, :] = pool_refs[k][...]
            target_row = lax.broadcasted_iota(jnp.int32, (chunk, chunk), 0)
            base = lax.broadcasted_iota(jnp.int32, (1, chunk), 1) // cap * cap
            for i, out_ref in enumerate((give_ref, keep_ref)):
                at_src = here(m, x, i)
                triple = []
                for c in range(spb):
                    chosen = []
                    for q in range(PAIRS):
                        which = q * nblock + at_src * spb + c
                        v = pool_all[pl.ds(pl.multiple_of(m[at_row + which], BLK), BLK), :]
                        chosen.append(jnp.where(m[at_half + which] == 1, v[:, trip:], v[:, :trip]))
                    summed = dot(
                        tiles_ref[at_src * spb + c].reshape(NSPH * BLK, PAIRS * BLK),
                        jnp.concatenate(chosen, axis=0),
                    )
                    summed = (summed * tri_scale).astype(BF16)
                    triple.append(
                        jnp.concatenate(
                            [summed[l * BLK : (l + 1) * BLK] for l in range(NSPH)], axis=1
                        )
                    )
                triple = jnp.concatenate(triple, axis=0)
                size = chunk
                message = []
                for h in range(sb // size):
                    pre = dot(state_ref[span(at_src * (sb // size) + h, size), :], w_ref[level, 0])
                    pre = pre + dot(triple[h * size : (h + 1) * size], up_ref[level])
                    counts_h = counts_at(cnt_ref, at_src)[h * size // cap : (h + 1) * size // cap]
                    message.append(masked(silu(pre), cap, counts_h).astype(BF16))
                message = jnp.concatenate(message, axis=0)
                mine_ref[span(at_src & 1, sb), :] = message
                for h in chunks:
                    at = slice(h * chunk, (h + 1) * chunk)
                    pick = jnp.where(target_row == rev_ref[at_src, :, at] + base, 1.0, 0.0)
                    hold[at, :] = dot(pick.astype(BF16), message[at]).astype(BF16)
                for j in range(n_dst):
                    out_ref[j * cap : (j + 1) * cap, :] = hold[span(m[1] ^ j, cap), :]

        return call(
            kernel,
            (cnt, meta),
            (tiles, state, edge_w, trip_w, rev_row, *pool),
            [array((2 * sb, width)), array((sb, width)), array((sb, width))],
            [pltpu.VMEM((n_src * prows, 2 * trip), BF16), pltpu.VMEM((sb, width), BF16)],
            4 * sb * width * (width + 2 * NSPH * trip) + 4 * sb * NSPH * 512 * 256,
            9 * 2**20,
        )

    def join_call(keep, received):
        def kernel(keep_ref, received_ref, *out_refs):
            for j, out_ref in enumerate(out_refs):
                out_ref[:cap, :] = keep_ref[j * cap : (j + 1) * cap, :]
                out_ref[cap:, :] = received_ref[j * cap : (j + 1) * cap, :]

        return call(
            kernel,
            (),
            (keep, received),
            [array((2 * cap, width))] * n_dst,
            (),
            0,
            4 * sb * width * 2,
        )

    x_id, j_id, c_id = jnp.meshgrid(
        jnp.arange(groups), jnp.arange(n_dst), jnp.arange(2), indexing="ij"
    )
    bucket = ((s ^ (2 * x_id + c_id)) * n_dst + (d ^ j_id)).reshape(-1)
    dst_rel = jnp.take(dst_atom.reshape(n, cap), bucket, axis=0).reshape(groups, 1, 2 * sb)

    def refine_call(level, x, js, mine, theirs, refined, sums, last):
        first = refined is None
        size = len(js) * 2 * cap

        def kernel(m, dst_ref, w_ref, mine_ref, *refs):
            their_refs, refs = refs[: len(js)], refs[len(js) :]
            if not first:
                sums_ref, refs = refs[1], refs[2:]
            out_ref, sum_ref = refs
            slots = [(here(m, x, 1 - c), m[1] ^ j) for j in js for c in range(2)]
            own = jnp.concatenate(
                [mine_ref[span((src & 1) * n_dst + dst, cap), :] for src, dst in slots], axis=0
            )
            other = jnp.concatenate([ref[...] for ref in their_refs], axis=0)
            symmetric = (own.astype(F32) + other.astype(F32)).astype(BF16)
            inner = silu(dot(symmetric, w_ref[level, 1])).astype(BF16)
            out = (symmetric.astype(F32) + dot(inner, w_ref[level, 2])).astype(BF16)
            for k, (src, dst) in enumerate(slots):
                out_ref[span(src * n_dst + dst, cap), :] = out[k * cap : (k + 1) * cap]
            targets = dst_ref[x, :, js[0] * 2 * cap : js[0] * 2 * cap + size]
            atoms = lax.broadcasted_iota(jnp.int32, (dst_rows, size), 0)
            total = dot(jnp.where(atoms == targets, 1.0, 0.0).astype(BF16), out)
            if not first:
                total = total + sums_ref[...]
            sum_ref[...] = total.astype(sum_ref.dtype)

        args = (dst_rel, edge_w, mine, *[theirs[j] for j in js])
        aliases = {}
        if not first:
            aliases = {1 + len(args): 0}
            args = (*args, refined, sums)
        return call(
            kernel,
            (meta,),
            args,
            [array((rows, width)), array((dst_rows, width), BF16 if last else F32)],
            (),
            2 * size * width * (2 * width + dst_rows),
            6 * size * width,
            aliases,
        )

    def update_call(level, state, refined, projected, pieces):
        last = level == NBLK - 1

        def kernel(cnt_ref, m, src_ref, state_ref, refined_ref, projected_ref, w_ref, down_ref, *refs):
            piece_refs, refs = refs[: len(pieces)], refs[len(pieces) :]
            out_ref, refs = refs[0], refs[1:]
            region = refs[1] if not last else refs[0]
            filled = 0
            for piece_ref in piece_refs:
                fed = dot(piece_ref[...], w_ref[level, 3]).astype(BF16)
                region[filled : filled + piece_ref.shape[0], :] = fed
                filled += piece_ref.shape[0]
            many = 2 if last else 1
            size = many * sb
            lines = lax.broadcasted_iota(jnp.int32, (region_rows, size), 0)

            @pl.loop(0, n_src // many)
            def _(i):
                atom = jnp.concatenate([src_ref[i * many + k] for k in range(many)], axis=1)
                where = (atom // dst_rows ^ m[1] % ratio) * dst_rows + atom % dst_rows
                pick = jnp.where(lines == where, 1.0, 0.0).astype(BF16)
                at = span(i, size)
                refined_v = refined_ref[at, :].astype(F32)
                one = silu(projected_ref[at, :] + dot_first(pick, region[...])).astype(BF16)
                two = silu(dot(one, w_ref[level, 4])).astype(BF16)
                counts_i = []
                for k in range(many):
                    counts_i += counts_at(cnt_ref, i * many + k)
                new = state_ref[at, :].astype(F32) + refined_v + dot(two, w_ref[level, 5])
                new = masked(new * (0.5**0.5), cap, counts_i).astype(BF16)
                if last:
                    refs[1][at, :] = new
                    pltpu.make_async_copy(refs[1].at[at], out_ref.at[at], refs[2].at[i]).start()
                else:
                    out_ref[at, :] = new
                    low = masked(silu(dot_last(new, down_ref[level + 1])), cap, counts_i)
                    refs[0][span(i, half), :] = pack(low.astype(BF16))

            if last:
                for i in range(n_src // many):
                    at = slice(i * size, (i + 1) * size)
                    pltpu.make_async_copy(refs[1].at[at], out_ref.at[at], refs[2].at[i]).wait()

        scratch = [pltpu.VMEM((region_rows, width), BF16)]
        if last:
            out_shape, out_specs = [array((rows, width))], [ANY]
            scratch += [pltpu.VMEM((rows, width), BF16), pltpu.SemaphoreType.DMA((n_src,))]
        else:
            out_shape, out_specs = [array((rows, width)), array((prows, 2 * trip))], None
        return call(
            kernel,
            (cnt, meta),
            (src_row, state, refined, projected, edge_w, down_t, *pieces),
            out_shape,
            scratch,
            2 * rows * width * (3 * width + region_rows + trip),
            8 * 2**20,
            None,
            out_specs,
        )

    def exchange_order():
        mid = n_dst // 2
        over = [(k + 1.5 * x, x, j) for x in range(groups) for k, j in enumerate(range(mid, n_dst))]
        near = [
            (k + 1.5 * x, x, j)
            for x in range(groups)
            for k, j in enumerate(range(mid - 1, -1, -1))
            if (x, j) != (0, 0)
        ]
        order = []
        for k, (_, x, j) in enumerate(sorted(over)):
            order.append((x, j))
            if k < len(near):
                order.append(sorted(near)[k][1:])
        return order

    def exchange(level, state, pool, window):
        mine, joined, arrived = [], [], [[None] * n_dst for _ in range(groups)]
        sent = []

        def prepare(x):
            own, give, keep = message_call(level, x, state, pool)
            mine.append(own)
            joined.append(join_call(keep, lax.ppermute(give, "src", src_perm(1))))

        prepare(0)
        arrived[0][0] = joined[0][0]
        for x, j in exchange_order():
            while len(joined) <= x:
                prepare(len(joined))
            operand, offset = joined[x][j], 2 * x * n_dst + j
            if len(sent) >= window:
                operand, _ = lax.optimization_barrier((operand, sent[-window]))
            sent.append(lax.ppermute(operand, both, [(a, a ^ offset) for a in range(n)]))
            arrived[x][j] = sent[-1]
        return mine, arrived

    def atoms_of(sums):
        other = lax.ppermute(sums, "src", src_perm(1))
        sums = (sums.astype(F32) + other.astype(F32)).astype(BF16)
        total = sums.astype(F32)
        for i in range(2, n_src, 2):
            total = total + lax.ppermute(sums, "src", src_perm(i)).astype(F32)
        return (total * DEGREE ** (-0.5)).astype(BF16)

    def to_sources(atoms):
        slots = []
        for r in range(ratio):
            perm = []
            for a in range(n):
                t, u, j = a // n_dst, a % n_dst // ratio, a % ratio
                v = t % groups * 2 + t // groups
                perm.append((a, u * n_dst + v * ratio + (j ^ r)))
            slots.append(lax.ppermute(atoms, both, perm))
        return slots

    state = edge_state
    for level in range(NBLK):
        pool = gather_src(lowered, tiles if level == 0 else None)
        mine, theirs = exchange(level, state, pool, 5)
        refined, sums = None, None
        parts = [(x, list(range(n_dst))) for x in range(groups)]
        parts[-1:] = [(groups - 1, list(range(n_dst - 1))), (groups - 1, [n_dst - 1])]
        for k, (x, js) in enumerate(parts):
            refined, sums = refine_call(
                level, x, js, mine[x], theirs[x], refined, sums, k == len(parts) - 1
            )
        region = to_sources(atoms_of(sums))
        out = update_call(level, state, refined, project(level, 3, refined), region)
        state = out[0]
        if level < NBLK - 1:
            lowered = out[1]
    return state


def solution(mesh):
    placed = (
        P(("src", "dst"), None),
        P(None, ("src", "dst")),
        P(("src", "dst")),
        P(("src", "dst")),
        P(("src", "dst")),
        P(("src", "dst"), None),
        P(("src", "dst"), None),
        P(),
        P(),
        P(),
    )
    return jax.shard_map(
        body, mesh=mesh, in_specs=placed, out_specs=P(("src", "dst"), None), check_vma=False
    )
```

```python
import functools

import jax
import jax.numpy as jnp
from jax import lax
from jax.experimental import pallas as pl
from jax.experimental.pallas import tpu as pltpu
from jax.sharding import PartitionSpec as P

BLK = 128
PAIRS = 4
NBLK = 2
NSPH = 4
ATOM_DEV = 32
DEGREE = 64
VMEM_LIMIT = 20 * 1024 * 1024

F32 = jnp.float32
BF16 = jnp.bfloat16


def silu(value):
    half = 0.5 * value
    return half + half * jnp.tanh(half)


def dot(a, b):
    return jnp.dot(a, b, preferred_element_type=F32)


def dot_last(a, b):
    return lax.dot_general(a, b, (((1,), (1,)), ((), ())), preferred_element_type=F32)


def dot_first(a, b):
    return lax.dot_general(a, b, (((0,), (0,)), ((), ())), preferred_element_type=F32)


def legendre(cosine):
    square = cosine * cosine
    return [
        cosine,
        1.5 * square - 0.5,
        (2.5 * square - 1.5) * cosine,
        (4.375 * square - 3.75) * square + 0.375,
    ]


def masked(value, cap, counts):
    position = lax.broadcasted_iota(jnp.int32, (cap, value.shape[1]), 0)
    parts = [
        jnp.where(position < count, value[i * cap : (i + 1) * cap], 0.0)
        for i, count in enumerate(counts)
    ]
    return jnp.concatenate(parts, axis=0)


def pack(low):
    half = low.shape[0] // 2
    return jnp.concatenate([low[:half], low[half:]], axis=1)


SMEM = pl.BlockSpec(memory_space=pltpu.SMEM)
VMEM = pl.BlockSpec(memory_space=pltpu.VMEM)
ANY = pl.BlockSpec(memory_space=pl.ANY)


def call(kernel, scalars, args, out_shape, scratch=(), flops=0, nbytes=0, aliases=None, out_specs=None):
    several = isinstance(out_shape, list)
    return pl.pallas_call(
        kernel,
        in_specs=[SMEM] * len(scalars) + [VMEM] * len(args),
        out_specs=out_specs or ([VMEM] * len(out_shape) if several else VMEM),
        out_shape=out_shape,
        scratch_shapes=list(scratch),
        input_output_aliases=aliases or {},
        compiler_params=pltpu.CompilerParams(vmem_limit_bytes=VMEM_LIMIT),
        cost_estimate=pl.CostEstimate(flops=flops, bytes_accessed=nbytes, transcendentals=0),
    )(*scalars, *args)


def array(shape, kind=BF16):
    return jax.ShapeDtypeStruct(shape, kind)


def span(start, size):
    return pl.ds(pl.multiple_of(start * size, size), size)


def body(
    edge_state, directions, src_atom, dst_atom, rev_pos, counts, triplets, down_w, trip_w, edge_w
):
    n_src = lax.axis_size("src")
    n_dst = lax.axis_size("dst")
    n = n_src * n_dst
    rows, width = edge_state.shape
    trip = down_w.shape[2]
    cap = rows // n
    sb = rows // n_src
    spb = sb // BLK
    half = sb // 2
    chunk = min(sb, 256)
    groups = n_src // 2
    nblock = rows // BLK
    ratio = n_dst // n_src
    dst_rows = ATOM_DEV * n_src
    region_rows = ratio * dst_rows
    prows = rows // 2
    both = ("src", "dst")
    chunks = range(sb // chunk)
    per = chunk // cap

    s = lax.axis_index("src")
    d = lax.axis_index("dst")

    cnt = counts.reshape(-1)
    flat = triplets.T.reshape(-1)
    block = flat % nblock
    rel = (flat // nblock) ^ s
    pool_row = rel * prows + block // spb * half + block % (spb // 2) * BLK
    pool_half = (block % spb) // (spb // 2)
    meta = jnp.concatenate([jnp.stack([s, d]), pool_row, pool_half, rel * nblock + block]).astype(jnp.int32)
    at_row = 2
    at_half = at_row + nblock * PAIRS
    at_block = at_half + nblock * PAIRS
    down_t = jnp.swapaxes(down_w, 1, 2)

    def counts_at(cnt_ref, block, h=None):
        first = block * n_dst + (0 if h is None else h * per)
        return [cnt_ref[first + i] for i in range(n_dst if h is None else per)]

    def split(value):
        return [value[h * chunk : (h + 1) * chunk] for h in chunks]

    def lower_kernel(cnt_ref, state_ref, down_ref, out_ref):
        @pl.loop(0, n_src)
        def _(i):
            low = silu(dot_last(state_ref[span(i, sb), :], down_ref[0]))
            out_ref[span(i, half), :] = pack(masked(low, cap, counts_at(cnt_ref, i)).astype(BF16))

    lowered = call(
        lower_kernel,
        (cnt,),
        (edge_state, down_t),
        array((prows, 2 * trip)),
        (),
        2 * rows * width * trip,
        rows * width * 2,
    )

    def project(level, index, x):
        def kernel(x_ref, w_ref, out_ref):
            @pl.loop(0, n_src)
            def _(i):
                out_ref[span(i, sb), :] = dot(x_ref[span(i, sb), :], w_ref[level, index])

        return call(
            kernel, (), (x, edge_w), array((rows, width), F32), (),
            2 * rows * width * width, 6 * rows * width,
        )

    def src_perm(i):
        return [(a, a ^ i) for a in range(n_src)]

    def gather_src(x, before=None):
        slots = [None] * n_src
        slots[0] = x
        for i in range(2, n_src, 2):
            slots[i] = lax.ppermute(x, "src", src_perm(i))
        for i in range(0, n_src, 2):
            if i and before is not None:
                slots[i], _ = lax.optimization_barrier((slots[i], before))
            slots[i + 1] = lax.ppermute(slots[i], "src", src_perm(1))
        return slots

    dirs_pool = gather_src(directions)

    def tiles_kernel(m, *refs):
        own_ref, out_ref, pool_ref = refs[0], refs[n_src], refs[n_src + 1]
        for k in range(n_src):
            pool_ref[:, k * rows : (k + 1) * rows] = refs[k][...]

        @pl.loop(0, nblock)
        def _(c):
            own = own_ref[:, span(c, BLK)]
            col = jnp.concatenate([own, jnp.zeros((5, BLK), F32)], axis=0).T
            for q in range(PAIRS):
                chosen = pool_ref[:, span(m[at_block + q * nblock + c], BLK)]
                cosine = (
                    col[:, 0:1] * chosen[0:1]
                    + col[:, 1:2] * chosen[1:2]
                    + col[:, 2:3] * chosen[2:3]
                )
                for degree, tile in enumerate(legendre(cosine)):
                    out_ref[c, degree, :, q * BLK : (q + 1) * BLK] = tile.astype(BF16)

    tiles = call(
        tiles_kernel,
        (meta,),
        dirs_pool,
        array((nblock, NSPH, BLK, PAIRS * BLK)),
        [pltpu.VMEM((3, n_src * rows), F32)],
        nblock * BLK * PAIRS * BLK * 2000,
        nblock * NSPH * BLK * PAIRS * BLK * 2,
    )

    rev_row = rev_pos.reshape(n_src, 1, sb)
    dst_row = dst_atom.reshape(n_src, 1, sb)
    src_row = src_atom.reshape(n_src, 1, sb)
    tri_scale = (BLK * PAIRS) ** (-0.5)

    def here(m, x, i):
        return m[0] ^ (2 * x) ^ 1 ^ i

    def message_call(level, x, state, pool):
        def kernel(cnt_ref, m, tiles_ref, state_ref, w_ref, up_ref, rev_ref, *refs):
            pool_refs, refs = refs[:n_src], refs[n_src:]
            mine_ref, give_ref, keep_ref, pool_all, hold = refs
            for k in range(n_src):
                pool_all[k * prows : (k + 1) * prows, :] = pool_refs[k][...]
            target_row = lax.broadcasted_iota(jnp.int32, (chunk, chunk), 0)
            base = lax.broadcasted_iota(jnp.int32, (1, chunk), 1) // cap * cap
            for i, out_ref in enumerate((give_ref, keep_ref)):
                at_src = here(m, x, i)
                triple = []
                for c in range(spb):
                    chosen = []
                    for q in range(PAIRS):
                        which = q * nblock + at_src * spb + c
                        v = pool_all[pl.ds(pl.multiple_of(m[at_row + which], BLK), BLK), :]
                        chosen.append(jnp.where(m[at_half + which] == 1, v[:, trip:], v[:, :trip]))
                    summed = dot(
                        tiles_ref[at_src * spb + c].reshape(NSPH * BLK, PAIRS * BLK),
                        jnp.concatenate(chosen, axis=0),
                    )
                    summed = (summed * tri_scale).astype(BF16)
                    triple.append(
                        jnp.concatenate(
                            [summed[l * BLK : (l + 1) * BLK] for l in range(NSPH)], axis=1
                        )
                    )
                triple = jnp.concatenate(triple, axis=0)
                size = chunk
                message = []
                for h in range(sb // size):
                    pre = dot(state_ref[span(at_src * (sb // size) + h, size), :], w_ref[level, 0])
                    pre = pre + dot(triple[h * size : (h + 1) * size], up_ref[level])
                    counts_h = counts_at(cnt_ref, at_src)[h * size // cap : (h + 1) * size // cap]
                    message.append(masked(silu(pre), cap, counts_h).astype(BF16))
                message = jnp.concatenate(message, axis=0)
                mine_ref[span(at_src & 1, sb), :] = message
                for h in chunks:
                    at = slice(h * chunk, (h + 1) * chunk)
                    pick = jnp.where(target_row == rev_ref[at_src, :, at] + base, 1.0, 0.0)
                    hold[at, :] = dot(pick.astype(BF16), message[at]).astype(BF16)
                for j in range(n_dst):
                    out_ref[j * cap : (j + 1) * cap, :] = hold[span(m[1] ^ j, cap), :]

        return call(
            kernel,
            (cnt, meta),
            (tiles, state, edge_w, trip_w, rev_row, *pool),
            [array((2 * sb, width)), array((sb, width)), array((sb, width))],
            [pltpu.VMEM((n_src * prows, 2 * trip), BF16), pltpu.VMEM((sb, width), BF16)],
            4 * sb * width * (width + 2 * NSPH * trip) + 4 * sb * NSPH * 512 * 256,
            9 * 2**20,
        )

    def join_call(keep, received):
        def kernel(keep_ref, received_ref, *out_refs):
            for j, out_ref in enumerate(out_refs):
                out_ref[:cap, :] = keep_ref[j * cap : (j + 1) * cap, :]
                out_ref[cap:, :] = received_ref[j * cap : (j + 1) * cap, :]

        return call(
            kernel,
            (),
            (keep, received),
            [array((2 * cap, width))] * n_dst,
            (),
            0,
            4 * sb * width * 2,
        )

    def refine_call(level, x, js, mine, theirs, refined, sums, last):
        adds = js[-1] == n_dst - 1
        first = refined is None
        size = len(js) * 2 * cap

        def kernel(m, dst_ref, w_ref, mine_ref, *refs):
            their_refs, refs = refs[: len(js)], refs[len(js) :]
            if not first:
                sums_ref, refs = refs[1], refs[2:]
            out_ref, sum_ref = refs
            slots = [(here(m, x, 1 - c), m[1] ^ j) for j in js for c in range(2)]
            own = jnp.concatenate(
                [mine_ref[span((src & 1) * n_dst + dst, cap), :] for src, dst in slots], axis=0
            )
            other = jnp.concatenate([ref[...] for ref in their_refs], axis=0)
            symmetric = (own.astype(F32) + other.astype(F32)).astype(BF16)
            inner = silu(dot(symmetric, w_ref[level, 1])).astype(BF16)
            out = (symmetric.astype(F32) + dot(inner, w_ref[level, 2])).astype(BF16)
            for k, (src, dst) in enumerate(slots):
                out_ref[span(src * n_dst + dst, cap), :] = out[k * cap : (k + 1) * cap]
            total = None if first else sums_ref[...]
            for i in range(2 if adds else 0):
                atoms = lax.broadcasted_iota(jnp.int32, (dst_rows, sb), 0)
                onehot = jnp.where(atoms == dst_ref[here(m, x, i)], 1.0, 0.0).astype(BF16)
                part = dot(onehot, out_ref[span(here(m, x, i), sb), :])
                total = part if total is None else total + part
            sum_ref[...] = total.astype(sum_ref.dtype)

        args = (dst_row, edge_w, mine, *[theirs[j] for j in js])
        aliases = {}
        if not first:
            aliases = {1 + len(args): 0}
            args = (*args, refined, sums)
        return call(
            kernel,
            (meta,),
            args,
            [array((rows, width)), array((dst_rows, width), BF16 if last else F32)],
            (),
            2 * size * width * (2 * width + dst_rows),
            6 * size * width,
            aliases,
        )

    def update_call(level, state, refined, projected, pieces):
        last = level == NBLK - 1

        def kernel(cnt_ref, m, src_ref, state_ref, refined_ref, projected_ref, w_ref, down_ref, *refs):
            piece_refs, refs = refs[: len(pieces)], refs[len(pieces) :]
            out_ref, refs = refs[0], refs[1:]
            region = refs[1] if not last else refs[0]
            filled = 0
            for piece_ref in piece_refs:
                fed = dot(piece_ref[...], w_ref[level, 3]).astype(BF16)
                region[filled : filled + piece_ref.shape[0], :] = fed
                filled += piece_ref.shape[0]
            many = 2 if last else 1
            size = many * sb
            lines = lax.broadcasted_iota(jnp.int32, (region_rows, size), 0)

            @pl.loop(0, n_src // many)
            def _(i):
                atom = jnp.concatenate([src_ref[i * many + k] for k in range(many)], axis=1)
                where = (atom // dst_rows ^ m[1] % ratio) * dst_rows + atom % dst_rows
                pick = jnp.where(lines == where, 1.0, 0.0).astype(BF16)
                at = span(i, size)
                refined_v = refined_ref[at, :].astype(F32)
                one = silu(projected_ref[at, :] + dot_first(pick, region[...])).astype(BF16)
                two = silu(dot(one, w_ref[level, 4])).astype(BF16)
                counts_i = []
                for k in range(many):
                    counts_i += counts_at(cnt_ref, i * many + k)
                new = state_ref[at, :].astype(F32) + refined_v + dot(two, w_ref[level, 5])
                new = masked(new * (0.5**0.5), cap, counts_i).astype(BF16)
                if last:
                    refs[1][at, :] = new
                    pltpu.make_async_copy(refs[1].at[at], out_ref.at[at], refs[2].at[i]).start()
                else:
                    out_ref[at, :] = new
                    low = masked(silu(dot_last(new, down_ref[level + 1])), cap, counts_i)
                    refs[0][span(i, half), :] = pack(low.astype(BF16))

            if last:
                for i in range(n_src // many):
                    at = slice(i * size, (i + 1) * size)
                    pltpu.make_async_copy(refs[1].at[at], out_ref.at[at], refs[2].at[i]).wait()

        scratch = [pltpu.VMEM((region_rows, width), BF16)]
        if last:
            out_shape, out_specs = [array((rows, width))], [ANY]
            scratch += [pltpu.VMEM((rows, width), BF16), pltpu.SemaphoreType.DMA((n_src,))]
        else:
            out_shape, out_specs = [array((rows, width)), array((prows, 2 * trip))], None
        return call(
            kernel,
            (cnt, meta),
            (src_row, state, refined, projected, edge_w, down_t, *pieces),
            out_shape,
            scratch,
            2 * rows * width * (3 * width + region_rows + trip),
            8 * 2**20,
            None,
            out_specs,
        )

    def exchange_order():
        mid = n_dst // 2
        over = [(k + 1.5 * x, x, j) for x in range(groups) for k, j in enumerate(range(mid, n_dst))]
        near = [
            (k + 1.5 * x, x, j)
            for x in range(groups)
            for k, j in enumerate(range(mid - 1, -1, -1))
            if (x, j) != (0, 0)
        ]
        order = []
        for k, (_, x, j) in enumerate(sorted(over)):
            order.append((x, j))
            if k < len(near):
                order.append(sorted(near)[k][1:])
        return order

    def exchange(level, state, pool, window):
        mine, joined, arrived = [], [], [[None] * n_dst for _ in range(groups)]
        sent = []

        def prepare(x):
            own, give, keep = message_call(level, x, state, pool)
            mine.append(own)
            joined.append(join_call(keep, lax.ppermute(give, "src", src_perm(1))))

        prepare(0)
        arrived[0][0] = joined[0][0]
        for x, j in exchange_order():
            while len(joined) <= x:
                prepare(len(joined))
            operand, offset = joined[x][j], 2 * x * n_dst + j
            if len(sent) >= window:
                operand, _ = lax.optimization_barrier((operand, sent[-window]))
            sent.append(lax.ppermute(operand, both, [(a, a ^ offset) for a in range(n)]))
            arrived[x][j] = sent[-1]
        return mine, arrived

    def atoms_of(sums):
        other = lax.ppermute(sums, "src", src_perm(1))
        sums = (sums.astype(F32) + other.astype(F32)).astype(BF16)
        total = sums.astype(F32)
        for i in range(2, n_src, 2):
            total = total + lax.ppermute(sums, "src", src_perm(i)).astype(F32)
        return (total * DEGREE ** (-0.5)).astype(BF16)

    def to_sources(atoms):
        slots = []
        for r in range(ratio):
            perm = []
            for a in range(n):
                t, u, j = a // n_dst, a % n_dst // ratio, a % ratio
                v = t % groups * 2 + t // groups
                perm.append((a, u * n_dst + v * ratio + (j ^ r)))
            slots.append(lax.ppermute(atoms, both, perm))
        return slots

    state = edge_state
    for level in range(NBLK):
        pool = gather_src(lowered, tiles if level == 0 else None)
        mine, theirs = exchange(level, state, pool, 5)
        refined, sums = None, None
        parts = [(x, list(range(n_dst))) for x in range(groups)]
        parts[-1:] = [(groups - 1, list(range(n_dst - 1))), (groups - 1, [n_dst - 1])]
        for k, (x, js) in enumerate(parts):
            refined, sums = refine_call(
                level, x, js, mine[x], theirs[x], refined, sums, k == len(parts) - 1
            )
        region = to_sources(atoms_of(sums))
        out = update_call(level, state, refined, project(level, 3, refined), region)
        state = out[0]
        if level < NBLK - 1:
            lowered = out[1]
    return state


def solution(mesh):
    placed = (
        P(("src", "dst"), None),
        P(None, ("src", "dst")),
        P(("src", "dst")),
        P(("src", "dst")),
        P(("src", "dst")),
        P(("src", "dst"), None),
        P(("src", "dst"), None),
        P(),
        P(),
        P(),
    )
    return jax.shard_map(
        body, mesh=mesh, in_specs=placed, out_specs=P(("src", "dst"), None), check_vma=False
    )
```
